256 devices in a mesh: dp: 16 (over y_hi, z), vt: 16 (over y_lo, x, core).
Axes of the slice: x: 4, y: 4 (y_hi: 2, y_lo: 2; y = y_hi * 2 + y_lo), z: 8, core: 2. Of those that a mesh axis runs over, the one named last changes fastest.
Arguments:
- tokens: bfloat16 [16, 16, 1, 128, 1152], P('dp', 'vt'), may hold values from -170 to 170
- cotangent: bfloat16 [16, 16, 1, 128, 1152], P('dp', 'vt'), may hold values from -6 to 6
- modulation: float32 [16, 16, 3, 1152], P('dp', 'vt'), may hold values from -4 to 4
- q_gain: float32 [72], replicated, may hold values from 0.25 to 1.75
- k_gain: float32 [72], replicated, may hold values from 0.25 to 1.75
- w_qkv: bfloat16 [1152, 3456], replicated, may hold values from -0.1875 to 0.1875
- w_out: bfloat16 [1152, 1152], replicated, may hold values from -0.1875 to 0.1875
- neighbours: int32 [16, 16, 2], P('dp', 'vt'), may hold values from 0 to 15, as said below
Outputs:
- grad_tokens: bfloat16 [16, 16, 1, 128, 1152], P('dp', 'vt')
- grad_qkv: bfloat16 [1152, 3456], P('vt')
- grad_out: bfloat16 [1152, 1152], P('vt')
The draws below stay inside these ranges and needn't reach their ends.
Inputs may be any that keep to these rules, and one draw needn't show every extreme that they name: `neighbours`: along each row the 16 cameras form consecutive samples of 3 to 8 cameras; each sample's cameras form a cycle in position order, running either way (drawn per sample): column 0 holds a camera's left and column 1 its right neighbour on that cycle, so that in a sample running the other way a camera's left is the next position and the sample's last camera's left is its first; some row holds a sample of 8 cameras.
All inputs are finite; a program needn't handle non-finite values.
Results may differ from the reference program's by a relative error of at most 0.03.
Values may be sent and summed in bfloat16 or wider, within the bound.
No kernel may reach another device: no remote copies, remote signals or barrier semaphores. Data moves between devices by JAX's collectives and lax.ppermute only.
A program may use at most 128 MiB of HBM per device.

```python
import math
import jax
import jax.numpy as jnp
from jax import lax

D = 1152
HEAD_DIM = 72
FRAMES = 1
PATCHES = 128
ROWS = 16
CAMS = 16


def draw_tokens(key, part):
    key = jax.random.fold_in(key, 7)
    key_base, key_rows, key_features = jax.random.split(key, 3)
    full_shape = (ROWS, CAMS, FRAMES, PATCHES, D)
    row_shape = (ROWS, CAMS, FRAMES, PATCHES, 1)
    base_values = jnp.clip(jax.random.normal(key_base, full_shape, jnp.float32), -6.0, 6.0)
    row_scale = jnp.exp(jax.random.uniform(key_rows, row_shape, jnp.float32, 0.0, math.log(10.0)))
    feature_scale = jnp.exp(jax.random.uniform(key_features, (D,), jnp.float32, 0.0, math.log(10.0)))
    return (base_values * row_scale * feature_scale * 0.25).astype(jnp.bfloat16)


def split_row(key_row, forced):
    positions = jnp.arange(CAMS, dtype=jnp.int32)
    options = jnp.arange(3, 9, dtype=jnp.int32)

    def one_sample(sample_index, loop_state):
        starts, lengths, turned, cursor = loop_state
        remaining = CAMS - cursor
        allowed = jnp.logical_and(options <= remaining, jnp.logical_or(options == remaining, remaining - options >= 3))
        priority = jax.random.randint(jax.random.fold_in(key_row, sample_index), (6,), 0, 1000) * 8 + jnp.arange(6, dtype=jnp.int32)
        picked = options[jnp.argmax(jnp.where(allowed, priority, -1))]
        picked = jnp.where(jnp.logical_and(forced, sample_index == 0), min(8, CAMS), picked)
        flip_bit = jax.random.randint(jax.random.fold_in(key_row, 1000 + sample_index), (), 0, 2)
        active = remaining > 0
        inside = jnp.logical_and(jnp.logical_and(positions >= cursor, positions < cursor + picked), active)
        starts = jnp.where(inside, cursor, starts)
        lengths = jnp.where(inside, picked, lengths)
        turned = jnp.where(inside, flip_bit, turned)
        cursor = cursor + jnp.where(active, picked, 0)
        return (starts, lengths, turned, cursor)
    empty_slots = jnp.zeros((CAMS,), jnp.int32)
    starts, lengths, turned, cursor = lax.fori_loop(0, CAMS, one_sample, (empty_slots, empty_slots, empty_slots, jnp.int32(0)))
    lower_of = jnp.where(positions == starts, starts + lengths - 1, positions - 1)
    upper_of = jnp.where(positions == starts + lengths - 1, starts, positions + 1)
    left_of = jnp.where(turned == 1, upper_of, lower_of)
    right_of = jnp.where(turned == 1, lower_of, upper_of)
    return jnp.stack([left_of, right_of], axis=-1)


def draw_neighbours(key, part):
    key = jax.random.fold_in(key, 19)
    key_pick, key_rows = jax.random.split(key)
    chosen_row = jax.random.randint(key_pick, (), 0, ROWS)
    row_keys = jax.random.split(key_rows, ROWS)
    forced = jnp.arange(ROWS) == chosen_row
    return jax.vmap(split_row)(row_keys, forced).astype(jnp.int32)


def shard_levels(rng, shape, cuts, smallest, high):
    level, own = 1.0, jax.random.fold_in(rng, 6)
    for position, parts in cuts:
        steps = jnp.exp(jax.random.uniform(jax.random.fold_in(own, position), (parts,), jnp.float32, smallest / len(cuts), high / len(cuts)))
        level = level * jnp.repeat(steps, shape[position] // parts).reshape([-1 if axis == position else 1 for axis in range(len(shape))])
    return level


def centred(own_key, shape, scale, reach, cuts=(), kind=jnp.bfloat16):
    level = shard_levels(own_key, shape, cuts, -0.22, 0.18) if cuts else 1.0
    entries = jax.random.normal(own_key, shape, jnp.float32) * scale * level
    return jnp.minimum(jnp.maximum(entries, -reach), reach).astype(kind)


def setup_inputs(seed: int = 0) -> dict:
    key_of = jax.random.split(jax.random.key(seed), 9)
    tokens = draw_tokens(jax.random.fold_in(key_of[8], 71), 0)
    cotangent = centred(key_of[1], (ROWS, CAMS, FRAMES, PATCHES, D), 1.0, 6.0, ((0, 16), (1, 16)))
    modulation = centred(key_of[2], (ROWS, CAMS, 3, D), 0.7, 4.0, ((0, 16), (1, 16)), jnp.float32)
    q_gain = jnp.clip(1.0 + 0.15 * jax.random.normal(key_of[3], (HEAD_DIM,), jnp.float32), 0.25, 1.75)
    k_gain = jnp.clip(1.0 + 0.15 * jax.random.normal(key_of[4], (HEAD_DIM,), jnp.float32), 0.25, 1.75)
    w_qkv = centred(key_of[5], (D, 3 * D), D ** -0.5, 0.1875)
    w_out = centred(key_of[6], (D, D), D ** -0.5, 0.1875)
    neighbours = draw_neighbours(jax.random.fold_in(key_of[8], 71), 0)
    return {"tokens": tokens, "cotangent": cotangent, "modulation": modulation, "q_gain": q_gain, "k_gain": k_gain, "w_qkv": w_qkv, "w_out": w_out, "neighbours": neighbours}


def layer_norm(values):
    center = values - lax.optimization_barrier(jnp.mean(values, axis=-1, keepdims=True))
    spread = lax.optimization_barrier(jnp.mean(center * center, axis=-1, keepdims=True))
    inverse = lax.rsqrt(spread + 1e-06)
    return (center * inverse, inverse)

def head_norm(raw_values, gain_vector):
    radius = jnp.sqrt(lax.optimization_barrier(jnp.mean(raw_values * raw_values, axis=-1, keepdims=True)) + 1e-06)
    return (raw_values / radius * gain_vector, radius)

def head_back(upstream, raw_values, radius, gain_vector):
    shaped = upstream * gain_vector
    inner_sum = lax.optimization_barrier(jnp.sum(shaped * raw_values, axis=-1, keepdims=True))
    return shaped / radius - raw_values * inner_sum / (raw_values.shape[-1] * radius * radius * radius)

def rounded(values):
    return lax.optimization_barrier(values.astype(jnp.bfloat16)).astype(jnp.float32)

def collect_terms(grad_sets, left_index, right_index, patches):
    to_left = rounded(grad_sets[:, :, :patches])
    own_terms = grad_sets[:, :, patches:2 * patches]
    to_right = rounded(grad_sets[:, :, 2 * patches:])
    return own_terms + jnp.take(to_right, left_index, axis=0) + jnp.take(to_left, right_index, axis=0)

def row_pass(tokens, cotangent, modulation, q_gain, k_gain, w_qkv, w_out, neighbours):
    cameras = tokens.shape[0]
    frames = tokens.shape[1]
    patches = tokens.shape[2]
    features = tokens.shape[3]
    head_dim = q_gain.shape[0]
    head_count = features // head_dim
    scale_inv = 1.0 / math.sqrt(head_dim)
    values = tokens.astype(jnp.float32)
    normed, inverse = layer_norm(values)
    shifts = modulation[:, 0][:, None, None, :]
    scales = modulation[:, 1][:, None, None, :]
    gating = modulation[:, 2][:, None, None, :]
    hidden = (normed * (1.0 + scales) + shifts).astype(jnp.bfloat16)
    hidden_flat = hidden.reshape(cameras * frames * patches, features)
    project = jnp.dot(hidden_flat, w_qkv, preferred_element_type=jnp.float32)
    project = project.reshape(cameras, frames, patches, 3, head_count, head_dim)
    q_raw = project[:, :, :, 0]
    k_raw = project[:, :, :, 1]
    query_heads, q_radius = head_norm(q_raw, q_gain)
    key_heads, k_radius = head_norm(k_raw, k_gain)
    query_heads = query_heads.astype(jnp.bfloat16)
    key_heads = key_heads.astype(jnp.bfloat16)
    value_heads = project[:, :, :, 2].astype(jnp.bfloat16)
    left_index = neighbours[:, 0]
    right_index = neighbours[:, 1]
    key_sets = jnp.concatenate([jnp.take(key_heads, left_index, axis=0), key_heads, jnp.take(key_heads, right_index, axis=0)], axis=2)
    value_sets = jnp.concatenate([jnp.take(value_heads, left_index, axis=0), value_heads, jnp.take(value_heads, right_index, axis=0)], axis=2)
    query_wide = query_heads.astype(jnp.float32)
    key_wide = key_sets.astype(jnp.float32)
    value_wide = value_sets.astype(jnp.float32)
    scores = jnp.einsum('cfqhd,cfkhd->cfhqk', query_wide, key_wide) * scale_inv
    exponent_values = jnp.exp(scores)
    attn_probs = exponent_values / lax.optimization_barrier(jnp.sum(exponent_values, axis=-1, keepdims=True))
    probs_low = attn_probs.astype(jnp.bfloat16)
    probs_wide = probs_low.astype(jnp.float32)
    attended = jnp.einsum('cfhqk,cfkhd->cfqhd', probs_wide, value_wide).astype(jnp.bfloat16)
    branch = (gating * cotangent.astype(jnp.float32)).astype(jnp.bfloat16)
    branch_flat = branch.reshape(cameras * frames * patches, features)
    grad_attended = jnp.dot(branch_flat, w_out.T, preferred_element_type=jnp.float32).astype(jnp.bfloat16)
    grad_attended = grad_attended.reshape(cameras, frames, patches, head_count, head_dim)
    grad_att_wide = grad_attended.astype(jnp.float32)
    grad_probs = jnp.einsum('cfqhd,cfkhd->cfhqk', grad_att_wide, value_wide)
    centre = lax.optimization_barrier(jnp.sum(attn_probs * grad_probs, axis=-1, keepdims=True))
    grad_scores = rounded(attn_probs * (grad_probs - centre) * scale_inv)
    grad_queries = jnp.einsum('cfhqk,cfkhd->cfqhd', grad_scores, key_wide)
    grad_key_sets = jnp.einsum('cfhqk,cfqhd->cfkhd', grad_scores, query_wide)
    grad_value_sets = jnp.einsum('cfhqk,cfqhd->cfkhd', probs_wide, grad_att_wide)
    grad_keys = collect_terms(grad_key_sets, left_index, right_index, patches)
    grad_values = collect_terms(grad_value_sets, left_index, right_index, patches)
    grad_q_raw = head_back(grad_queries, q_raw, q_radius, q_gain)
    grad_k_raw = head_back(grad_keys, k_raw, k_radius, k_gain)
    grad_project = jnp.stack([grad_q_raw, grad_k_raw, grad_values], axis=3).astype(jnp.bfloat16)
    grad_flat = grad_project.reshape(cameras * frames * patches, 3 * features)
    grad_hidden = jnp.dot(grad_flat, w_qkv.T, preferred_element_type=jnp.float32)
    grad_hidden = grad_hidden.reshape(cameras, frames, patches, features)
    grad_normed = grad_hidden * (1.0 + scales)
    grad_input = inverse * (grad_normed - lax.optimization_barrier(jnp.mean(grad_normed, axis=-1, keepdims=True)) - normed * lax.optimization_barrier(jnp.mean(grad_normed * normed, axis=-1, keepdims=True)))
    grad_tokens = (cotangent.astype(jnp.float32) + grad_input).astype(jnp.bfloat16)
    tokens_each = frames * patches
    pieces = (hidden.reshape(cameras, tokens_each, features), grad_flat.reshape(cameras, tokens_each, 3 * features), attended.reshape(cameras, tokens_each, features), branch.reshape(cameras, tokens_each, features))
    return (grad_tokens, pieces)

def reference(tokens, cotangent, modulation, q_gain, k_gain, w_qkv, w_out, neighbours):
    features = tokens.shape[-1]

    def camera_step(running, camera_pieces):
        hidden_one, grad_one, attended_one, branch_one = camera_pieces
        term_in = jnp.dot(hidden_one.T, grad_one, preferred_element_type=jnp.float32)
        term_out = jnp.dot(attended_one.T, branch_one, preferred_element_type=jnp.float32)
        return ((running[0] + rounded(term_in), running[1] + rounded(term_out)), jnp.zeros((), jnp.float32))

    def row_step(running, row_inputs):
        row_tokens, row_cotangent, row_modulation, row_neighbours = row_inputs
        grad_tokens, pieces = row_pass(row_tokens, row_cotangent, row_modulation, q_gain, k_gain, w_qkv, w_out, row_neighbours)
        running = lax.scan(camera_step, running, pieces)[0]
        return (running, grad_tokens)
    initial = (jnp.zeros((features, 3 * features), jnp.float32), jnp.zeros((features, features), jnp.float32))
    totals, grad_tokens = lax.scan(row_step, initial, (tokens, cotangent, modulation, neighbours))
    factor = 1.0 / (ROWS * CAMS)
    return (grad_tokens, (totals[0] * factor).astype(jnp.bfloat16), (totals[1] * factor).astype(jnp.bfloat16))
```

```python
import math

import jax
import jax.numpy as jnp
from jax import lax
from jax.experimental import pallas as pl
from jax.experimental.pallas import tpu as pltpu
from jax.sharding import PartitionSpec as P

BF = jnp.bfloat16
F32 = jnp.float32
EPS = 1e-06
NN = (((1,), (0,)), ((), ()))
NT = (((1,), (1,)), ((), ()))
MIB = 1024 * 1024


def dot(a, b, dims=NN):
    return lax.dot_general(a, b, dims, preferred_element_type=F32)


def whole(shape):
    return pl.BlockSpec(shape, lambda *_: (0,) * len(shape))


def params(mib):
    return pltpu.CompilerParams(vmem_limit_bytes=mib * MIB)


def normalise(values):
    center = values - jnp.mean(values, axis=-1, keepdims=True)
    spread = jnp.mean(center * center, axis=-1, keepdims=True)
    inverse = lax.rsqrt(spread + EPS)
    return center * inverse, inverse


def enter_kernel(tok_ref, cot_ref, mod_ref, out_ref):
    features = tok_ref.shape[-1]
    normed, _ = normalise(tok_ref[...].astype(F32))
    hidden = normed * (1.0 + mod_ref[1:2, :]) + mod_ref[0:1, :]
    out_ref[:, :features] = hidden.astype(BF)
    out_ref[:, features:] = (mod_ref[2:3, :] * cot_ref[...].astype(F32)).astype(BF)


def enter(tok, cot, mod):
    rows, features = tok.shape
    return pl.pallas_call(
        enter_kernel,
        out_shape=jax.ShapeDtypeStruct((rows, 2 * features), BF),
        compiler_params=params(16),
        name="enter",
    )(tok, cot, mod)


def project_kernel(heads, head_dim, nb_ref, hb_ref, w_ref, wo_ref, out_ref, scr):
    part = pl.program_id(0)
    features = w_ref.shape[0]
    piece = wo_ref.shape[0]
    tokens = hb_ref.shape[0]
    scr[part] = dot(hb_ref[:, :features], w_ref[...]).T
    rows = pl.ds(pl.multiple_of(part * piece, piece), piece)
    scr[3, rows, :] = dot(wo_ref[...], hb_ref[:, features:], NT)

    @pl.when(part == 2)
    def _():
        left = nb_ref[0].astype(F32)
        right = nb_ref[1].astype(F32)
        row = lax.broadcasted_iota(jnp.int32, (16, tokens), 0)
        marks = jnp.where(row == 0, left, right).astype(BF)
        for h in range(heads):
            block = [scr[p, head_dim * h : head_dim * (h + 1), :] for p in range(4)]
            out_ref[h, : 4 * head_dim, :] = jnp.concatenate(block, axis=0).astype(BF)
            out_ref[h, 4 * head_dim :, :] = marks


def project(hb, w_qkv, w_out, nb, heads, head_dim):
    tokens = hb.shape[0]
    features = w_out.shape[0]
    shape = (heads, 4 * head_dim + 16, tokens)

    def body(*refs):
        project_kernel(heads, head_dim, *refs)

    return pl.pallas_call(
        body,
        grid=(3,),
        in_specs=[
            pl.BlockSpec(memory_space=pltpu.SMEM),
            whole(hb.shape),
            pl.BlockSpec((features, features), lambda p: (0, p)),
            pl.BlockSpec((features // 3, features), lambda p: (p, 0)),
        ],
        out_specs=whole(shape),
        out_shape=jax.ShapeDtypeStruct(shape, BF),
        scratch_shapes=[pltpu.VMEM((4, features, tokens), F32)],
        compiler_params=params(32),
        name="project",
    )(nb, hb, w_qkv, w_out)


def attend_kernel(nb_ref, x_ref, qg_ref, kg_ref, gp_ref, at_ref, qn, kn, rad, qh, kh, vh, gh, krow, vrow, gq, gk, gv):
    cams, _, tokens = x_ref.shape
    dim = qg_ref.shape[0]
    scale = 1.0 / math.sqrt(dim)
    qgain = qg_ref[...]
    kgain = kg_ref[...]
    pad = jnp.zeros((tokens - dim, tokens), F32)

    def prepare(c, _):
        x = x_ref[c, : 4 * dim, :].astype(F32)
        q, k, v, g = (x[dim * i : dim * (i + 1)] for i in range(4))
        rq = lax.rsqrt(jnp.mean(q * q, axis=0, keepdims=True) + EPS)
        rk = lax.rsqrt(jnp.mean(k * k, axis=0, keepdims=True) + EPS)
        q = q * rq
        k = k * rk
        qn[c] = q
        kn[c] = k
        rad[c, 0:1, :] = rq
        rad[c, 1:2, :] = rk
        q = q * qgain
        k = k * kgain
        qh[c] = jnp.concatenate([q, pad], axis=0).astype(BF)
        gh[c] = jnp.concatenate([g, pad], axis=0).astype(BF)
        kh[c] = k.astype(BF)
        vh[c] = v.astype(BF)
        krow[c] = jnp.concatenate([k, pad], axis=0).T.astype(BF)
        vrow[c] = jnp.concatenate([v, pad], axis=0).T.astype(BF)
        return 0

    lax.fori_loop(0, cams, prepare, 0, unroll=2)

    def camera(c, _):
        left = nb_ref[c, 0]
        right = nb_ref[c, 1]
        q = qh[c]
        g = gh[c]
        keys = jnp.concatenate([krow[left], krow[c], krow[right]], axis=0)
        values = jnp.concatenate([vrow[left], vrow[c], vrow[right]], axis=0)
        keys_t = jnp.concatenate([kh[left], kh[c], kh[right]], axis=1)
        values_t = jnp.concatenate([vh[left], vh[c], vh[right]], axis=1)
        e = jnp.exp(dot(keys, q) * scale)
        probs = e * (1.0 / jnp.sum(e, axis=0, keepdims=True))
        low = probs.astype(BF)
        gprobs = dot(values, g)
        centre = jnp.sum(probs * gprobs, axis=0, keepdims=True)
        gs = (probs * (gprobs - centre) * scale).astype(BF)
        at_ref[c] = dot(values_t, low).astype(BF)
        gq[c] = dot(keys_t, gs)
        gk[c] = dot(q, gs, NT)[:dim]
        gv[c] = dot(g, low, NT)[:dim]
        return 0

    lax.fori_loop(0, cams, camera, 0, unroll=2)

    def back(grad, unit, radius, gain):
        shaped = grad * gain
        return (shaped - unit * jnp.mean(shaped * unit, axis=0, keepdims=True)) * radius

    def finish(c, _):
        left = nb_ref[c, 0]
        right = nb_ref[c, 1]
        grad_k = gk[c, :, tokens : 2 * tokens] + gk[left, :, 2 * tokens :] + gk[right, :, :tokens]
        grad_v = gv[c, :, tokens : 2 * tokens] + gv[left, :, 2 * tokens :] + gv[right, :, :tokens]
        grad_q = back(gq[c], qn[c], rad[c, 0:1, :], qgain)
        grad_k = back(grad_k, kn[c], rad[c, 1:2, :], kgain)
        gp_ref[c] = jnp.concatenate([grad_q, grad_k, grad_v], axis=0).astype(BF)
        return 0

    lax.fori_loop(0, cams, finish, 0, unroll=2)


def attend(nb, x, q_gain, k_gain):
    cams, _, tokens = x.shape
    dim = q_gain.shape[0]
    vm = pl.BlockSpec(memory_space=pltpu.VMEM)
    return pl.pallas_call(
        attend_kernel,
        in_specs=[pl.BlockSpec(memory_space=pltpu.SMEM), vm, vm, vm],
        out_specs=[vm, vm],
        out_shape=[
            jax.ShapeDtypeStruct((cams, 3 * dim, tokens), BF),
            jax.ShapeDtypeStruct((cams, dim, tokens), BF),
        ],
        scratch_shapes=[
            pltpu.VMEM((cams, dim, tokens), F32),
            pltpu.VMEM((cams, dim, tokens), F32),
            pltpu.VMEM((cams, 8, tokens), F32),
            pltpu.VMEM((cams, tokens, tokens), BF),
            pltpu.VMEM((cams, dim, tokens), BF),
            pltpu.VMEM((cams, dim, tokens), BF),
            pltpu.VMEM((cams, tokens, tokens), BF),
            pltpu.VMEM((cams, tokens, tokens), BF),
            pltpu.VMEM((cams, tokens, tokens), BF),
            pltpu.VMEM((cams, dim, tokens), F32),
            pltpu.VMEM((cams, dim, 3 * tokens), F32),
            pltpu.VMEM((cams, dim, 3 * tokens), F32),
        ],
        compiler_params=params(32),
        name="attend",
    )(nb, x, q_gain.reshape(dim, 1), k_gain.reshape(dim, 1))


def term_kernel(gp_ref, at_ref, hb_ref, zin_ref, zout_ref, acc, acc_out):
    step = pl.program_id(0)
    pair, width, tokens = gp_ref.shape
    features = hb_ref.shape[-1] // 2
    blocks, rows, _ = zin_ref.shape

    @pl.when(step == 0)
    def _():
        acc[...] = jnp.zeros_like(acc)
        acc_out[...] = jnp.zeros_like(acc_out)

    grads = jnp.concatenate([gp_ref[i] for i in range(pair)], axis=1)
    atts = jnp.concatenate([at_ref[i] for i in range(pair)], axis=1)
    both = hb_ref[...].reshape(pair * tokens, 2 * features)
    acc[:width, :] += dot(grads, both[:, :features])
    acc_out[...] += dot(atts, both[:, features:])

    @pl.when(step == pl.num_programs(0) - 1)
    def _():
        turned = acc[...].T
        for b in range(blocks):
            zin_ref[b] = turned[rows * b : rows * (b + 1), :width].astype(BF)
        zout_ref[...] = acc_out[...].astype(BF)


def terms(gp, at, hb_all, blocks):
    cams, width, tokens = gp.shape
    dim = at.shape[1]
    features = hb_all.shape[-1] // 2
    padded = -(-width // 128) * 128
    rows = features // blocks
    return pl.pallas_call(
        term_kernel,
        grid=(cams // 2,),
        in_specs=[
            pl.BlockSpec((2, width, tokens), lambda s: (s, 0, 0)),
            pl.BlockSpec((2, dim, tokens), lambda s: (s, 0, 0)),
            pl.BlockSpec((2, tokens, 2 * features), lambda s: (s, 0, 0)),
        ],
        out_specs=[whole((blocks, rows, width)), whole((dim, features))],
        out_shape=[
            jax.ShapeDtypeStruct((blocks, rows, width), BF),
            jax.ShapeDtypeStruct((dim, features), BF),
        ],
        scratch_shapes=[pltpu.VMEM((padded, features), F32), pltpu.VMEM((dim, features), F32)],
        compiler_params=params(32),
        name="terms",
    )(gp, at, hb_all)


def leave_kernel(x_ref, w_ref, tok_ref, cot_ref, mod_ref, out_ref, scr, acc):
    part = pl.program_id(0)
    heads, width, _ = x_ref.shape
    dim = width // 3

    @pl.when(part == 0)
    def _():
        for h in range(heads):
            x = x_ref[h].astype(F32)
            for p in range(3):
                scr[p, dim * h : dim * (h + 1), :] = x[dim * p : dim * (p + 1)]
        acc[...] = jnp.zeros_like(acc)

    acc[...] += dot(w_ref[...], scr[part].astype(BF))

    @pl.when(part == 2)
    def _():
        scaled = acc[...].T * (1.0 + mod_ref[1:2, :])
        normed, inverse = normalise(tok_ref[...].astype(F32))
        mean = jnp.mean(scaled, axis=-1, keepdims=True)
        along = jnp.mean(scaled * normed, axis=-1, keepdims=True)
        grad = inverse * (scaled - mean - normed * along)
        out_ref[...] = (cot_ref[...].astype(F32) + grad).astype(BF)


def leave(x, w_qkv, tok, cot, mod):
    rows, features = tok.shape
    return pl.pallas_call(
        leave_kernel,
        grid=(3,),
        in_specs=[
            whole(x.shape),
            pl.BlockSpec((features, features), lambda p: (0, p)),
            whole(tok.shape),
            whole(cot.shape),
            whole(mod.shape),
        ],
        out_specs=whole(tok.shape),
        out_shape=jax.ShapeDtypeStruct(tok.shape, BF),
        scratch_shapes=[
            pltpu.VMEM((3, features, rows), F32),
            pltpu.VMEM((features, rows), F32),
        ],
        compiler_params=params(32),
        name="leave",
    )(x, w_qkv, tok, cot, mod)


def shards(tokens, cotangent, modulation, q_gain, k_gain, w_qkv, w_out, neighbours):
    rows, features = tokens.shape[-2:]
    head_dim = q_gain.shape[0]
    heads = features // head_dim
    cams = lax.axis_size("vt")
    n_dp = lax.axis_size("dp")
    tok = tokens.reshape(rows, features)
    cot = cotangent.reshape(rows, features)
    mod = modulation.reshape(3, features)
    hb = enter(tok, cot, mod)
    hb_all = lax.all_gather(hb, "vt")
    mine = project(hb, w_qkv, w_out, neighbours.reshape(2), heads, head_dim)
    x = lax.all_to_all(mine, "vt", 0, 0)
    nb = x[:, 4 * head_dim : 4 * head_dim + 2, 0].astype(jnp.int32)
    gp, at = attend(nb, x, q_gain, k_gain)
    gp_mine = lax.all_to_all(gp, "vt", 0, 0)
    zin, zout = terms(gp, at, hb_all, cams)
    grad_tokens = leave(gp_mine, w_qkv, tok, cot, mod)
    mixed = lax.all_to_all(zin, "vt", 0, 0)
    split = zout.reshape(head_dim, heads, head_dim).transpose(1, 0, 2)
    payload = jnp.concatenate([mixed, split], axis=-1)
    parts = lax.all_to_all(payload, "dp", 0, 0, tiled=True)
    parts = parts.reshape((n_dp, heads // n_dp) + payload.shape[1:])
    total = jnp.sum(parts.astype(F32), axis=0) * (1.0 / (n_dp * cams))
    full = lax.all_gather(total.astype(BF), "dp", tiled=True)
    width = 3 * head_dim
    grad_in = full[:, :, :width].reshape(heads, head_dim, 3, head_dim)
    grad_in = grad_in.transpose(1, 2, 0, 3).reshape(head_dim, 3 * features)
    grad_out = full[:, :, width:].transpose(1, 0, 2).reshape(head_dim, features)
    return grad_tokens.reshape(tokens.shape), grad_in, grad_out


def solution(mesh):
    placed = (
        P("dp", "vt", None, None, None),
        P("dp", "vt", None, None, None),
        P("dp", "vt", None, None),
        P(),
        P(),
        P(),
        P(),
        P("dp", "vt", None),
    )
    return jax.shard_map(
        shards,
        mesh=mesh,
        in_specs=placed,
        out_specs=(P("dp", "vt", None, None, None), P("vt", None), P("vt", None)),
        check_vma=False,
    )
```

```python
import math

import jax
import jax.numpy as jnp
from jax import lax
from jax.experimental import pallas as pl
from jax.experimental.pallas import tpu as pltpu
from jax.sharding import PartitionSpec as P

BF = jnp.bfloat16
F32 = jnp.float32
EPS = 1e-06
NN = (((1,), (0,)), ((), ()))
NT = (((1,), (1,)), ((), ()))
MIB = 1024 * 1024


def dot(a, b, dims=NN):
    return lax.dot_general(a, b, dims, preferred_element_type=F32)


def whole(shape):
    return pl.BlockSpec(shape, lambda *_: (0,) * len(shape))


def params(mib):
    return pltpu.CompilerParams(vmem_limit_bytes=mib * MIB)


def normalise(values):
    center = values - jnp.mean(values, axis=-1, keepdims=True)
    spread = jnp.mean(center * center, axis=-1, keepdims=True)
    inverse = lax.rsqrt(spread + EPS)
    return center * inverse, inverse


def enter_kernel(tok_ref, cot_ref, mod_ref, out_ref):
    features = tok_ref.shape[-1]
    normed, _ = normalise(tok_ref[...].astype(F32))
    hidden = normed * (1.0 + mod_ref[1:2, :]) + mod_ref[0:1, :]
    out_ref[:, :features] = hidden.astype(BF)
    out_ref[:, features:] = (mod_ref[2:3, :] * cot_ref[...].astype(F32)).astype(BF)


def enter(tok, cot, mod):
    rows, features = tok.shape
    return pl.pallas_call(
        enter_kernel,
        out_shape=jax.ShapeDtypeStruct((rows, 2 * features), BF),
        compiler_params=params(16),
        name="enter",
    )(tok, cot, mod)


def project_kernel(heads, head_dim, nb_ref, hb_ref, w_hbm, wo_hbm, out_ref, w, wo, scr, sem):
    features = wo.shape[0]
    tokens = hb_ref.shape[0]
    copies = [
        pltpu.make_async_copy(w_hbm.at[:, pl.ds(features * p, features)], w.at[p], sem.at[p])
        for p in range(3)
    ]
    copies.append(pltpu.make_async_copy(wo_hbm, wo, sem.at[3]))
    for copy in copies:
        copy.start()
    hidden = hb_ref[:, :features]
    for p in range(3):
        copies[p].wait()
        scr[p] = dot(hidden, w[p]).T
    copies[3].wait()
    scr[3] = dot(wo[...], hb_ref[:, features:], NT)
    left = nb_ref[0].astype(F32)
    right = nb_ref[1].astype(F32)
    row = lax.broadcasted_iota(jnp.int32, (16, tokens), 0)
    marks = jnp.where(row == 0, left, right).astype(BF)
    for h in range(heads):
        block = [scr[p, head_dim * h : head_dim * (h + 1), :] for p in range(4)]
        out_ref[h, : 4 * head_dim, :] = jnp.concatenate(block, axis=0).astype(BF)
        out_ref[h, 4 * head_dim :, :] = marks


def project(hb, w_qkv, w_out, nb, heads, head_dim):
    tokens = hb.shape[0]
    features = w_out.shape[0]
    vm = pl.BlockSpec(memory_space=pltpu.VMEM)
    hbm = pl.BlockSpec(memory_space=pltpu.HBM)

    def body(*refs):
        project_kernel(heads, head_dim, *refs)

    return pl.pallas_call(
        body,
        in_specs=[pl.BlockSpec(memory_space=pltpu.SMEM), vm, hbm, hbm],
        out_specs=vm,
        out_shape=jax.ShapeDtypeStruct((heads, 4 * head_dim + 16, tokens), BF),
        scratch_shapes=[
            pltpu.VMEM((3, features, features), BF),
            pltpu.VMEM((features, features), BF),
            pltpu.VMEM((4, features, tokens), F32),
            pltpu.SemaphoreType.DMA((4,)),
        ],
        compiler_params=params(32),
        name="project",
    )(nb, hb, w_qkv, w_out)


def attend_kernel(nb_ref, x_ref, qg_ref, kg_ref, gp_ref, at_ref, qn, kn, rad, qh, kh, vh, gh, krow, vrow, gq, gk, gv):
    cams, _, tokens = x_ref.shape
    dim = qg_ref.shape[0]
    scale = 1.0 / math.sqrt(dim)
    qgain = qg_ref[...]
    kgain = kg_ref[...]
    pad = jnp.zeros((tokens - dim, tokens), F32)

    def prepare(c, _):
        x = x_ref[c, : 4 * dim, :].astype(F32)
        q, k, v, g = (x[dim * i : dim * (i + 1)] for i in range(4))
        rq = lax.rsqrt(jnp.mean(q * q, axis=0, keepdims=True) + EPS)
        rk = lax.rsqrt(jnp.mean(k * k, axis=0, keepdims=True) + EPS)
        q = q * rq
        k = k * rk
        qn[c] = q
        kn[c] = k
        rad[c, 0:1, :] = rq
        rad[c, 1:2, :] = rk
        q = q * qgain
        k = k * kgain
        qh[c] = jnp.concatenate([q, pad], axis=0).astype(BF)
        gh[c] = jnp.concatenate([g, pad], axis=0).astype(BF)
        kh[c] = k.astype(BF)
        vh[c] = v.astype(BF)
        krow[c] = jnp.concatenate([k, pad], axis=0).T.astype(BF)
        vrow[c] = jnp.concatenate([v, pad], axis=0).T.astype(BF)
        return 0

    lax.fori_loop(0, cams, prepare, 0, unroll=2)

    def camera(c, _):
        left = nb_ref[c, 0]
        right = nb_ref[c, 1]
        q = qh[c]
        g = gh[c]
        keys = jnp.concatenate([krow[left], krow[c], krow[right]], axis=0)
        values = jnp.concatenate([vrow[left], vrow[c], vrow[right]], axis=0)
        keys_t = jnp.concatenate([kh[left], kh[c], kh[right]], axis=1)
        values_t = jnp.concatenate([vh[left], vh[c], vh[right]], axis=1)
        e = jnp.exp(dot(keys, q) * scale)
        probs = e * (1.0 / jnp.sum(e, axis=0, keepdims=True))
        low = probs.astype(BF)
        gprobs = dot(values, g)
        centre = jnp.sum(probs * gprobs, axis=0, keepdims=True)
        gs = (probs * (gprobs - centre) * scale).astype(BF)
        at_ref[c] = dot(values_t, low).astype(BF)
        gq[c] = dot(keys_t, gs)
        gk[c] = dot(q, gs, NT)[:dim]
        gv[c] = dot(g, low, NT)[:dim]
        return 0

    lax.fori_loop(0, cams, camera, 0, unroll=2)

    def back(grad, unit, radius, gain):
        shaped = grad * gain
        return (shaped - unit * jnp.mean(shaped * unit, axis=0, keepdims=True)) * radius

    def finish(c, _):
        left = nb_ref[c, 0]
        right = nb_ref[c, 1]
        grad_k = gk[c, :, tokens : 2 * tokens] + gk[left, :, 2 * tokens :] + gk[right, :, :tokens]
        grad_v = gv[c, :, tokens : 2 * tokens] + gv[left, :, 2 * tokens :] + gv[right, :, :tokens]
        grad_q = back(gq[c], qn[c], rad[c, 0:1, :], qgain)
        grad_k = back(grad_k, kn[c], rad[c, 1:2, :], kgain)
        gp_ref[c] = jnp.concatenate([grad_q, grad_k, grad_v], axis=0).astype(BF)
        return 0

    lax.fori_loop(0, cams, finish, 0, unroll=2)


def attend(nb, x, q_gain, k_gain):
    cams, _, tokens = x.shape
    dim = q_gain.shape[0]
    vm = pl.BlockSpec(memory_space=pltpu.VMEM)
    return pl.pallas_call(
        attend_kernel,
        in_specs=[pl.BlockSpec(memory_space=pltpu.SMEM), vm, vm, vm],
        out_specs=[vm, vm],
        out_shape=[
            jax.ShapeDtypeStruct((cams, 3 * dim, tokens), BF),
            jax.ShapeDtypeStruct((cams, dim, tokens), BF),
        ],
        scratch_shapes=[
            pltpu.VMEM((cams, dim, tokens), F32),
            pltpu.VMEM((cams, dim, tokens), F32),
            pltpu.VMEM((cams, 8, tokens), F32),
            pltpu.VMEM((cams, tokens, tokens), BF),
            pltpu.VMEM((cams, dim, tokens), BF),
            pltpu.VMEM((cams, dim, tokens), BF),
            pltpu.VMEM((cams, tokens, tokens), BF),
            pltpu.VMEM((cams, tokens, tokens), BF),
            pltpu.VMEM((cams, tokens, tokens), BF),
            pltpu.VMEM((cams, dim, tokens), F32),
            pltpu.VMEM((cams, dim, 3 * tokens), F32),
            pltpu.VMEM((cams, dim, 3 * tokens), F32),
        ],
        compiler_params=params(32),
        name="attend",
    )(nb, x, q_gain.reshape(dim, 1), k_gain.reshape(dim, 1))


def term_kernel(gp_ref, at_ref, hb_hbm, zin_ref, zout_ref, hb, acc, acc_out, sem):
    cams, width, tokens = gp_ref.shape
    features = hb.shape[-1] // 2
    blocks, rows, _ = zin_ref.shape
    copies = [
        pltpu.make_async_copy(
            hb_hbm.at[pl.ds(2 * tokens * s, 2 * tokens)], hb.at[pl.ds(2 * tokens * s, 2 * tokens)], sem.at[s]
        )
        for s in range(cams // 2)
    ]
    for copy in copies:
        copy.start()
    acc[width:, :] = jnp.zeros_like(acc[width:, :])
    for s in range(cams // 2):
        grads = jnp.concatenate([gp_ref[2 * s], gp_ref[2 * s + 1]], axis=1)
        atts = jnp.concatenate([at_ref[2 * s], at_ref[2 * s + 1]], axis=1)
        copies[s].wait()
        both = hb[2 * tokens * s : 2 * tokens * (s + 1), :]
        one = dot(grads, both[:, :features])
        two = dot(atts, both[:, features:])
        acc[:width, :] = one if s == 0 else acc[:width, :] + one
        acc_out[...] = two if s == 0 else acc_out[...] + two
    turned = acc[...].T
    for b in range(blocks):
        zin_ref[b] = turned[rows * b : rows * (b + 1), :width].astype(BF)
    zout_ref[...] = acc_out[...].astype(BF)


def terms(gp, at, hb_all, blocks):
    cams, width, tokens = gp.shape
    dim = at.shape[1]
    features = hb_all.shape[-1] // 2
    padded = -(-width // 128) * 128
    rows = features // blocks
    vm = pl.BlockSpec(memory_space=pltpu.VMEM)
    return pl.pallas_call(
        term_kernel,
        in_specs=[vm, vm, pl.BlockSpec(memory_space=pltpu.HBM)],
        out_specs=[vm, vm],
        out_shape=[
            jax.ShapeDtypeStruct((blocks, rows, width), BF),
            jax.ShapeDtypeStruct((dim, features), BF),
        ],
        scratch_shapes=[
            pltpu.VMEM((cams * tokens, 2 * features), BF),
            pltpu.VMEM((padded, features), F32),
            pltpu.VMEM((dim, features), F32),
            pltpu.SemaphoreType.DMA((cams // 2,)),
        ],
        compiler_params=params(32),
        name="terms",
    )(gp, at, hb_all)


def leave_kernel(x_ref, w_ref, tok_ref, cot_ref, mod_ref, out_ref, scr, acc):
    part = pl.program_id(0)
    heads, width, _ = x_ref.shape
    dim = width // 3

    @pl.when(part == 0)
    def _():
        for h in range(heads):
            x = x_ref[h].astype(F32)
            for p in range(3):
                scr[p, dim * h : dim * (h + 1), :] = x[dim * p : dim * (p + 1)]
        acc[...] = jnp.zeros_like(acc)

    acc[...] += dot(w_ref[...], scr[part].astype(BF))

    @pl.when(part == 2)
    def _():
        scaled = acc[...].T * (1.0 + mod_ref[1:2, :])
        normed, inverse = normalise(tok_ref[...].astype(F32))
        mean = jnp.mean(scaled, axis=-1, keepdims=True)
        along = jnp.mean(scaled * normed, axis=-1, keepdims=True)
        grad = inverse * (scaled - mean - normed * along)
        out_ref[...] = (cot_ref[...].astype(F32) + grad).astype(BF)


def leave(x, w_qkv, tok, cot, mod):
    rows, features = tok.shape
    return pl.pallas_call(
        leave_kernel,
        grid=(3,),
        in_specs=[
            whole(x.shape),
            pl.BlockSpec((features, features), lambda p: (0, p)),
            whole(tok.shape),
            whole(cot.shape),
            whole(mod.shape),
        ],
        out_specs=whole(tok.shape),
        out_shape=jax.ShapeDtypeStruct(tok.shape, BF),
        scratch_shapes=[
            pltpu.VMEM((3, features, rows), F32),
            pltpu.VMEM((features, rows), F32),
        ],
        compiler_params=params(32),
        name="leave",
    )(x, w_qkv, tok, cot, mod)


def pack_kernel(me_ref, in_ref, out_ref, *outs):
    heads, rows, width = in_ref.shape
    dim = rows
    own = me_ref[0] % 4
    spread = outs[-1]
    for h in range(heads):
        spread[h, :, :width] = in_ref[h]
        spread[h, :, width:] = out_ref[:, dim * h : dim * (h + 1)]
    for k in range(4):
        for a in range(4):
            outs[k][a] = spread[4 * a + (own ^ k)]


def pack(me, mixed, zout):
    heads, rows, width = mixed.shape
    total = width + rows
    vm = pl.BlockSpec(memory_space=pltpu.VMEM)
    return pl.pallas_call(
        pack_kernel,
        in_specs=[pl.BlockSpec(memory_space=pltpu.SMEM), vm, vm],
        out_specs=[vm] * 4,
        out_shape=[jax.ShapeDtypeStruct((4, rows, total), BF)] * 4,
        scratch_shapes=[pltpu.VMEM((heads, rows, total), BF)],
        compiler_params=params(16),
        name="pack",
    )(me, mixed, zout)


def fold_kernel(me_ref, a_ref, b_ref, c_ref, d_ref, *outs):
    far = me_ref[0] // 4
    for k in range(4):
        a = far ^ k
        total = a_ref[a].astype(F32) + b_ref[a].astype(F32) + c_ref[a].astype(F32) + d_ref[a].astype(F32)
        outs[k][...] = total.astype(BF)


def fold(me, parts):
    vm = pl.BlockSpec(memory_space=pltpu.VMEM)
    return pl.pallas_call(
        fold_kernel,
        in_specs=[pl.BlockSpec(memory_space=pltpu.SMEM)] + [vm] * 4,
        out_specs=[vm] * 4,
        out_shape=[jax.ShapeDtypeStruct(parts[0].shape[1:], BF)] * 4,
        compiler_params=params(16),
        name="fold",
    )(me, *parts)


def final_kernel(me_ref, a_ref, b_ref, c_ref, d_ref, in_ref, out_ref, all_ref):
    rows, total = a_ref.shape[1:]
    heads = 16
    near = me_ref[0] % 4
    far = me_ref[0] // 4
    for k, ref in enumerate((a_ref, b_ref, c_ref, d_ref)):
        all_ref[k] = ref[...]
    blocks = [all_ref[near ^ (h % 4), far ^ (h // 4)].astype(F32) for h in range(heads)]
    dim = total // 4
    for p in range(4):
        line = jnp.concatenate([b[:, dim * p : dim * (p + 1)] for b in blocks], axis=1).astype(BF)
        if p < 3:
            in_ref[:, heads * dim * p : heads * dim * (p + 1)] = line
        else:
            out_ref[...] = line


def final(me, parts):
    _, rows, total = parts[0].shape
    wide = 16 * (total // 4)
    vm = pl.BlockSpec(memory_space=pltpu.VMEM)
    return pl.pallas_call(
        final_kernel,
        in_specs=[pl.BlockSpec(memory_space=pltpu.SMEM)] + [vm] * 4,
        out_specs=[vm] * 2,
        out_shape=[
            jax.ShapeDtypeStruct((rows, 3 * wide), BF),
            jax.ShapeDtypeStruct((rows, wide), BF),
        ],
        scratch_shapes=[pltpu.VMEM((4,) + parts[0].shape, BF)],
        compiler_params=params(16),
        name="final",
    )(me, *parts)


def swap(part, bits):
    return lax.ppermute(part, "dp", [(i, i ^ bits) for i in range(16)])


def over_rows(mixed, zout, factor):
    me = lax.axis_index("dp").reshape(1)
    sent = pack(me, mixed, zout)
    sums = fold(me, [sent[0]] + [swap(sent[k], k) for k in (1, 2, 3)])
    mine = sums[0].astype(F32)
    for k in (1, 2, 3):
        mine = mine + swap(sums[k], 4 * k).astype(F32)
    mine = (mine * factor).astype(BF)
    group = jnp.stack([mine] + [swap(mine, 4 * k) for k in (1, 2, 3)])
    return final(me, [group] + [swap(group, k) for k in (1, 2, 3)])


def over_rows_plain(mixed, zout, factor):
    heads, dim, width = mixed.shape
    total = (lax.psum(mixed.astype(F32), "dp") * factor).astype(BF)
    grad_in = total.reshape(heads, dim, 3, dim).transpose(1, 2, 0, 3).reshape(dim, heads * width)
    return grad_in, (lax.psum(zout.astype(F32), "dp") * factor).astype(BF)


def shards(tokens, cotangent, modulation, q_gain, k_gain, w_qkv, w_out, neighbours):
    rows, features = tokens.shape[-2:]
    head_dim = q_gain.shape[0]
    heads = features // head_dim
    cams = lax.axis_size("vt")
    n_dp = lax.axis_size("dp")
    tok = tokens.reshape(rows, features)
    cot = cotangent.reshape(rows, features)
    mod = modulation.reshape(3, features)
    hb = enter(tok, cot, mod)
    hb_all = lax.all_gather(hb, "vt", tiled=True)
    mine = project(hb, w_qkv, w_out, neighbours.reshape(2), heads, head_dim)
    x = lax.all_to_all(mine, "vt", 0, 0)
    nb = x[:, 4 * head_dim : 4 * head_dim + 2, 0].astype(jnp.int32)
    gp, at = attend(nb, x, q_gain, k_gain)
    gp_mine = lax.all_to_all(gp, "vt", 0, 0)
    hb_all, gp_mine = lax.optimization_barrier((hb_all, gp_mine))
    zin, zout = terms(gp, at, hb_all, cams)
    grad_tokens = leave(gp_mine, w_qkv, tok, cot, mod)
    mixed = lax.all_to_all(zin, "vt", 0, 0)
    reduce = over_rows if n_dp == 16 and heads == 16 else over_rows_plain
    grad_in, grad_out = reduce(mixed, zout, 1.0 / (n_dp * cams))
    return grad_tokens.reshape(tokens.shape), grad_in, grad_out


def solution(mesh):
    placed = (
        P("dp", "vt", None, None, None),
        P("dp", "vt", None, None, None),
        P("dp", "vt", None, None),
        P(),
        P(),
        P(),
        P(),
        P("dp", "vt", None),
    )
    return jax.shard_map(
        shards,
        mesh=mesh,
        in_specs=placed,
        out_specs=(P("dp", "vt", None, None, None), P("vt", None), P("vt", None)),
        check_vma=False,
    )
```

```python
import math

import jax
import jax.numpy as jnp
from jax import lax
from jax.experimental import pallas as pl
from jax.experimental.pallas import tpu as pltpu
from jax.sharding import PartitionSpec as P

BF = jnp.bfloat16
F32 = jnp.float32
EPS = 1e-06
NN = (((1,), (0,)), ((), ()))
NT = (((1,), (1,)), ((), ()))
MIB = 1024 * 1024


def dot(a, b, dims=NN):
    return lax.dot_general(a, b, dims, preferred_element_type=F32)


def whole(shape):
    return pl.BlockSpec(shape, lambda *_: (0,) * len(shape))


def params(mib):
    return pltpu.CompilerParams(vmem_limit_bytes=mib * MIB)


def normalise(values):
    center = values - jnp.mean(values, axis=-1, keepdims=True)
    spread = jnp.mean(center * center, axis=-1, keepdims=True)
    inverse = lax.rsqrt(spread + EPS)
    return center * inverse, inverse


def line(mod_ref, i):
    count = mod_ref.shape[0] // 3
    return jnp.concatenate([mod_ref[count * i + t : count * i + t + 1, :] for t in range(count)], axis=1)


def enter_kernel(tok_ref, cot_ref, mod_ref, out_ref):
    features = tok_ref.shape[-1]
    normed, _ = normalise(tok_ref[...].astype(F32))
    hidden = normed * (1.0 + line(mod_ref, 1)) + line(mod_ref, 0)
    out_ref[:, :features] = hidden.astype(BF)
    out_ref[:, features:] = (line(mod_ref, 2) * cot_ref[...].astype(F32)).astype(BF)


def enter(tok, cot, mod):
    rows, features = tok.shape
    return pl.pallas_call(
        enter_kernel,
        out_shape=jax.ShapeDtypeStruct((rows, 2 * features), BF),
        compiler_params=params(58),
        name="enter",
    )(tok, cot, mod)


def project_kernel(heads, head_dim, nb_ref, hb_ref, w_hbm, wo_hbm, out_ref, w, wo, scr, sem):
    features = wo.shape[0]
    tokens = hb_ref.shape[0]
    copies = [
        pltpu.make_async_copy(w_hbm.at[:, pl.ds(features * p, features)], w.at[p], sem.at[p])
        for p in range(3)
    ]
    copies.append(pltpu.make_async_copy(wo_hbm, wo, sem.at[3]))
    for copy in copies:
        copy.start()
    hidden = hb_ref[:, :features]
    for p in range(3):
        copies[p].wait()
        scr[p] = dot(hidden, w[p]).T
    copies[3].wait()
    scr[3] = dot(wo[...], hb_ref[:, features:], NT)
    left = nb_ref[0].astype(F32)
    right = nb_ref[1].astype(F32)
    row = lax.broadcasted_iota(jnp.int32, (16, tokens), 0)
    marks = jnp.where(row == 0, left, right).astype(BF)
    for h in range(heads):
        block = [scr[p, head_dim * h : head_dim * (h + 1), :] for p in range(4)]
        out_ref[h, : 4 * head_dim, :] = jnp.concatenate(block, axis=0).astype(BF)
        out_ref[h, 4 * head_dim :, :] = marks


def project(hb, w_qkv, w_out, nb, heads, head_dim):
    tokens = hb.shape[0]
    features = w_out.shape[0]
    vm = pl.BlockSpec(memory_space=pltpu.VMEM)
    hbm = pl.BlockSpec(memory_space=pltpu.HBM)

    def body(*refs):
        project_kernel(heads, head_dim, *refs)

    return pl.pallas_call(
        body,
        in_specs=[pl.BlockSpec(memory_space=pltpu.SMEM), vm, hbm, hbm],
        out_specs=vm,
        out_shape=jax.ShapeDtypeStruct((heads, 4 * head_dim + 16, tokens), BF),
        scratch_shapes=[
            pltpu.VMEM((3, features, features), BF),
            pltpu.VMEM((features, features), BF),
            pltpu.VMEM((4, features, tokens), F32),
            pltpu.SemaphoreType.DMA((4,)),
        ],
        compiler_params=params(58),
        name="project",
    )(nb, hb, w_qkv, w_out)


def attend_kernel(nb_ref, x_ref, qg_ref, kg_ref, gp_ref, at_ref, qn, kn, rad, qh, kh, vh, gh, krow, vrow, gq, gk, gv):
    cams, _, tokens = x_ref.shape
    dim = qg_ref.shape[0]
    scale = 1.0 / math.sqrt(dim)
    qgain = qg_ref[...]
    kgain = kg_ref[...]
    pad = jnp.zeros((tokens - dim, tokens), F32)

    def prepare(c, _):
        x = x_ref[c, : 4 * dim, :].astype(F32)
        q, k, v, g = (x[dim * i : dim * (i + 1)] for i in range(4))
        rq = lax.rsqrt(jnp.mean(q * q, axis=0, keepdims=True) + EPS)
        rk = lax.rsqrt(jnp.mean(k * k, axis=0, keepdims=True) + EPS)
        q = q * rq
        k = k * rk
        qn[c] = q
        kn[c] = k
        rad[c, 0:1, :] = rq
        rad[c, 1:2, :] = rk
        q = q * qgain
        k = k * kgain
        qh[c] = jnp.concatenate([q, pad], axis=0).astype(BF)
        gh[c] = jnp.concatenate([g, pad], axis=0).astype(BF)
        kh[c] = k.astype(BF)
        vh[c] = v.astype(BF)
        krow[c] = jnp.concatenate([k, pad], axis=0).T.astype(BF)
        vrow[c] = jnp.concatenate([v, pad], axis=0).T.astype(BF)
        return 0

    lax.fori_loop(0, cams, prepare, 0, unroll=2)

    def camera(c, _):
        left = nb_ref[c, 0]
        right = nb_ref[c, 1]
        q = qh[c]
        g = gh[c]
        keys = jnp.concatenate([krow[left], krow[c], krow[right]], axis=0)
        values = jnp.concatenate([vrow[left], vrow[c], vrow[right]], axis=0)
        keys_t = jnp.concatenate([kh[left], kh[c], kh[right]], axis=1)
        values_t = jnp.concatenate([vh[left], vh[c], vh[right]], axis=1)
        e = jnp.exp(dot(keys, q) * scale)
        probs = e * (1.0 / jnp.sum(e, axis=0, keepdims=True))
        low = probs.astype(BF)
        gprobs = dot(values, g)
        centre = jnp.sum(probs * gprobs, axis=0, keepdims=True)
        gs = (probs * (gprobs - centre) * scale).astype(BF)
        at_ref[c] = dot(values_t, low).astype(BF)
        gq[c] = dot(keys_t, gs)
        gk[c] = dot(q, gs, NT)[:dim]
        gv[c] = dot(g, low, NT)[:dim]
        return 0

    lax.fori_loop(0, cams, camera, 0, unroll=2)

    def back(grad, unit, radius, gain):
        shaped = grad * gain
        return (shaped - unit * jnp.mean(shaped * unit, axis=0, keepdims=True)) * radius

    def finish(c, _):
        left = nb_ref[c, 0]
        right = nb_ref[c, 1]
        grad_k = gk[c, :, tokens : 2 * tokens] + gk[left, :, 2 * tokens :] + gk[right, :, :tokens]
        grad_v = gv[c, :, tokens : 2 * tokens] + gv[left, :, 2 * tokens :] + gv[right, :, :tokens]
        grad_q = back(gq[c], qn[c], rad[c, 0:1, :], qgain)
        grad_k = back(grad_k, kn[c], rad[c, 1:2, :], kgain)
        gp_ref[c] = jnp.concatenate([grad_q, grad_k, grad_v], axis=0).astype(BF)
        return 0

    lax.fori_loop(0, cams, finish, 0, unroll=2)


def attend(nb, x, q_gain, k_gain):
    cams, _, tokens = x.shape
    dim = q_gain.shape[0]
    vm = pl.BlockSpec(memory_space=pltpu.VMEM)
    return pl.pallas_call(
        attend_kernel,
        in_specs=[pl.BlockSpec(memory_space=pltpu.SMEM), vm, vm, vm],
        out_specs=[vm, vm],
        out_shape=[
            jax.ShapeDtypeStruct((cams, 3 * dim, tokens), BF),
            jax.ShapeDtypeStruct((cams, dim, tokens), BF),
        ],
        scratch_shapes=[
            pltpu.VMEM((cams, dim, tokens), F32),
            pltpu.VMEM((cams, dim, tokens), F32),
            pltpu.VMEM((cams, 8, tokens), F32),
            pltpu.VMEM((cams, tokens, tokens), BF),
            pltpu.VMEM((cams, dim, tokens), BF),
            pltpu.VMEM((cams, dim, tokens), BF),
            pltpu.VMEM((cams, tokens, tokens), BF),
            pltpu.VMEM((cams, tokens, tokens), BF),
            pltpu.VMEM((cams, tokens, tokens), BF),
            pltpu.VMEM((cams, dim, tokens), F32),
            pltpu.VMEM((cams, dim, 3 * tokens), F32),
            pltpu.VMEM((cams, dim, 3 * tokens), F32),
        ],
        compiler_params=params(32),
        name="attend",
    )(nb, x, q_gain.reshape(dim, 1), k_gain.reshape(dim, 1))


def term_kernel(gp_ref, at_ref, hb_hbm, zin_ref, zout_ref, hb, acc, acc_out, sem):
    cams, width, tokens = gp_ref.shape
    features = hb.shape[-1] // 2
    blocks, rows, _ = zin_ref.shape
    copies = [
        pltpu.make_async_copy(
            hb_hbm.at[pl.ds(2 * tokens * s, 2 * tokens)], hb.at[pl.ds(2 * tokens * s, 2 * tokens)], sem.at[s]
        )
        for s in range(cams // 2)
    ]
    for copy in copies:
        copy.start()
    acc[width:, :] = jnp.zeros_like(acc[width:, :])
    for s in range(cams // 2):
        grads = jnp.concatenate([gp_ref[2 * s], gp_ref[2 * s + 1]], axis=1)
        atts = jnp.concatenate([at_ref[2 * s], at_ref[2 * s + 1]], axis=1)
        copies[s].wait()
        both = hb[2 * tokens * s : 2 * tokens * (s + 1), :]
        one = dot(grads, both[:, :features])
        two = dot(atts, both[:, features:])
        acc[:width, :] = one if s == 0 else acc[:width, :] + one
        acc_out[...] = two if s == 0 else acc_out[...] + two
    turned = acc[...].T
    for b in range(blocks):
        zin_ref[b] = turned[rows * b : rows * (b + 1), :width].astype(BF)
    zout_ref[...] = acc_out[...].astype(BF)


def terms(gp, at, hb_all, blocks):
    cams, width, tokens = gp.shape
    dim = at.shape[1]
    features = hb_all.shape[-1] // 2
    padded = -(-width // 128) * 128
    rows = features // blocks
    vm = pl.BlockSpec(memory_space=pltpu.VMEM)
    return pl.pallas_call(
        term_kernel,
        in_specs=[vm, vm, pl.BlockSpec(memory_space=pltpu.HBM)],
        out_specs=[vm, vm],
        out_shape=[
            jax.ShapeDtypeStruct((blocks, rows, width), BF),
            jax.ShapeDtypeStruct((dim, features), BF),
        ],
        scratch_shapes=[
            pltpu.VMEM((cams * tokens, 2 * features), BF),
            pltpu.VMEM((padded, features), F32),
            pltpu.VMEM((dim, features), F32),
            pltpu.SemaphoreType.DMA((cams // 2,)),
        ],
        compiler_params=params(55),
        name="terms",
    )(gp, at, hb_all)


def leave_kernel(x_ref, w_ref, tok_ref, cot_ref, mod_ref, out_ref, scr, acc):
    part = pl.program_id(0)
    heads, width, _ = x_ref.shape
    dim = width // 3

    @pl.when(part == 0)
    def _():
        for h in range(heads):
            x = x_ref[h].astype(F32)
            for p in range(3):
                scr[p, dim * h : dim * (h + 1), :] = x[dim * p : dim * (p + 1)]
        acc[...] = jnp.zeros_like(acc)

    acc[...] += dot(w_ref[...], scr[part].astype(BF))

    @pl.when(part == 2)
    def _():
        scaled = acc[...].T * (1.0 + line(mod_ref, 1))
        normed, inverse = normalise(tok_ref[...].astype(F32))
        mean = jnp.mean(scaled, axis=-1, keepdims=True)
        along = jnp.mean(scaled * normed, axis=-1, keepdims=True)
        grad = inverse * (scaled - mean - normed * along)
        out_ref[...] = (cot_ref[...].astype(F32) + grad).astype(BF)


def leave(x, w_qkv, tok, cot, mod):
    rows, features = tok.shape
    return pl.pallas_call(
        leave_kernel,
        grid=(3,),
        in_specs=[
            whole(x.shape),
            pl.BlockSpec((features, features), lambda p: (0, p)),
            whole(tok.shape),
            whole(cot.shape),
            whole(mod.shape),
        ],
        out_specs=whole(tok.shape),
        out_shape=jax.ShapeDtypeStruct(tok.shape, BF),
        scratch_shapes=[
            pltpu.VMEM((3, features, rows), F32),
            pltpu.VMEM((features, rows), F32),
        ],
        compiler_params=params(58),
        name="leave",
    )(x, w_qkv, tok, cot, mod)


def near(i):
    return i % 2 + 2 * (i // 8)


def far(i):
    return (i // 2) % 4


def near_bits(k):
    return k % 2 + 8 * (k // 2)


def pack_kernel(me_ref, in_ref, out_ref, *outs):
    blocks, dim, width = in_ref.shape
    spread = outs[-1]
    for b in range(blocks):
        spread[b, :, :width] = in_ref[b]
        spread[b, :, width:] = out_ref[:, dim * b : dim * (b + 1)]
    me = me_ref[0]
    for k in range(4):
        for a in range(4):
            outs[k][a] = spread[near_bits(near(me) ^ k) + 2 * a]


def pack(me, zin, zout):
    blocks, dim, width = zin.shape
    total = width + dim
    vm = pl.BlockSpec(memory_space=pltpu.VMEM)
    return pl.pallas_call(
        pack_kernel,
        in_specs=[pl.BlockSpec(memory_space=pltpu.SMEM), vm, vm],
        out_specs=[vm] * 4,
        out_shape=[jax.ShapeDtypeStruct((4, dim, total), BF)] * 4,
        scratch_shapes=[pltpu.VMEM((blocks, dim, total), BF)],
        compiler_params=params(16),
        name="pack",
    )(me, zin, zout)


def fold_kernel(me_ref, a_ref, b_ref, c_ref, d_ref, *outs):
    for k in range(4):
        a = far(me_ref[0]) ^ k
        total = a_ref[a].astype(F32) + b_ref[a].astype(F32) + c_ref[a].astype(F32) + d_ref[a].astype(F32)
        outs[k][...] = total.astype(BF)


def fold(me, parts):
    vm = pl.BlockSpec(memory_space=pltpu.VMEM)
    return pl.pallas_call(
        fold_kernel,
        in_specs=[pl.BlockSpec(memory_space=pltpu.SMEM)] + [vm] * 4,
        out_specs=[vm] * 4,
        out_shape=[jax.ShapeDtypeStruct(parts[0].shape[1:], BF)] * 4,
        compiler_params=params(16),
        name="fold",
    )(me, *parts)


def close_kernel(factor, a_ref, b_ref, c_ref, d_ref, in_ref, out_ref):
    width = in_ref.shape[1]
    total = a_ref[...].astype(F32) + b_ref[...].astype(F32) + c_ref[...].astype(F32) + d_ref[...].astype(F32)
    total = (total * factor).astype(BF)
    in_ref[...] = total[:, :width]
    out_ref[...] = total[:, width:]


def close(parts, factor):
    dim, total = parts[0].shape
    vm = pl.BlockSpec(memory_space=pltpu.VMEM)

    def body(*refs):
        close_kernel(factor, *refs)

    return pl.pallas_call(
        body,
        in_specs=[vm] * 4,
        out_specs=[vm] * 2,
        out_shape=[
            jax.ShapeDtypeStruct((dim, total - dim), BF),
            jax.ShapeDtypeStruct((dim, dim), BF),
        ],
        compiler_params=params(16),
        name="close",
    )(*parts)


def final_kernel(me_ref, a_ref, b_ref, c_ref, d_ref, in_ref, out_ref, all_ref):
    total = a_ref.shape[2]
    heads = 16
    me = me_ref[0]
    for k, ref in enumerate((a_ref, b_ref, c_ref, d_ref)):
        all_ref[k] = ref[...]
    blocks = [all_ref[near(me) ^ near(h), far(me) ^ far(h)].astype(F32) for h in range(heads)]
    dim = total // 4
    for p in range(4):
        part = jnp.concatenate([b[:, dim * p : dim * (p + 1)] for b in blocks], axis=1).astype(BF)
        if p < 3:
            in_ref[:, heads * dim * p : heads * dim * (p + 1)] = part
        else:
            out_ref[...] = part


def final(me, parts):
    _, rows, total = parts[0].shape
    wide = 16 * (total // 4)
    vm = pl.BlockSpec(memory_space=pltpu.VMEM)
    return pl.pallas_call(
        final_kernel,
        in_specs=[pl.BlockSpec(memory_space=pltpu.SMEM)] + [vm] * 4,
        out_specs=[vm] * 2,
        out_shape=[
            jax.ShapeDtypeStruct((rows, 3 * wide), BF),
            jax.ShapeDtypeStruct((rows, wide), BF),
        ],
        scratch_shapes=[pltpu.VMEM((4,) + parts[0].shape, BF)],
        compiler_params=params(16),
        name="final",
    )(me, *parts)


def swap(part, bits):
    return lax.ppermute(part, "dp", [(i, i ^ bits) for i in range(16)])


def over_rows(me, parts, factor):
    sums = fold(me, parts)
    part_in, part_out = close([sums[0]] + [swap(sums[k], 2 * k) for k in (1, 2, 3)], factor)
    turn = [(16 * a + b, 16 * b + a) for a in range(16) for b in range(16)]
    mine = jnp.concatenate([lax.ppermute(part_in, ("dp", "vt"), turn), part_out], axis=1)
    group = jnp.stack([mine] + [swap(mine, 2 * k) for k in (1, 2, 3)])
    return final(me, [group] + [swap(group, near_bits(k)) for k in (1, 2, 3)])


def over_rows_plain(zin, zout, factor):
    mixed = lax.all_to_all(zin, "vt", 0, 0)
    heads, dim, width = mixed.shape
    total = (lax.psum(mixed.astype(F32), "dp") * factor).astype(BF)
    grad_in = total.reshape(heads, dim, 3, dim).transpose(1, 2, 0, 3).reshape(dim, heads * width)
    return grad_in, (lax.psum(zout.astype(F32), "dp") * factor).astype(BF)


def shards(tokens, cotangent, modulation, q_gain, k_gain, w_qkv, w_out, neighbours):
    rows, features = tokens.shape[-2:]
    head_dim = q_gain.shape[0]
    heads = features // head_dim
    cams = lax.axis_size("vt")
    n_dp = lax.axis_size("dp")
    tok = tokens.reshape(rows, features)
    cot = cotangent.reshape(rows, features)
    mod = modulation.reshape(3 * features // 128, 128)
    hb = enter(tok, cot, mod)
    hb_all = lax.all_gather(hb, "vt", tiled=True)
    mine = project(hb, w_qkv, w_out, neighbours.reshape(2), heads, head_dim)
    x = lax.all_to_all(mine, "vt", 0, 0)
    nb = x[:, 4 * head_dim : 4 * head_dim + 2, 0].astype(jnp.int32)
    gp, at = attend(nb, x, q_gain, k_gain)
    zin, zout = terms(gp, at, hb_all, cams)
    factor = 1.0 / (n_dp * cams)
    if n_dp == 16 and cams == 16 and heads == 16:
        me = lax.axis_index("dp").reshape(1)
        sent = pack(me, zin, zout)
        gp, *sent = lax.optimization_barrier((gp, *sent))
        parts = [sent[0]] + [swap(sent[k], near_bits(k)) for k in (1, 2, 3)]
        gp_mine = lax.all_to_all(gp, "vt", 0, 0)
        gp_mine, *parts = lax.optimization_barrier((gp_mine, *parts))
        grad_in, grad_out = over_rows(me, parts, factor)
    else:
        grad_in, grad_out = over_rows_plain(zin, zout, factor)
        gp_mine = lax.all_to_all(gp, "vt", 0, 0)
    grad_tokens = leave(gp_mine, w_qkv, tok, cot, mod)
    return grad_tokens.reshape(tokens.shape), grad_in, grad_out


def solution(mesh):
    placed = (
        P("dp", "vt", None, None, None),
        P("dp", "vt", None, None, None),
        P("dp", "vt", None, None),
        P(),
        P(),
        P(),
        P(),
        P("dp", "vt", None),
    )
    return jax.shard_map(
        shards,
        mesh=mesh,
        in_specs=placed,
        out_specs=(P("dp", "vt", None, None, None), P("vt", None), P("vt", None)),
        check_vma=False,
    )
```

```python
import math

import jax
import jax.numpy as jnp
from jax import lax
from jax.experimental import pallas as pl
from jax.experimental.pallas import tpu as pltpu
from jax.sharding import PartitionSpec as P

BF = jnp.bfloat16
F32 = jnp.float32
EPS = 1e-06
NN = (((1,), (0,)), ((), ()))
NT = (((1,), (1,)), ((), ()))
MIB = 1024 * 1024


def dot(a, b, dims=NN):
    return lax.dot_general(a, b, dims, preferred_element_type=F32)


def whole(shape):
    return pl.BlockSpec(shape, lambda *_: (0,) * len(shape))


def params(mib):
    return pltpu.CompilerParams(vmem_limit_bytes=mib * MIB)


def normalise(values):
    center = values - jnp.mean(values, axis=-1, keepdims=True)
    spread = jnp.mean(center * center, axis=-1, keepdims=True)
    inverse = lax.rsqrt(spread + EPS)
    return center * inverse, inverse


def line(mod_ref, i):
    return mod_ref[i : i + 1, :]


def enter_kernel(tok_ref, cot_ref, mod_ref, out_ref):
    features = tok_ref.shape[-1]
    normed, _ = normalise(tok_ref[...].astype(F32))
    hidden = normed * (1.0 + line(mod_ref, 1)) + line(mod_ref, 0)
    out_ref[:, :features] = hidden.astype(BF)
    out_ref[:, features:] = (line(mod_ref, 2) * cot_ref[...].astype(F32)).astype(BF)


def enter(tok, cot, mod):
    rows, features = tok.shape
    return pl.pallas_call(
        enter_kernel,
        out_shape=jax.ShapeDtypeStruct((rows, 2 * features), BF),
        compiler_params=params(58),
        name="enter",
    )(tok, cot, mod)


def project_kernel(heads, head_dim, nb_ref, hb_ref, w_hbm, wo_hbm, out_ref, w, wo, scr, sem):
    features = wo.shape[0]
    tokens = hb_ref.shape[0]
    copies = [
        pltpu.make_async_copy(w_hbm.at[:, pl.ds(features * p, features)], w.at[p], sem.at[p])
        for p in range(3)
    ]
    copies.append(pltpu.make_async_copy(wo_hbm, wo, sem.at[3]))
    for copy in copies:
        copy.start()
    hidden = hb_ref[:, :features]
    for p in range(3):
        copies[p].wait()
        scr[p] = dot(hidden, w[p]).T
    copies[3].wait()
    scr[3] = dot(wo[...], hb_ref[:, features:], NT)
    left = nb_ref[0].astype(F32)
    right = nb_ref[1].astype(F32)
    row = lax.broadcasted_iota(jnp.int32, (16, tokens), 0)
    marks = jnp.where(row == 0, left, right).astype(BF)
    for h in range(heads):
        block = [scr[p, head_dim * h : head_dim * (h + 1), :] for p in range(4)]
        out_ref[h, : 4 * head_dim, :] = jnp.concatenate(block, axis=0).astype(BF)
        out_ref[h, 4 * head_dim :, :] = marks


def project(hb, w_qkv, w_out, nb, heads, head_dim):
    tokens = hb.shape[0]
    features = w_out.shape[0]
    vm = pl.BlockSpec(memory_space=pltpu.VMEM)
    hbm = pl.BlockSpec(memory_space=pltpu.HBM)

    def body(*refs):
        project_kernel(heads, head_dim, *refs)

    return pl.pallas_call(
        body,
        in_specs=[pl.BlockSpec(memory_space=pltpu.SMEM), vm, hbm, hbm],
        out_specs=vm,
        out_shape=jax.ShapeDtypeStruct((heads, 4 * head_dim + 16, tokens), BF),
        scratch_shapes=[
            pltpu.VMEM((3, features, features), BF),
            pltpu.VMEM((features, features), BF),
            pltpu.VMEM((4, features, tokens), F32),
            pltpu.SemaphoreType.DMA((4,)),
        ],
        compiler_params=params(58),
        name="project",
    )(nb, hb, w_qkv, w_out)


def attend_kernel(nb_ref, x_ref, qg_ref, kg_ref, gp_ref, at_ref, qn, kn, rad, qh, kh, vh, gh, krow, vrow, gq, gk, gv):
    cams, _, tokens = x_ref.shape
    dim = qg_ref.shape[0]
    scale = 1.0 / math.sqrt(dim)
    qgain = qg_ref[...]
    kgain = kg_ref[...]
    pad = jnp.zeros((tokens - dim, tokens), F32)

    def prepare(c, _):
        x = x_ref[c, : 4 * dim, :].astype(F32)
        q, k, v, g = (x[dim * i : dim * (i + 1)] for i in range(4))
        rq = lax.rsqrt(jnp.mean(q * q, axis=0, keepdims=True) + EPS)
        rk = lax.rsqrt(jnp.mean(k * k, axis=0, keepdims=True) + EPS)
        q = q * rq
        k = k * rk
        qn[c] = q
        kn[c] = k
        rad[c, 0:1, :] = rq
        rad[c, 1:2, :] = rk
        q = q * qgain
        k = k * kgain
        qh[c] = jnp.concatenate([q, pad], axis=0).astype(BF)
        gh[c] = jnp.concatenate([g, pad], axis=0).astype(BF)
        kh[c] = k.astype(BF)
        vh[c] = v.astype(BF)
        krow[c] = jnp.concatenate([k, pad], axis=0).T.astype(BF)
        vrow[c] = jnp.concatenate([v, pad], axis=0).T.astype(BF)
        return 0

    lax.fori_loop(0, cams, prepare, 0, unroll=2)

    def camera(c, _):
        left = nb_ref[c, 0]
        right = nb_ref[c, 1]
        q = qh[c]
        g = gh[c]
        keys = jnp.concatenate([krow[left], krow[c], krow[right]], axis=0)
        values = jnp.concatenate([vrow[left], vrow[c], vrow[right]], axis=0)
        keys_t = jnp.concatenate([kh[left], kh[c], kh[right]], axis=1)
        values_t = jnp.concatenate([vh[left], vh[c], vh[right]], axis=1)
        e = jnp.exp(dot(keys, q) * scale)
        probs = e * (1.0 / jnp.sum(e, axis=0, keepdims=True))
        low = probs.astype(BF)
        gprobs = dot(values, g)
        centre = jnp.sum(probs * gprobs, axis=0, keepdims=True)
        gs = (probs * (gprobs - centre) * scale).astype(BF)
        at_ref[c] = dot(values_t, low).astype(BF)
        gq[c] = dot(keys_t, gs)
        gk[c] = dot(q, gs, NT)[:dim]
        gv[c] = dot(g, low, NT)[:dim]
        return 0

    lax.fori_loop(0, cams, camera, 0, unroll=2)

    def back(grad, unit, radius, gain):
        shaped = grad * gain
        return (shaped - unit * jnp.mean(shaped * unit, axis=0, keepdims=True)) * radius

    def finish(c, _):
        left = nb_ref[c, 0]
        right = nb_ref[c, 1]
        grad_k = gk[c, :, tokens : 2 * tokens] + gk[left, :, 2 * tokens :] + gk[right, :, :tokens]
        grad_v = gv[c, :, tokens : 2 * tokens] + gv[left, :, 2 * tokens :] + gv[right, :, :tokens]
        grad_q = back(gq[c], qn[c], rad[c, 0:1, :], qgain)
        grad_k = back(grad_k, kn[c], rad[c, 1:2, :], kgain)
        gp_ref[c] = jnp.concatenate([grad_q, grad_k, grad_v], axis=0).astype(BF)
        return 0

    lax.fori_loop(0, cams, finish, 0, unroll=2)


def attend(nb, x, q_gain, k_gain):
    cams, _, tokens = x.shape
    dim = q_gain.shape[0]
    vm = pl.BlockSpec(memory_space=pltpu.VMEM)
    return pl.pallas_call(
        attend_kernel,
        in_specs=[pl.BlockSpec(memory_space=pltpu.SMEM), vm, vm, vm],
        out_specs=[vm, vm],
        out_shape=[
            jax.ShapeDtypeStruct((cams, 3 * dim, tokens), BF),
            jax.ShapeDtypeStruct((cams, dim, tokens), BF),
        ],
        scratch_shapes=[
            pltpu.VMEM((cams, dim, tokens), F32),
            pltpu.VMEM((cams, dim, tokens), F32),
            pltpu.VMEM((cams, 8, tokens), F32),
            pltpu.VMEM((cams, tokens, tokens), BF),
            pltpu.VMEM((cams, dim, tokens), BF),
            pltpu.VMEM((cams, dim, tokens), BF),
            pltpu.VMEM((cams, tokens, tokens), BF),
            pltpu.VMEM((cams, tokens, tokens), BF),
            pltpu.VMEM((cams, tokens, tokens), BF),
            pltpu.VMEM((cams, dim, tokens), F32),
            pltpu.VMEM((cams, dim, 3 * tokens), F32),
            pltpu.VMEM((cams, dim, 3 * tokens), F32),
        ],
        compiler_params=params(32),
        name="attend",
    )(nb, x, q_gain.reshape(dim, 1), k_gain.reshape(dim, 1))


def near(i):
    return i % 2 + 2 * (i // 8)


def far(i):
    return (i // 2) % 4


def near_bits(k):
    return k % 2 + 8 * (k // 2)


def term_kernel(me_ref, gp_ref, at_ref, hb_hbm, a_ref, b_ref, c_ref, d_ref, hb, acc, acc_out, spread, sem):
    cams, width, tokens = gp_ref.shape
    features = hb.shape[-1] // 2
    blocks, dim, _ = spread.shape
    copies = [
        pltpu.make_async_copy(
            hb_hbm.at[pl.ds(2 * tokens * s, 2 * tokens)], hb.at[pl.ds(2 * tokens * s, 2 * tokens)], sem.at[s]
        )
        for s in range(cams // 2)
    ]
    for copy in copies:
        copy.start()
    acc[width:, :] = jnp.zeros_like(acc[width:, :])
    for s in range(cams // 2):
        grads = jnp.concatenate([gp_ref[2 * s], gp_ref[2 * s + 1]], axis=1)
        atts = jnp.concatenate([at_ref[2 * s], at_ref[2 * s + 1]], axis=1)
        copies[s].wait()
        both = hb[2 * tokens * s : 2 * tokens * (s + 1), :]
        one = dot(grads, both[:, :features])
        two = dot(atts, both[:, features:])
        acc[:width, :] = one if s == 0 else acc[:width, :] + one
        acc_out[...] = two if s == 0 else acc_out[...] + two
    turned = acc[...].T
    for b in range(blocks):
        spread[b, :, :width] = turned[dim * b : dim * (b + 1), :width].astype(BF)
        spread[b, :, width:] = acc_out[:, dim * b : dim * (b + 1)].astype(BF)
    me = me_ref[0]
    for k, ref in enumerate((a_ref, b_ref, c_ref, d_ref)):
        for a in range(4):
            ref[a] = spread[near_bits(near(me) ^ k) + 2 * a]


def terms(me, gp, at, hb_all):
    cams, width, tokens = gp.shape
    dim = at.shape[1]
    features = hb_all.shape[-1] // 2
    padded = -(-width // 128) * 128
    vm = pl.BlockSpec(memory_space=pltpu.VMEM)
    return pl.pallas_call(
        term_kernel,
        in_specs=[pl.BlockSpec(memory_space=pltpu.SMEM), vm, vm, pl.BlockSpec(memory_space=pltpu.HBM)],
        out_specs=[vm] * 4,
        out_shape=[jax.ShapeDtypeStruct((4, dim, width + dim), BF)] * 4,
        scratch_shapes=[
            pltpu.VMEM((cams * tokens, 2 * features), BF),
            pltpu.VMEM((padded, features), F32),
            pltpu.VMEM((dim, features), F32),
            pltpu.VMEM((features // dim, dim, width + dim), BF),
            pltpu.SemaphoreType.DMA((cams // 2,)),
        ],
        compiler_params=params(54),
        name="terms",
    )(me, gp, at, hb_all)


def leave_kernel(x_ref, w_ref, tok_ref, cot_ref, mod_ref, out_ref, scr, acc):
    part = pl.program_id(0)
    heads, width, _ = x_ref.shape
    dim = width // 3

    @pl.when(part == 0)
    def _():
        for h in range(heads):
            x = x_ref[h].astype(F32)
            for p in range(3):
                scr[p, dim * h : dim * (h + 1), :] = x[dim * p : dim * (p + 1)]
        acc[...] = jnp.zeros_like(acc)

    acc[...] += dot(w_ref[...], scr[part].astype(BF))

    @pl.when(part == 2)
    def _():
        scaled = acc[...].T * (1.0 + line(mod_ref, 1))
        normed, inverse = normalise(tok_ref[...].astype(F32))
        mean = jnp.mean(scaled, axis=-1, keepdims=True)
        along = jnp.mean(scaled * normed, axis=-1, keepdims=True)
        grad = inverse * (scaled - mean - normed * along)
        out_ref[...] = (cot_ref[...].astype(F32) + grad).astype(BF)


def leave(x, w_qkv, tok, cot, mod):
    rows, features = tok.shape
    return pl.pallas_call(
        leave_kernel,
        grid=(3,),
        in_specs=[
            whole(x.shape),
            pl.BlockSpec((features, features), lambda p: (0, p)),
            whole(tok.shape),
            whole(cot.shape),
            whole(mod.shape),
        ],
        out_specs=whole(tok.shape),
        out_shape=jax.ShapeDtypeStruct(tok.shape, BF),
        scratch_shapes=[
            pltpu.VMEM((3, features, rows), F32),
            pltpu.VMEM((features, rows), F32),
        ],
        compiler_params=params(58),
        name="leave",
    )(x, w_qkv, tok, cot, mod)


def fold_kernel(me_ref, a_ref, b_ref, c_ref, d_ref, *outs):
    dim, width = outs[0].shape
    me = far(me_ref[0])
    for k in range(4):
        a = me ^ k
        total = a_ref[a].astype(F32) + b_ref[a].astype(F32) + c_ref[a].astype(F32) + d_ref[a].astype(F32)
        outs[k][...] = total[:, :width].astype(BF)
    sums = []
    for a in range(4):
        total = a_ref[a].astype(F32) + b_ref[a].astype(F32) + c_ref[a].astype(F32) + d_ref[a].astype(F32)
        sums.append(total[:, width:])
    outs[4][...] = jnp.concatenate(sums, axis=1).astype(BF)


def fold(me, parts):
    _, dim, total = parts[0].shape
    vm = pl.BlockSpec(memory_space=pltpu.VMEM)
    shapes = [jax.ShapeDtypeStruct((dim, total - dim), BF)] * 4 + [jax.ShapeDtypeStruct((dim, 4 * dim), BF)]
    return pl.pallas_call(
        fold_kernel,
        in_specs=[pl.BlockSpec(memory_space=pltpu.SMEM)] + [vm] * 4,
        out_specs=[vm] * 5,
        out_shape=shapes,
        compiler_params=params(16),
        name="fold",
    )(me, *parts)


def close_kernel(factor, a_ref, b_ref, c_ref, d_ref, rest_ref, out_ref):
    width = a_ref.shape[1]
    total = a_ref[...].astype(F32) + b_ref[...].astype(F32) + c_ref[...].astype(F32) + d_ref[...].astype(F32)
    both = jnp.concatenate([total * factor, rest_ref[...].astype(F32)], axis=1)
    out_ref[...] = both.astype(BF)


def close(parts, rest, factor):
    dim, width = parts[0].shape
    vm = pl.BlockSpec(memory_space=pltpu.VMEM)

    def body(*refs):
        close_kernel(factor, *refs)

    return pl.pallas_call(
        body,
        in_specs=[vm] * 5,
        out_specs=vm,
        out_shape=jax.ShapeDtypeStruct((dim, width + 4 * dim), BF),
        compiler_params=params(16),
        name="close",
    )(*parts, rest)


def join_kernel(factor, me_ref, a_ref, b_ref, c_ref, d_ref, out_ref):
    dim = a_ref.shape[0]
    width = out_ref.shape[2] - dim
    me = far(me_ref[0])
    four = [ref[...].astype(F32) for ref in (a_ref, b_ref, c_ref, d_ref)]
    rest = (four[0] + four[1] + four[2] + four[3])[:, width:] * factor
    for k in range(4):
        out_ref[me ^ k, :, :width] = four[k][:, :width].astype(BF)
    for a in range(4):
        out_ref[a, :, width:] = rest[:, dim * a : dim * (a + 1)].astype(BF)


def join(me, parts, factor):
    dim, wide = parts[0].shape
    vm = pl.BlockSpec(memory_space=pltpu.VMEM)

    def body(*refs):
        join_kernel(factor, *refs)

    return pl.pallas_call(
        body,
        in_specs=[pl.BlockSpec(memory_space=pltpu.SMEM)] + [vm] * 4,
        out_specs=vm,
        out_shape=jax.ShapeDtypeStruct((4, dim, wide - 3 * dim), BF),
        compiler_params=params(16),
        name="join",
    )(me, *parts)


def final_kernel(me_ref, a_ref, b_ref, c_ref, d_ref, in_ref, out_ref, all_ref):
    total = a_ref.shape[2]
    heads = 16
    me = me_ref[0]
    for k, ref in enumerate((a_ref, b_ref, c_ref, d_ref)):
        all_ref[k] = ref[...]
    blocks = [all_ref[near(me) ^ near(h), far(h)].astype(F32) for h in range(heads)]
    dim = total // 4
    for p in range(4):
        part = jnp.concatenate([b[:, dim * p : dim * (p + 1)] for b in blocks], axis=1).astype(BF)
        if p < 3:
            in_ref[:, heads * dim * p : heads * dim * (p + 1)] = part
        else:
            out_ref[...] = part


def final(me, parts):
    _, rows, total = parts[0].shape
    wide = 16 * (total // 4)
    vm = pl.BlockSpec(memory_space=pltpu.VMEM)
    return pl.pallas_call(
        final_kernel,
        in_specs=[pl.BlockSpec(memory_space=pltpu.SMEM)] + [vm] * 4,
        out_specs=[vm] * 2,
        out_shape=[
            jax.ShapeDtypeStruct((rows, 3 * wide), BF),
            jax.ShapeDtypeStruct((rows, wide), BF),
        ],
        scratch_shapes=[pltpu.VMEM((4,) + parts[0].shape, BF)],
        compiler_params=params(16),
        name="final",
    )(me, *parts)


def swap(part, bits):
    return lax.ppermute(part, "dp", [(i, i ^ bits) for i in range(16)])


def cross(part, bits):
    return lax.ppermute(part, ("dp", "vt"), [(16 * a + b, 16 * b + (a ^ bits)) for a in range(16) for b in range(16)])


def chunk(me, parts, factor):
    *sums, rest = fold(me, parts)
    return close([cross(sums[k], 2 * k) for k in range(4)], rest, factor)


def shards(tokens, cotangent, modulation, q_gain, k_gain, w_qkv, w_out, neighbours):
    rows, features = tokens.shape[-2:]
    head_dim = q_gain.shape[0]
    heads = features // head_dim
    factor = 1.0 / (lax.axis_size("dp") * lax.axis_size("vt"))
    me = lax.axis_index("dp").reshape(1)
    tok = tokens.reshape(rows, features)
    cot = cotangent.reshape(rows, features)
    mod = modulation.reshape(3, features)
    hb = enter(tok, cot, mod)
    hb_all = lax.all_gather(hb, "vt", tiled=True)
    mine = project(hb, w_qkv, w_out, neighbours.reshape(2), heads, head_dim)
    x = lax.all_to_all(mine, "vt", 0, 0)
    nb = x[:, 4 * head_dim : 4 * head_dim + 2, 0].astype(jnp.int32)
    gp, at = attend(nb, x, q_gain, k_gain)
    sent = terms(me, gp, at, hb_all)
    parts = [sent[0]] + [swap(sent[k], near_bits(k)) for k in (1, 2, 3)]
    gp, *parts = lax.optimization_barrier((gp, *parts))
    gp_mine = lax.all_to_all(gp, "vt", 0, 0)
    mine = chunk(me, parts, factor)
    group = join(me, [mine] + [swap(mine, 2 * k) for k in (1, 2, 3)], factor)
    gp_mine, group = lax.optimization_barrier((gp_mine, group))
    grad_in, grad_out = final(me, [group] + [swap(group, near_bits(k)) for k in (1, 2, 3)])
    grad_tokens = leave(gp_mine, w_qkv, tok, cot, mod)
    return grad_tokens.reshape(tokens.shape), grad_in, grad_out


def solution(mesh):
    placed = (
        P("dp", "vt", None, None, None),
        P("dp", "vt", None, None, None),
        P("dp", "vt", None, None),
        P(),
        P(),
        P(),
        P(),
        P("dp", "vt", None),
    )
    return jax.shard_map(
        shards,
        mesh=mesh,
        in_specs=placed,
        out_specs=(P("dp", "vt", None, None, None), P("vt", None), P("vt", None)),
        check_vma=False,
    )
```

```python
import math

import jax
import jax.numpy as jnp
from jax import lax
from jax.experimental import pallas as pl
from jax.experimental.pallas import tpu as pltpu
from jax.sharding import PartitionSpec as P

BF = jnp.bfloat16
F32 = jnp.float32
EPS = 1e-06
NN = (((1,), (0,)), ((), ()))
NT = (((1,), (1,)), ((), ()))
MIB = 1024 * 1024
LANES = 128


def dot(a, b, dims=NN):
    return lax.dot_general(a, b, dims, preferred_element_type=F32)


def whole(shape):
    return pl.BlockSpec(shape, lambda *_: (0,) * len(shape))


def params(mib):
    return pltpu.CompilerParams(vmem_limit_bytes=mib * MIB)


def normalise(values):
    center = values - jnp.mean(values, axis=-1, keepdims=True)
    spread = jnp.mean(center * center, axis=-1, keepdims=True)
    inverse = lax.rsqrt(spread + EPS)
    return center * inverse, inverse


def line(mod_ref, i):
    return mod_ref[i : i + 1, :]


def enter_kernel(nb_ref, tok_ref, cot_ref, mod_ref, out_ref):
    rows, features = tok_ref.shape
    normed, _ = normalise(tok_ref[...].astype(F32))
    hidden = normed * (1.0 + line(mod_ref, 1)) + line(mod_ref, 0)
    out_ref[:, :features] = hidden.astype(BF)
    lane = lax.broadcasted_iota(jnp.int32, (rows, LANES), 1)
    marks = jnp.where(lane == 0, nb_ref[0].astype(F32), nb_ref[1].astype(F32))
    out_ref[:, features : features + LANES] = marks.astype(BF)
    out_ref[:, features + LANES :] = (line(mod_ref, 2) * cot_ref[...].astype(F32)).astype(BF)


def enter(nb, tok, cot, mod):
    rows, features = tok.shape
    vm = pl.BlockSpec(memory_space=pltpu.VMEM)
    return pl.pallas_call(
        enter_kernel,
        in_specs=[pl.BlockSpec(memory_space=pltpu.SMEM), vm, vm, vm],
        out_specs=vm,
        out_shape=jax.ShapeDtypeStruct((rows, 2 * features + LANES), BF),
        compiler_params=params(32),
        name="enter",
    )(nb, tok, cot, mod)


def weights_kernel(head_ref, w_hbm, wo_hbm, w_ref, wo_ref, win, wo_win, sem):
    features, wide = w_ref.shape
    dim = wo_ref.shape[0]
    head = head_ref[0]
    copies = []
    gaps = []
    for p in range(3):
        first = features * p + dim * head
        start = jnp.minimum(first // LANES * LANES, 3 * features - wide)
        gaps.append(first - start)
        window = w_hbm.at[:, pl.ds(pl.multiple_of(start, LANES), wide)]
        copies.append(pltpu.make_async_copy(window, win.at[p], sem.at[p]))
    first = dim * head
    start = first // 16 * 16
    window = wo_hbm.at[pl.ds(pl.multiple_of(start, 16), wo_win.shape[0])]
    copies.append(pltpu.make_async_copy(window, wo_win, sem.at[3]))
    for copy in copies:
        copy.start()
    row = lax.broadcasted_iota(jnp.int32, (wide, wide), 0)
    column = lax.broadcasted_iota(jnp.int32, (wide, wide), 1)
    total = jnp.zeros((features, wide), F32)
    for p in range(3):
        inside = (column >= dim * p) & (column < dim * (p + 1))
        pick = jnp.where(inside & (row == column - dim * p + gaps[p]), 1.0, 0.0).astype(BF)
        copies[p].wait()
        total = total + dot(win[p], pick)
    w_ref[...] = total.astype(BF)
    row = lax.broadcasted_iota(jnp.int32, (dim, wo_win.shape[0]), 0)
    column = lax.broadcasted_iota(jnp.int32, (dim, wo_win.shape[0]), 1)
    pick = jnp.where(column == row + (first - start), 1.0, 0.0).astype(BF)
    copies[3].wait()
    wo_ref[...] = dot(pick, wo_win[...]).astype(BF)


def weights(head, w_qkv, w_out, dim):
    features = w_out.shape[0]
    wide = 2 * LANES
    vm = pl.BlockSpec(memory_space=pltpu.VMEM)
    hbm = pl.BlockSpec(memory_space=pltpu.HBM)
    return pl.pallas_call(
        weights_kernel,
        in_specs=[pl.BlockSpec(memory_space=pltpu.SMEM), hbm, hbm],
        out_specs=[vm, vm],
        out_shape=[
            jax.ShapeDtypeStruct((features, wide), BF),
            jax.ShapeDtypeStruct((dim, features), BF),
        ],
        scratch_shapes=[
            pltpu.VMEM((3, features, wide), BF),
            pltpu.VMEM((dim + 8, features), BF),
            pltpu.SemaphoreType.DMA((4,)),
        ],
        compiler_params=params(58),
        name="weights",
    )(head, w_qkv, w_out)


def place(y, x, core):
    return (y * 4 + x) * 2 + core


def move(part, dy, dx, dc):
    pairs = [
        (place(y, x, c), place(y ^ dy, (x + dx) % 4, c ^ dc)) for y in range(2) for x in range(4) for c in range(2)
    ]
    return lax.ppermute(part, "vt", pairs)


def mix_kernel(a_ref, b_ref, c_ref, up_ref, down_ref, over_ref):
    half = down_ref.shape[1] // 2
    first = a_ref.shape[1] - half
    up_ref[:, :first] = a_ref[:, :first]
    up_ref[:, first:] = c_ref[:, :first]
    down_ref[:, :half] = b_ref[:, first:]
    down_ref[:, half:] = c_ref[:, first:]
    over_ref[:, :half] = a_ref[:, first:]
    over_ref[:, half:] = b_ref[:, :first]


def mix(a, b, c, first):
    rows, wide = a.shape
    half = wide - first
    return pl.pallas_call(
        mix_kernel,
        out_shape=[
            jax.ShapeDtypeStruct((rows, 2 * first), BF),
            jax.ShapeDtypeStruct((rows, 2 * half), BF),
            jax.ShapeDtypeStruct((rows, wide), BF),
        ],
        compiler_params=params(16),
        name="mix",
    )(a, b, c)


def gather(hb, first, w, wo):
    half = hb.shape[1] - first
    low = move(hb, 0, 1, 0)
    high = move(hb, 0, -1, 0)
    side = move(hb, 1, 0, 0)
    twin = move(hb, 0, 0, 1)
    low, high, side, w, wo = lax.optimization_barrier((low, high, side, w, wo))
    up, down, over = mix(low, high, side, first)
    up, down, over = move(up, 0, 1, 0), move(down, 0, -1, 0), move(over, 1, 0, 0)
    twins = [move(a, 0, 0, 1) for a in (low, high, side)]
    far_up = move(up[:, first:], 0, 1, 0)
    far_down = move(down[:, half:], 0, -1, 0)
    twins += [move(a, 0, 0, 1) for a in (up, down, over)]
    twins += [move(a, 0, 0, 1) for a in (far_up, far_down)]
    arrays = [hb, low, high, side, up, down, over, far_up, far_down, twin] + twins
    slots = []
    for dc in range(2):
        n = 9 * dc
        slots += [
            ((0, 0, dc), (n, 0), (n, first)),
            ((0, 3, dc), (n + 1, 0), (n + 1, first)),
            ((0, 1, dc), (n + 2, 0), (n + 2, first)),
            ((1, 0, dc), (n + 3, 0), (n + 3, first)),
            ((0, 2, dc), (n + 4, 0), (n + 5, 0)),
            ((1, 3, dc), (n + 4, first), (n + 6, 0)),
            ((1, 1, dc), (n + 6, half), (n + 5, half)),
            ((1, 2, dc), (n + 7, 0), (n + 8, 0)),
        ]
    return arrays, slots, w, wo


def near(i):
    return i % 2 + 2 * (i // 8)


def far(i):
    return (i // 2) % 4


def near_bits(k):
    return k % 2 + 8 * (k // 2)


def heads_kernel(slots, dim, features, cams, me_ref, vt_ref, w_ref, wo_ref, qg_ref, kg_ref, *refs):
    count = len({n for _, *pairs in slots for n, _ in pairs})
    arrays, refs = refs[:count], refs[count:]
    gp_ref, *sends, nb, at, qn, kn, rad, qh, kh, vh, gh, krow, vrow, gq, gk, gv, acc, acc_out, spread = refs
    tokens = arrays[0].shape[0]
    width = 3 * dim
    scale = 1.0 / math.sqrt(dim)
    qgain = qg_ref[...]
    kgain = kg_ref[...]
    pad = jnp.zeros((tokens - dim, tokens), F32)
    vt = vt_ref[0]
    y, x, core = vt // 8, vt // 2 % 4, vt % 2
    cameras = [place((y + dy) % 2, (x + dx) % 4, (core + dc) % 2) for (dy, dx, dc), _, _ in slots]

    def hidden(s):
        n, lane = slots[s][1]
        return arrays[n][:, lane : lane + features]

    def branch(s):
        n, lane = slots[s][2]
        return arrays[n][:, lane : lane + features]

    for s, c in enumerate(cameras):
        n, lane = slots[s][1]
        marks = arrays[n][:16, lane + features : lane + features + LANES].astype(F32)
        nb[c, 0] = marks[0, 0].astype(jnp.int32)
        nb[c, 1] = marks[0, 1].astype(jnp.int32)
        turned = dot(hidden(s), w_ref[...]).T
        q, k, v = (turned[dim * i : dim * (i + 1)] for i in range(3))
        g = dot(wo_ref[...], branch(s), NT)
        rq = lax.rsqrt(jnp.mean(q * q, axis=0, keepdims=True) + EPS)
        rk = lax.rsqrt(jnp.mean(k * k, axis=0, keepdims=True) + EPS)
        q = q * rq
        k = k * rk
        qn[c] = q
        kn[c] = k
        rad[c, 0:1, :] = rq
        rad[c, 1:2, :] = rk
        q = q * qgain
        k = k * kgain
        qh[c] = jnp.concatenate([q, pad], axis=0).astype(BF)
        gh[c] = jnp.concatenate([g, pad], axis=0).astype(BF)
        kh[c] = k.astype(BF)
        vh[c] = v.astype(BF)
        krow[c] = jnp.concatenate([k, pad], axis=0).T.astype(BF)
        vrow[c] = jnp.concatenate([v, pad], axis=0).T.astype(BF)

    def camera(c, _):
        left = nb[c, 0]
        right = nb[c, 1]
        q = qh[c]
        g = gh[c]
        keys = jnp.concatenate([krow[left], krow[c], krow[right]], axis=0)
        values = jnp.concatenate([vrow[left], vrow[c], vrow[right]], axis=0)
        keys_t = jnp.concatenate([kh[left], kh[c], kh[right]], axis=1)
        values_t = jnp.concatenate([vh[left], vh[c], vh[right]], axis=1)
        e = jnp.exp(dot(keys, q) * scale)
        probs = e * (1.0 / jnp.sum(e, axis=0, keepdims=True))
        low = probs.astype(BF)
        gprobs = dot(values, g)
        centre = jnp.sum(probs * gprobs, axis=0, keepdims=True)
        gs = (probs * (gprobs - centre) * scale).astype(BF)
        at[c] = dot(values_t, low).astype(BF)
        gq[c] = dot(keys_t, gs)
        gk[c] = dot(q, gs, NT)[:dim]
        gv[c] = dot(g, low, NT)[:dim]
        return 0

    lax.fori_loop(0, cams, camera, 0, unroll=4)

    def back(grad, unit, radius, gain):
        shaped = grad * gain
        return (shaped - unit * jnp.mean(shaped * unit, axis=0, keepdims=True)) * radius

    def finish(c, _):
        left = nb[c, 0]
        right = nb[c, 1]
        grad_k = gk[c, :, tokens : 2 * tokens] + gk[left, :, 2 * tokens :] + gk[right, :, :tokens]
        grad_v = gv[c, :, tokens : 2 * tokens] + gv[left, :, 2 * tokens :] + gv[right, :, :tokens]
        grad_q = back(gq[c], qn[c], rad[c, 0:1, :], qgain)
        grad_k = back(grad_k, kn[c], rad[c, 1:2, :], kgain)
        gp_ref[c] = jnp.concatenate([grad_q, grad_k, grad_v], axis=0).astype(BF)
        return 0

    lax.fori_loop(0, cams, finish, 0, unroll=4)

    acc[width:, :] = jnp.zeros_like(acc[width:, :])
    for s in range(0, cams, 4):
        four = range(s, s + 4)
        grads = jnp.concatenate([gp_ref[cameras[i]] for i in four], axis=1)
        atts = jnp.concatenate([at[cameras[i]] for i in four], axis=1)
        one = dot(grads, jnp.concatenate([hidden(i) for i in four], axis=0))
        two = dot(atts, jnp.concatenate([branch(i) for i in four], axis=0))
        acc[:width, :] = one if s == 0 else acc[:width, :] + one
        acc_out[...] = two if s == 0 else acc_out[...] + two
    turned = acc[...].T
    for b in range(features // dim):
        spread[b, :, :width] = turned[dim * b : dim * (b + 1), :width].astype(BF)
        spread[b, :, width:] = acc_out[:, dim * b : dim * (b + 1)].astype(BF)
    me = me_ref[0]
    for k, ref in enumerate(sends):
        for a in range(4):
            ref[a] = spread[near_bits(near(me) ^ k) + 2 * a]


def heads(me, vt, w, wo, q_gain, k_gain, arrays, slots):
    dim, features = wo.shape
    tokens = arrays[0].shape[0]
    cams = len(slots)
    vm = pl.BlockSpec(memory_space=pltpu.VMEM)
    sm = pl.BlockSpec(memory_space=pltpu.SMEM)

    def body(*refs):
        heads_kernel(slots, dim, features, cams, *refs)

    return pl.pallas_call(
        body,
        in_specs=[sm, sm] + [vm] * (4 + len(arrays)),
        out_specs=[vm] * 5,
        out_shape=[jax.ShapeDtypeStruct((cams, 3 * dim, tokens), BF)]
        + [jax.ShapeDtypeStruct((4, dim, 4 * dim), BF)] * 4,
        scratch_shapes=[
            pltpu.SMEM((cams, 2), jnp.int32),
            pltpu.VMEM((cams, dim, tokens), BF),
            pltpu.VMEM((cams, dim, tokens), F32),
            pltpu.VMEM((cams, dim, tokens), F32),
            pltpu.VMEM((cams, 8, tokens), F32),
            pltpu.VMEM((cams, tokens, tokens), BF),
            pltpu.VMEM((cams, dim, tokens), BF),
            pltpu.VMEM((cams, dim, tokens), BF),
            pltpu.VMEM((cams, tokens, tokens), BF),
            pltpu.VMEM((cams, tokens, tokens), BF),
            pltpu.VMEM((cams, tokens, tokens), BF),
            pltpu.VMEM((cams, dim, tokens), F32),
            pltpu.VMEM((cams, dim, 3 * tokens), F32),
            pltpu.VMEM((cams, dim, 3 * tokens), F32),
            pltpu.VMEM((2 * LANES, features), F32),
            pltpu.VMEM((dim, features), F32),
            pltpu.VMEM((features // dim, dim, 4 * dim), BF),
        ],
        compiler_params=params(36),
        name="heads",
    )(me, vt, w, wo, q_gain.reshape(dim, 1), k_gain.reshape(dim, 1), *arrays)


def leave_kernel(x_ref, w_ref, tok_ref, cot_ref, mod_ref, out_ref, scr, acc):
    part = pl.program_id(0)
    heads, width, _ = x_ref.shape
    dim = width // 3

    @pl.when(part == 0)
    def _():
        for h in range(heads):
            x = x_ref[h].astype(F32)
            for p in range(3):
                scr[p, dim * h : dim * (h + 1), :] = x[dim * p : dim * (p + 1)]
        acc[...] = jnp.zeros_like(acc)

    acc[...] += dot(w_ref[...], scr[part].astype(BF))

    @pl.when(part == 2)
    def _():
        scaled = acc[...].T * (1.0 + line(mod_ref, 1))
        normed, inverse = normalise(tok_ref[...].astype(F32))
        mean = jnp.mean(scaled, axis=-1, keepdims=True)
        along = jnp.mean(scaled * normed, axis=-1, keepdims=True)
        grad = inverse * (scaled - mean - normed * along)
        out_ref[...] = (cot_ref[...].astype(F32) + grad).astype(BF)


def leave(x, w_qkv, tok, cot, mod):
    rows, features = tok.shape
    return pl.pallas_call(
        leave_kernel,
        grid=(3,),
        in_specs=[
            whole(x.shape),
            pl.BlockSpec((features, features), lambda p: (0, p)),
            whole(tok.shape),
            whole(cot.shape),
            whole(mod.shape),
        ],
        out_specs=whole(tok.shape),
        out_shape=jax.ShapeDtypeStruct(tok.shape, BF),
        scratch_shapes=[
            pltpu.VMEM((3, features, rows), F32),
            pltpu.VMEM((features, rows), F32),
        ],
        compiler_params=params(58),
        name="leave",
    )(x, w_qkv, tok, cot, mod)


def fold_kernel(me_ref, a_ref, b_ref, c_ref, d_ref, *outs):
    dim, width = outs[0].shape
    me = far(me_ref[0])
    for k in range(4):
        a = me ^ k
        total = a_ref[a].astype(F32) + b_ref[a].astype(F32) + c_ref[a].astype(F32) + d_ref[a].astype(F32)
        outs[k][...] = total[:, :width].astype(BF)
    sums = []
    for a in range(4):
        total = a_ref[a].astype(F32) + b_ref[a].astype(F32) + c_ref[a].astype(F32) + d_ref[a].astype(F32)
        sums.append(total[:, width:])
    outs[4][...] = jnp.concatenate(sums, axis=1).astype(BF)


def fold(me, parts):
    _, dim, total = parts[0].shape
    vm = pl.BlockSpec(memory_space=pltpu.VMEM)
    shapes = [jax.ShapeDtypeStruct((dim, total - dim), BF)] * 4 + [jax.ShapeDtypeStruct((dim, 4 * dim), BF)]
    return pl.pallas_call(
        fold_kernel,
        in_specs=[pl.BlockSpec(memory_space=pltpu.SMEM)] + [vm] * 4,
        out_specs=[vm] * 5,
        out_shape=shapes,
        compiler_params=params(16),
        name="fold",
    )(me, *parts)


def close_kernel(factor, a_ref, b_ref, c_ref, d_ref, rest_ref, out_ref):
    width = a_ref.shape[1]
    total = a_ref[...].astype(F32) + b_ref[...].astype(F32) + c_ref[...].astype(F32) + d_ref[...].astype(F32)
    both = jnp.concatenate([total * factor, rest_ref[...].astype(F32)], axis=1)
    out_ref[...] = both.astype(BF)


def close(parts, rest, factor):
    dim, width = parts[0].shape
    vm = pl.BlockSpec(memory_space=pltpu.VMEM)

    def body(*refs):
        close_kernel(factor, *refs)

    return pl.pallas_call(
        body,
        in_specs=[vm] * 5,
        out_specs=vm,
        out_shape=jax.ShapeDtypeStruct((dim, width + 4 * dim), BF),
        compiler_params=params(16),
        name="close",
    )(*parts, rest)


def join_kernel(factor, me_ref, a_ref, b_ref, c_ref, d_ref, out_ref):
    dim = a_ref.shape[0]
    width = out_ref.shape[2] - dim
    me = far(me_ref[0])
    four = [ref[...].astype(F32) for ref in (a_ref, b_ref, c_ref, d_ref)]
    rest = (four[0] + four[1] + four[2] + four[3])[:, width:] * factor
    for k in range(4):
        out_ref[me ^ k, :, :width] = four[k][:, :width].astype(BF)
    for a in range(4):
        out_ref[a, :, width:] = rest[:, dim * a : dim * (a + 1)].astype(BF)


def join(me, parts, factor):
    dim, wide = parts[0].shape
    vm = pl.BlockSpec(memory_space=pltpu.VMEM)

    def body(*refs):
        join_kernel(factor, *refs)

    return pl.pallas_call(
        body,
        in_specs=[pl.BlockSpec(memory_space=pltpu.SMEM)] + [vm] * 4,
        out_specs=vm,
        out_shape=jax.ShapeDtypeStruct((4, dim, wide - 3 * dim), BF),
        compiler_params=params(16),
        name="join",
    )(me, *parts)


def final_kernel(me_ref, a_ref, b_ref, c_ref, d_ref, in_ref, out_ref, all_ref):
    total = a_ref.shape[2]
    heads = 16
    me = me_ref[0]
    for k, ref in enumerate((a_ref, b_ref, c_ref, d_ref)):
        all_ref[k] = ref[...]
    blocks = [all_ref[near(me) ^ near(h), far(h)].astype(F32) for h in range(heads)]
    dim = total // 4
    for p in range(4):
        part = jnp.concatenate([b[:, dim * p : dim * (p + 1)] for b in blocks], axis=1).astype(BF)
        if p < 3:
            in_ref[:, heads * dim * p : heads * dim * (p + 1)] = part
        else:
            out_ref[...] = part


def final(me, parts):
    _, rows, total = parts[0].shape
    wide = 16 * (total // 4)
    vm = pl.BlockSpec(memory_space=pltpu.VMEM)
    return pl.pallas_call(
        final_kernel,
        in_specs=[pl.BlockSpec(memory_space=pltpu.SMEM)] + [vm] * 4,
        out_specs=[vm] * 2,
        out_shape=[
            jax.ShapeDtypeStruct((rows, 3 * wide), BF),
            jax.ShapeDtypeStruct((rows, wide), BF),
        ],
        scratch_shapes=[pltpu.VMEM((4,) + parts[0].shape, BF)],
        compiler_params=params(16),
        name="final",
    )(me, *parts)


def swap(part, bits):
    return lax.ppermute(part, "dp", [(i, i ^ bits) for i in range(16)])


def cross(part, bits):
    return lax.ppermute(part, ("dp", "vt"), [(16 * a + b, 16 * b + (a ^ bits)) for a in range(16) for b in range(16)])


def chunk(me, parts, factor):
    *sums, rest = fold(me, parts)
    return close([cross(sums[k], 2 * k) for k in range(4)], rest, factor)


def front(me, tok, cot, mod, q_gain, k_gain, w_qkv, w_out, nb):
    features = tok.shape[-1]
    head_dim = q_gain.shape[0]
    vt = lax.axis_index("vt").reshape(1)
    hb = enter(nb, tok, cot, mod)
    w, wo = weights(vt, w_qkv, w_out, head_dim)
    arrays, slots, w, wo = gather(hb, features + LANES, w, wo)
    return heads(me, vt, w, wo, q_gain, k_gain, arrays, slots)


def shards(tokens, cotangent, modulation, q_gain, k_gain, w_qkv, w_out, neighbours):
    rows, features = tokens.shape[-2:]
    factor = 1.0 / (lax.axis_size("dp") * lax.axis_size("vt"))
    me = lax.axis_index("dp").reshape(1)
    tok = tokens.reshape(rows, features)
    cot = cotangent.reshape(rows, features)
    mod = modulation.reshape(3, features)
    gp, *sent = front(me, tok, cot, mod, q_gain, k_gain, w_qkv, w_out, neighbours.reshape(2))
    parts = [sent[0]] + [swap(sent[k], near_bits(k)) for k in (1, 2, 3)]
    gp, *parts = lax.optimization_barrier((gp, *parts))
    gp_mine = lax.all_to_all(gp, "vt", 0, 0)
    mine = chunk(me, parts, factor)
    group = join(me, [mine] + [swap(mine, 2 * k) for k in (1, 2, 3)], factor)
    gp_mine, group = lax.optimization_barrier((gp_mine, group))
    grad_in, grad_out = final(me, [group] + [swap(group, near_bits(k)) for k in (1, 2, 3)])
    grad_tokens = leave(gp_mine, w_qkv, tok, cot, mod)
    return grad_tokens.reshape(tokens.shape), grad_in, grad_out


def solution(mesh):
    placed = (
        P("dp", "vt", None, None, None),
        P("dp", "vt", None, None, None),
        P("dp", "vt", None, None),
        P(),
        P(),
        P(),
        P(),
        P("dp", "vt", None),
    )
    return jax.shard_map(
        shards,
        mesh=mesh,
        in_specs=placed,
        out_specs=(P("dp", "vt", None, None, None), P("vt", None), P("vt", None)),
        check_vma=False,
    )
```

```python
import math

import jax
import jax.numpy as jnp
from jax import lax
from jax.experimental import pallas as pl
from jax.experimental.pallas import tpu as pltpu
from jax.sharding import PartitionSpec as P

BF = jnp.bfloat16
F32 = jnp.float32
EPS = 1e-06
NN = (((1,), (0,)), ((), ()))
NT = (((1,), (1,)), ((), ()))
MIB = 1024 * 1024
LANES = 128


def dot(a, b, dims=NN):
    return lax.dot_general(a, b, dims, preferred_element_type=F32)


def whole(shape):
    return pl.BlockSpec(shape, lambda *_: (0,) * len(shape))


def params(mib):
    return pltpu.CompilerParams(vmem_limit_bytes=mib * MIB)


def normalise(values):
    center = values - jnp.mean(values, axis=-1, keepdims=True)
    spread = jnp.mean(center * center, axis=-1, keepdims=True)
    inverse = lax.rsqrt(spread + EPS)
    return center * inverse, inverse


def line(mod_ref, i):
    return mod_ref[i : i + 1, :]


def enter_kernel(nb_ref, tok_ref, cot_ref, mod_ref, out_ref):
    rows, features = tok_ref.shape
    normed, _ = normalise(tok_ref[...].astype(F32))
    hidden = normed * (1.0 + line(mod_ref, 1)) + line(mod_ref, 0)
    out_ref[:, :features] = hidden.astype(BF)
    lane = lax.broadcasted_iota(jnp.int32, (rows, LANES), 1)
    marks = jnp.where(lane == 0, nb_ref[0].astype(F32), nb_ref[1].astype(F32))
    out_ref[:, features : features + LANES] = marks.astype(BF)
    out_ref[:, features + LANES :] = (line(mod_ref, 2) * cot_ref[...].astype(F32)).astype(BF)


def enter(nb, tok, cot, mod):
    rows, features = tok.shape
    vm = pl.BlockSpec(memory_space=pltpu.VMEM)
    return pl.pallas_call(
        enter_kernel,
        in_specs=[pl.BlockSpec(memory_space=pltpu.SMEM), vm, vm, vm],
        out_specs=vm,
        out_shape=jax.ShapeDtypeStruct((rows, 2 * features + LANES), BF),
        compiler_params=params(58),
        name="enter",
    )(nb, tok, cot, mod)


def weights_kernel(head_ref, w_hbm, wo_hbm, w_ref, wo_ref, win, wo_win, sem):
    features, wide = w_ref.shape
    dim = wo_ref.shape[0]
    head = head_ref[0]
    copies = []
    gaps = []
    for p in range(3):
        first = features * p + dim * head
        start = jnp.minimum(first // LANES * LANES, 3 * features - wide)
        gaps.append(first - start)
        window = w_hbm.at[:, pl.ds(pl.multiple_of(start, LANES), wide)]
        copies.append(pltpu.make_async_copy(window, win.at[p], sem.at[p]))
    first = dim * head
    start = first // 16 * 16
    window = wo_hbm.at[pl.ds(pl.multiple_of(start, 16), wo_win.shape[0])]
    copies.append(pltpu.make_async_copy(window, wo_win, sem.at[3]))
    for copy in copies:
        copy.start()
    row = lax.broadcasted_iota(jnp.int32, (wide, wide), 0)
    column = lax.broadcasted_iota(jnp.int32, (wide, wide), 1)
    total = jnp.zeros((features, wide), F32)
    for p in range(3):
        inside = (column >= dim * p) & (column < dim * (p + 1))
        pick = jnp.where(inside & (row == column - dim * p + gaps[p]), 1.0, 0.0).astype(BF)
        copies[p].wait()
        total = total + dot(win[p], pick)
    w_ref[...] = total.astype(BF)
    row = lax.broadcasted_iota(jnp.int32, (dim, wo_win.shape[0]), 0)
    column = lax.broadcasted_iota(jnp.int32, (dim, wo_win.shape[0]), 1)
    pick = jnp.where(column == row + (first - start), 1.0, 0.0).astype(BF)
    copies[3].wait()
    wo_ref[...] = dot(pick, wo_win[...]).astype(BF)


def weights(head, w_qkv, w_out, dim):
    features = w_out.shape[0]
    wide = 2 * LANES
    vm = pl.BlockSpec(memory_space=pltpu.VMEM)
    hbm = pl.BlockSpec(memory_space=pltpu.HBM)
    return pl.pallas_call(
        weights_kernel,
        in_specs=[pl.BlockSpec(memory_space=pltpu.SMEM), hbm, hbm],
        out_specs=[vm, vm],
        out_shape=[
            jax.ShapeDtypeStruct((features, wide), BF),
            jax.ShapeDtypeStruct((dim, features), BF),
        ],
        scratch_shapes=[
            pltpu.VMEM((3, features, wide), BF),
            pltpu.VMEM((dim + 8, features), BF),
            pltpu.SemaphoreType.DMA((4,)),
        ],
        compiler_params=params(52),
        name="weights",
    )(head, w_qkv, w_out)


def place(y, x, core):
    return (y * 4 + x) * 2 + core


def move(part, dy, dx, dc):
    pairs = [
        (place(y, x, c), place(y ^ dy, (x + dx) % 4, c ^ dc)) for y in range(2) for x in range(4) for c in range(2)
    ]
    return lax.ppermute(part, "vt", pairs)


def mix_kernel(a_ref, b_ref, c_ref, up_ref, down_ref, over_ref):
    half = down_ref.shape[1] // 2
    first = a_ref.shape[1] - half
    up_ref[:, :first] = a_ref[:, :first]
    up_ref[:, first:] = c_ref[:, :first]
    down_ref[:, :half] = b_ref[:, first:]
    down_ref[:, half:] = c_ref[:, first:]
    over_ref[:, :half] = a_ref[:, first:]
    over_ref[:, half:] = b_ref[:, :first]


def mix(a, b, c, first):
    rows, wide = a.shape
    half = wide - first
    return pl.pallas_call(
        mix_kernel,
        out_shape=[
            jax.ShapeDtypeStruct((rows, 2 * first), BF),
            jax.ShapeDtypeStruct((rows, 2 * half), BF),
            jax.ShapeDtypeStruct((rows, wide), BF),
        ],
        compiler_params=params(16),
        name="mix",
    )(a, b, c)


def gather(hb, first, w, wo):
    half = hb.shape[1] - first
    low = move(hb, 0, 1, 0)
    high = move(hb, 0, -1, 0)
    side = move(hb, 1, 0, 0)
    twin = move(hb, 0, 0, 1)
    low, high, side, w, wo = lax.optimization_barrier((low, high, side, w, wo))
    up, down, over = mix(low, high, side, first)
    up, down, over = move(up, 0, 1, 0), move(down, 0, -1, 0), move(over, 1, 0, 0)
    twins = [move(a, 0, 0, 1) for a in (low, high, side)]
    far_up = move(up[:, first:], 0, 1, 0)
    far_down = move(down[:, half:], 0, -1, 0)
    twins += [move(a, 0, 0, 1) for a in (up, down, over)]
    twins += [move(a, 0, 0, 1) for a in (far_up, far_down)]
    arrays = [hb, low, high, side, up, down, over, far_up, far_down, twin] + twins
    slots = []
    for dc in range(2):
        n = 9 * dc
        slots += [
            ((0, 0, dc), (n, 0), (n, first)),
            ((0, 3, dc), (n + 1, 0), (n + 1, first)),
            ((0, 1, dc), (n + 2, 0), (n + 2, first)),
            ((1, 0, dc), (n + 3, 0), (n + 3, first)),
            ((0, 2, dc), (n + 4, 0), (n + 5, 0)),
            ((1, 3, dc), (n + 4, first), (n + 6, 0)),
            ((1, 1, dc), (n + 6, half), (n + 5, half)),
            ((1, 2, dc), (n + 7, 0), (n + 8, 0)),
        ]
    return arrays, slots, w, wo


def near(i):
    return i % 2 + 2 * (i // 8)


def far(i):
    return (i // 2) % 4


def near_bits(k):
    return k % 2 + 8 * (k // 2)


def heads_kernel(slots, dim, features, cams, me_ref, vt_ref, w_ref, wo_ref, qg_ref, kg_ref, *refs):
    count = len({n for _, *pairs in slots for n, _ in pairs})
    arrays, refs = refs[:count], refs[count:]
    gp_hbm, *sends, sem, gp_ref, nb, at, qn, kn, rad, qh, kh, vh, gh, krow, vrow, gq, gk, gv, acc, acc_out, spread = refs
    tokens = arrays[0].shape[0]
    width = 3 * dim
    scale = 1.0 / math.sqrt(dim)
    empty = jnp.zeros((1, tokens - dim), F32)
    qgain, kgain = (
        jnp.broadcast_to(jnp.concatenate([ref[...], empty], axis=1), (tokens, tokens)).T[:dim] for ref in (qg_ref, kg_ref)
    )
    pad = jnp.zeros((tokens - dim, tokens), F32)
    vt = vt_ref[0]
    y, x, core = vt // 8, vt // 2 % 4, vt % 2
    cameras = [place((y + dy) % 2, (x + dx) % 4, (core + dc) % 2) for (dy, dx, dc), _, _ in slots]

    def hidden(s):
        n, lane = slots[s][1]
        return arrays[n][:, lane : lane + features]

    def branch(s):
        n, lane = slots[s][2]
        return arrays[n][:, lane : lane + features]

    for s, c in enumerate(cameras):
        n, lane = slots[s][1]
        marks = arrays[n][:16, lane + features : lane + features + LANES].astype(F32)
        nb[c, 0] = marks[0, 0].astype(jnp.int32)
        nb[c, 1] = marks[0, 1].astype(jnp.int32)
        turned = dot(hidden(s), w_ref[...]).T
        q, k, v = (turned[dim * i : dim * (i + 1)] for i in range(3))
        g = dot(wo_ref[...], branch(s), NT)
        rq = lax.rsqrt(jnp.mean(q * q, axis=0, keepdims=True) + EPS)
        rk = lax.rsqrt(jnp.mean(k * k, axis=0, keepdims=True) + EPS)
        q = q * rq
        k = k * rk
        qn[c] = q
        kn[c] = k
        rad[c, 0:1, :] = rq
        rad[c, 1:2, :] = rk
        q = q * qgain
        k = k * kgain
        qh[c] = jnp.concatenate([q, pad], axis=0).astype(BF)
        gh[c] = jnp.concatenate([g, pad], axis=0).astype(BF)
        kh[c] = k.astype(BF)
        vh[c] = v.astype(BF)
        krow[c] = jnp.concatenate([k, pad], axis=0).T.astype(BF)
        vrow[c] = jnp.concatenate([v, pad], axis=0).T.astype(BF)

    def camera(c, _):
        left = nb[c, 0]
        right = nb[c, 1]
        q = qh[c]
        g = gh[c]
        keys = jnp.concatenate([krow[left], krow[c], krow[right]], axis=0)
        values = jnp.concatenate([vrow[left], vrow[c], vrow[right]], axis=0)
        keys_t = jnp.concatenate([kh[left], kh[c], kh[right]], axis=1)
        values_t = jnp.concatenate([vh[left], vh[c], vh[right]], axis=1)
        e = jnp.exp(dot(keys, q) * scale)
        probs = e * (1.0 / jnp.sum(e, axis=0, keepdims=True))
        low = probs.astype(BF)
        gprobs = dot(values, g)
        centre = jnp.sum(probs * gprobs, axis=0, keepdims=True)
        gs = (probs * (gprobs - centre) * scale).astype(BF)
        at[c] = dot(values_t, low).astype(BF)
        gq[c] = dot(keys_t, gs)
        gk[c] = dot(q, gs, NT)[:dim]
        gv[c] = dot(g, low, NT)[:dim]
        return 0

    lax.fori_loop(0, cams, camera, 0, unroll=4)

    def back(grad, unit, radius, gain):
        shaped = grad * gain
        return (shaped - unit * jnp.mean(shaped * unit, axis=0, keepdims=True)) * radius

    def finish(c, _):
        left = nb[c, 0]
        right = nb[c, 1]
        grad_k = gk[c, :, tokens : 2 * tokens] + gk[left, :, 2 * tokens :] + gk[right, :, :tokens]
        grad_v = gv[c, :, tokens : 2 * tokens] + gv[left, :, 2 * tokens :] + gv[right, :, :tokens]
        grad_q = back(gq[c], qn[c], rad[c, 0:1, :], qgain)
        grad_k = back(grad_k, kn[c], rad[c, 1:2, :], kgain)
        gp_ref[c] = jnp.concatenate([grad_q, grad_k, grad_v], axis=0).astype(BF)
        return 0

    lax.fori_loop(0, cams, finish, 0, unroll=4)

    out = pltpu.make_async_copy(gp_ref, gp_hbm, sem)
    out.start()
    acc[width:, :] = jnp.zeros_like(acc[width:, :])
    for s in range(0, cams, 4):
        four = range(s, s + 4)
        grads = jnp.concatenate([gp_ref[cameras[i]] for i in four], axis=1)
        atts = jnp.concatenate([at[cameras[i]] for i in four], axis=1)
        one = dot(grads, jnp.concatenate([hidden(i) for i in four], axis=0))
        two = dot(atts, jnp.concatenate([branch(i) for i in four], axis=0))
        acc[:width, :] = one if s == 0 else acc[:width, :] + one
        acc_out[...] = two if s == 0 else acc_out[...] + two
    turned = acc[...].T
    for b in range(features // dim):
        spread[b, :, :width] = turned[dim * b : dim * (b + 1), :width].astype(BF)
        spread[b, :, width:] = acc_out[:, dim * b : dim * (b + 1)].astype(BF)
    me = me_ref[0]
    for k, ref in enumerate(sends):
        for a in range(4):
            ref[a] = spread[near_bits(near(me) ^ k) + 2 * a]
    out.wait()


def heads(me, vt, w, wo, q_gain, k_gain, arrays, slots):
    dim, features = wo.shape
    tokens = arrays[0].shape[0]
    cams = len(slots)
    vm = pl.BlockSpec(memory_space=pltpu.VMEM)
    sm = pl.BlockSpec(memory_space=pltpu.SMEM)

    def body(*refs):
        heads_kernel(slots, dim, features, cams, *refs)

    return pl.pallas_call(
        body,
        in_specs=[sm, sm] + [vm] * (4 + len(arrays)),
        out_specs=[pl.BlockSpec(memory_space=pltpu.HBM)] + [vm] * 4,
        out_shape=[jax.ShapeDtypeStruct((cams, 3 * dim, tokens), BF)]
        + [jax.ShapeDtypeStruct((4, dim, 4 * dim), BF)] * 4,
        scratch_shapes=[
            pltpu.SemaphoreType.DMA,
            pltpu.VMEM((cams, 3 * dim, tokens), BF),
            pltpu.SMEM((cams, 2), jnp.int32),
            pltpu.VMEM((cams, dim, tokens), BF),
            pltpu.VMEM((cams, dim, tokens), F32),
            pltpu.VMEM((cams, dim, tokens), F32),
            pltpu.VMEM((cams, 8, tokens), F32),
            pltpu.VMEM((cams, tokens, tokens), BF),
            pltpu.VMEM((cams, dim, tokens), BF),
            pltpu.VMEM((cams, dim, tokens), BF),
            pltpu.VMEM((cams, tokens, tokens), BF),
            pltpu.VMEM((cams, tokens, tokens), BF),
            pltpu.VMEM((cams, tokens, tokens), BF),
            pltpu.VMEM((cams, dim, tokens), F32),
            pltpu.VMEM((cams, dim, 3 * tokens), F32),
            pltpu.VMEM((cams, dim, 3 * tokens), F32),
            pltpu.VMEM((2 * LANES, features), F32),
            pltpu.VMEM((dim, features), F32),
            pltpu.VMEM((features // dim, dim, 4 * dim), BF),
        ],
        compiler_params=params(36),
        name="heads",
    )(me, vt, w, wo, q_gain.reshape(1, dim), k_gain.reshape(1, dim), *arrays)


def leave_kernel(x_ref, w_ref, tok_ref, cot_ref, mod_ref, out_ref, scr, acc):
    part = pl.program_id(0)
    heads, width, _ = x_ref.shape
    dim = width // 3

    @pl.when(part == 0)
    def _():
        for h in range(heads):
            x = x_ref[h].astype(F32)
            for p in range(3):
                scr[p, dim * h : dim * (h + 1), :] = x[dim * p : dim * (p + 1)]
        acc[...] = jnp.zeros_like(acc)

    acc[...] += dot(w_ref[...], scr[part].astype(BF))

    @pl.when(part == 2)
    def _():
        scaled = acc[...].T * (1.0 + line(mod_ref, 1))
        normed, inverse = normalise(tok_ref[...].astype(F32))
        mean = jnp.mean(scaled, axis=-1, keepdims=True)
        along = jnp.mean(scaled * normed, axis=-1, keepdims=True)
        grad = inverse * (scaled - mean - normed * along)
        out_ref[...] = (cot_ref[...].astype(F32) + grad).astype(BF)


def leave(x, w_qkv, tok, cot, mod):
    rows, features = tok.shape
    return pl.pallas_call(
        leave_kernel,
        grid=(3,),
        in_specs=[
            whole(x.shape),
            pl.BlockSpec((features, features), lambda p: (0, p)),
            whole(tok.shape),
            whole(cot.shape),
            whole(mod.shape),
        ],
        out_specs=whole(tok.shape),
        out_shape=jax.ShapeDtypeStruct(tok.shape, BF),
        scratch_shapes=[
            pltpu.VMEM((3, features, rows), F32),
            pltpu.VMEM((features, rows), F32),
        ],
        compiler_params=params(58),
        name="leave",
    )(x, w_qkv, tok, cot, mod)


def fold_kernel(me_ref, a_ref, b_ref, c_ref, d_ref, *outs):
    dim, width = outs[0].shape
    me = far(me_ref[0])
    for k in range(4):
        a = me ^ k
        total = a_ref[a].astype(F32) + b_ref[a].astype(F32) + c_ref[a].astype(F32) + d_ref[a].astype(F32)
        outs[k][...] = total[:, :width].astype(BF)
    sums = []
    for a in range(4):
        total = a_ref[a].astype(F32) + b_ref[a].astype(F32) + c_ref[a].astype(F32) + d_ref[a].astype(F32)
        sums.append(total[:, width:])
    outs[4][...] = jnp.concatenate(sums, axis=1).astype(BF)


def fold(me, parts):
    _, dim, total = parts[0].shape
    vm = pl.BlockSpec(memory_space=pltpu.VMEM)
    shapes = [jax.ShapeDtypeStruct((dim, total - dim), BF)] * 4 + [jax.ShapeDtypeStruct((dim, 4 * dim), BF)]
    return pl.pallas_call(
        fold_kernel,
        in_specs=[pl.BlockSpec(memory_space=pltpu.SMEM)] + [vm] * 4,
        out_specs=[vm] * 5,
        out_shape=shapes,
        compiler_params=params(16),
        name="fold",
    )(me, *parts)


def close_kernel(factor, a_ref, b_ref, c_ref, d_ref, rest_ref, out_ref):
    width = a_ref.shape[1]
    total = a_ref[...].astype(F32) + b_ref[...].astype(F32) + c_ref[...].astype(F32) + d_ref[...].astype(F32)
    both = jnp.concatenate([total * factor, rest_ref[...].astype(F32)], axis=1)
    out_ref[...] = both.astype(BF)


def close(parts, rest, factor):
    dim, width = parts[0].shape
    vm = pl.BlockSpec(memory_space=pltpu.VMEM)

    def body(*refs):
        close_kernel(factor, *refs)

    return pl.pallas_call(
        body,
        in_specs=[vm] * 5,
        out_specs=vm,
        out_shape=jax.ShapeDtypeStruct((dim, width + 4 * dim), BF),
        compiler_params=params(16),
        name="close",
    )(*parts, rest)


def join_kernel(factor, me_ref, a_ref, b_ref, c_ref, d_ref, out_ref):
    dim = a_ref.shape[0]
    width = out_ref.shape[2] - dim
    me = far(me_ref[0])
    four = [ref[...].astype(F32) for ref in (a_ref, b_ref, c_ref, d_ref)]
    rest = (four[0] + four[1] + four[2] + four[3])[:, width:] * factor
    for k in range(4):
        out_ref[me ^ k, :, :width] = four[k][:, :width].astype(BF)
    for a in range(4):
        out_ref[a, :, width:] = rest[:, dim * a : dim * (a + 1)].astype(BF)


def join(me, parts, factor):
    dim, wide = parts[0].shape
    vm = pl.BlockSpec(memory_space=pltpu.VMEM)

    def body(*refs):
        join_kernel(factor, *refs)

    return pl.pallas_call(
        body,
        in_specs=[pl.BlockSpec(memory_space=pltpu.SMEM)] + [vm] * 4,
        out_specs=vm,
        out_shape=jax.ShapeDtypeStruct((4, dim, wide - 3 * dim), BF),
        compiler_params=params(16),
        name="join",
    )(me, *parts)


def final_kernel(me_ref, a_ref, b_ref, c_ref, d_ref, in_ref, out_ref, all_ref):
    total = a_ref.shape[2]
    heads = 16
    me = me_ref[0]
    for k, ref in enumerate((a_ref, b_ref, c_ref, d_ref)):
        all_ref[k] = ref[...]
    blocks = [all_ref[near(me) ^ near(h), far(h)].astype(F32) for h in range(heads)]
    dim = total // 4
    for p in range(4):
        part = jnp.concatenate([b[:, dim * p : dim * (p + 1)] for b in blocks], axis=1).astype(BF)
        if p < 3:
            in_ref[:, heads * dim * p : heads * dim * (p + 1)] = part
        else:
            out_ref[...] = part


def final(me, parts):
    _, rows, total = parts[0].shape
    wide = 16 * (total // 4)
    vm = pl.BlockSpec(memory_space=pltpu.VMEM)
    return pl.pallas_call(
        final_kernel,
        in_specs=[pl.BlockSpec(memory_space=pltpu.SMEM)] + [vm] * 4,
        out_specs=[vm] * 2,
        out_shape=[
            jax.ShapeDtypeStruct((rows, 3 * wide), BF),
            jax.ShapeDtypeStruct((rows, wide), BF),
        ],
        scratch_shapes=[pltpu.VMEM((4,) + parts[0].shape, BF)],
        compiler_params=params(16),
        name="final",
    )(me, *parts)


def swap(part, bits):
    return lax.ppermute(part, "dp", [(i, i ^ bits) for i in range(16)])


def cross(part, bits):
    return lax.ppermute(part, ("dp", "vt"), [(16 * a + b, 16 * b + (a ^ bits)) for a in range(16) for b in range(16)])


def front(me, tok, cot, mod, q_gain, k_gain, w_qkv, w_out, nb):
    features = tok.shape[-1]
    head_dim = q_gain.shape[0]
    vt = lax.axis_index("vt").reshape(1)
    hb = enter(nb, tok, cot, mod)
    w, wo = weights(vt, w_qkv, w_out, head_dim)
    arrays, slots, w, wo = gather(hb, features + LANES, w, wo)
    return heads(me, vt, w, wo, q_gain, k_gain, arrays, slots)


def shards(tokens, cotangent, modulation, q_gain, k_gain, w_qkv, w_out, neighbours):
    rows, features = tokens.shape[-2:]
    factor = 1.0 / (lax.axis_size("dp") * lax.axis_size("vt"))
    me = lax.axis_index("dp").reshape(1)
    tok = tokens.reshape(rows, features)
    cot = cotangent.reshape(rows, features)
    mod = modulation.reshape(3, features)
    gp, *sent = front(me, tok, cot, mod, q_gain, k_gain, w_qkv, w_out, neighbours.reshape(2))
    parts = [sent[0]] + [swap(sent[k], near_bits(k)) for k in (1, 2, 3)]
    *sums, rest = fold(me, parts)
    sums = [cross(sums[k], 2 * k) for k in range(4)]
    gp, sums[0] = lax.optimization_barrier((gp, sums[0]))
    gp_mine = lax.all_to_all(gp, "vt", 0, 0)
    mine = close(sums, rest, factor)
    group = join(me, [mine] + [swap(mine, 2 * k) for k in (1, 2, 3)], factor)
    gp_mine, group = lax.optimization_barrier((gp_mine, group))
    grad_in, grad_out = final(me, [group] + [swap(group, near_bits(k)) for k in (1, 2, 3)])
    grad_tokens = leave(gp_mine, w_qkv, tok, cot, mod)
    return grad_tokens.reshape(tokens.shape), grad_in, grad_out


def solution(mesh):
    placed = (
        P("dp", "vt", None, None, None),
        P("dp", "vt", None, None, None),
        P("dp", "vt", None, None),
        P(),
        P(),
        P(),
        P(),
        P("dp", "vt", None),
    )
    return jax.shard_map(
        shards,
        mesh=mesh,
        in_specs=placed,
        out_specs=(P("dp", "vt", None, None, None), P("vt", None), P("vt", None)),
        check_vma=False,
    )
```

```python
import math

import jax
import jax.numpy as jnp
from jax import lax
from jax.experimental import pallas as pl
from jax.experimental.pallas import tpu as pltpu
from jax.sharding import PartitionSpec as P

BF = jnp.bfloat16
F32 = jnp.float32
EPS = 1e-06
NN = (((1,), (0,)), ((), ()))
NT = (((1,), (1,)), ((), ()))
MIB = 1024 * 1024
LANES = 128


def dot(a, b, dims=NN):
    return lax.dot_general(a, b, dims, preferred_element_type=F32)


def whole(shape):
    return pl.BlockSpec(shape, lambda *_: (0,) * len(shape))


def params(mib):
    return pltpu.CompilerParams(vmem_limit_bytes=mib * MIB)


def normalise(values):
    center = values - jnp.mean(values, axis=-1, keepdims=True)
    spread = jnp.mean(center * center, axis=-1, keepdims=True)
    inverse = lax.rsqrt(spread + EPS)
    return center * inverse, inverse


def line(mod_ref, i):
    return mod_ref[i : i + 1, :]


def enter_kernel(nb_ref, tok_ref, cot_ref, mod_ref, out_ref):
    rows, features = tok_ref.shape
    normed, _ = normalise(tok_ref[...].astype(F32))
    hidden = normed * (1.0 + line(mod_ref, 1)) + line(mod_ref, 0)
    out_ref[:, :features] = hidden.astype(BF)
    lane = lax.broadcasted_iota(jnp.int32, (rows, LANES), 1)
    marks = jnp.where(lane == 0, nb_ref[0].astype(F32), nb_ref[1].astype(F32))
    out_ref[:, features : features + LANES] = marks.astype(BF)
    out_ref[:, features + LANES :] = (line(mod_ref, 2) * cot_ref[...].astype(F32)).astype(BF)


def enter(nb, tok, cot, mod):
    rows, features = tok.shape
    vm = pl.BlockSpec(memory_space=pltpu.VMEM)
    return pl.pallas_call(
        enter_kernel,
        in_specs=[pl.BlockSpec(memory_space=pltpu.SMEM), vm, vm, vm],
        out_specs=vm,
        out_shape=jax.ShapeDtypeStruct((rows, 2 * features + LANES), BF),
        compiler_params=params(58),
        name="enter",
    )(nb, tok, cot, mod)


def weights_kernel(head_ref, w_hbm, wo_hbm, w_ref, wo_ref, win, wo_win, sem):
    features, wide = w_ref.shape
    dim = wo_win.shape[0] - 8
    head = head_ref[0]
    copies = []
    gaps = []
    for p in range(3):
        first = features * p + dim * head
        start = jnp.minimum(first // LANES * LANES, 3 * features - wide)
        gaps.append(first - start)
        window = w_hbm.at[:, pl.ds(pl.multiple_of(start, LANES), wide)]
        copies.append(pltpu.make_async_copy(window, win.at[p], sem.at[p]))
    first = dim * head
    start = first // 16 * 16
    window = wo_hbm.at[pl.ds(pl.multiple_of(start, 16), wo_win.shape[0])]
    copies.append(pltpu.make_async_copy(window, wo_win, sem.at[3]))
    for copy in copies:
        copy.start()
    row = lax.broadcasted_iota(jnp.int32, (wide, wide), 0)
    column = lax.broadcasted_iota(jnp.int32, (wide, wide), 1)
    total = jnp.zeros((features, wide), F32)
    for p in range(3):
        inside = (column >= dim * p) & (column < dim * (p + 1))
        pick = jnp.where(inside & (row == column - dim * p + gaps[p]), 1.0, 0.0).astype(BF)
        copies[p].wait()
        total = total + dot(win[p], pick)
    w_ref[...] = total.astype(BF)
    row = lax.broadcasted_iota(jnp.int32, (LANES, dim + 8), 0)
    column = lax.broadcasted_iota(jnp.int32, (LANES, dim + 8), 1)
    pick = jnp.where((row < dim) & (column == row + (first - start)), 1.0, 0.0).astype(BF)
    copies[3].wait()
    wo_ref[...] = dot(pick, wo_win[...]).T.astype(BF)


def weights(head, w_qkv, w_out, dim):
    features = w_out.shape[0]
    wide = 2 * LANES
    vm = pl.BlockSpec(memory_space=pltpu.VMEM)
    hbm = pl.BlockSpec(memory_space=pltpu.HBM)
    return pl.pallas_call(
        weights_kernel,
        in_specs=[pl.BlockSpec(memory_space=pltpu.SMEM), hbm, hbm],
        out_specs=[vm, vm],
        out_shape=[
            jax.ShapeDtypeStruct((features, wide), BF),
            jax.ShapeDtypeStruct((features, LANES), BF),
        ],
        scratch_shapes=[
            pltpu.VMEM((3, features, wide), BF),
            pltpu.VMEM((dim + 8, features), BF),
            pltpu.SemaphoreType.DMA((4,)),
        ],
        compiler_params=params(52),
        name="weights",
    )(head, w_qkv, w_out)


def place(y, x, core):
    return (y * 4 + x) * 2 + core


def move(part, dy, dx, dc):
    pairs = [
        (place(y, x, c), place(y ^ dy, (x + dx) % 4, c ^ dc)) for y in range(2) for x in range(4) for c in range(2)
    ]
    return lax.ppermute(part, "vt", pairs)


def mix_kernel(a_ref, b_ref, c_ref, up_ref, down_ref, over_ref):
    half = down_ref.shape[1] // 2
    first = a_ref.shape[1] - half
    up_ref[:, :first] = a_ref[:, :first]
    up_ref[:, first:] = c_ref[:, :first]
    down_ref[:, :half] = b_ref[:, first:]
    down_ref[:, half:] = c_ref[:, first:]
    over_ref[:, :half] = a_ref[:, first:]
    over_ref[:, half:] = b_ref[:, :first]


def mix(a, b, c, first):
    rows, wide = a.shape
    half = wide - first
    return pl.pallas_call(
        mix_kernel,
        out_shape=[
            jax.ShapeDtypeStruct((rows, 2 * first), BF),
            jax.ShapeDtypeStruct((rows, 2 * half), BF),
            jax.ShapeDtypeStruct((rows, wide), BF),
        ],
        compiler_params=params(16),
        name="mix",
    )(a, b, c)


def gather(hb, first, w, wo):
    half = hb.shape[1] - first
    low = move(hb, 0, 1, 0)
    high = move(hb, 0, -1, 0)
    side = move(hb, 1, 0, 0)
    twin = move(hb, 0, 0, 1)
    low, high, side, w, wo = lax.optimization_barrier((low, high, side, w, wo))
    up, down, over = mix(low, high, side, first)
    up, down, over = move(up, 0, 1, 0), move(down, 0, -1, 0), move(over, 1, 0, 0)
    twins = [move(a, 0, 0, 1) for a in (low, high, side)]
    far_up = move(up[:, first:], 0, 1, 0)
    far_down = move(down[:, half:], 0, -1, 0)
    twins += [move(a, 0, 0, 1) for a in (up, down, over)]
    twins += [move(a, 0, 0, 1) for a in (far_up, far_down)]
    arrays = [hb, low, high, side, up, down, over, far_up, far_down, twin] + twins
    slots = []
    for dc in range(2):
        n = 9 * dc
        slots += [
            ((0, 0, dc), (n, 0), (n, first)),
            ((0, 3, dc), (n + 1, 0), (n + 1, first)),
            ((0, 1, dc), (n + 2, 0), (n + 2, first)),
            ((1, 0, dc), (n + 3, 0), (n + 3, first)),
            ((0, 2, dc), (n + 4, 0), (n + 5, 0)),
            ((1, 3, dc), (n + 4, first), (n + 6, 0)),
            ((1, 1, dc), (n + 6, half), (n + 5, half)),
            ((1, 2, dc), (n + 7, 0), (n + 8, 0)),
        ]
    return arrays, slots, w, wo


def near(i):
    return i % 2 + 2 * (i // 8)


def far(i):
    return (i // 2) % 4


def near_bits(k):
    return k % 2 + 8 * (k // 2)


def heads_kernel(slots, dim, features, cams, me_ref, vt_ref, w_ref, wo_ref, qg_ref, kg_ref, *refs):
    count = len({n for _, *pairs in slots for n, _ in pairs})
    arrays, refs = refs[:count], refs[count:]
    gp_hbm, *sends, sem, gp_ref, nb, at, qn, kn, rad, qh, kh, vh, gh, krow, vrow, gq, gk, gv, acc, acc_out, spread = refs
    tokens = arrays[0].shape[0]
    width = 3 * dim
    scale = 1.0 / math.sqrt(dim)
    empty = jnp.zeros((1, tokens - dim), F32)
    qgain, kgain = (
        jnp.broadcast_to(jnp.concatenate([ref[...], empty], axis=1), (tokens, tokens)).T[:dim] for ref in (qg_ref, kg_ref)
    )
    pad = jnp.zeros((tokens - dim, tokens), F32)
    vt = vt_ref[0]
    y, x, core = vt // 8, vt // 2 % 4, vt % 2
    cameras = [place((y + dy) % 2, (x + dx) % 4, (core + dc) % 2) for (dy, dx, dc), _, _ in slots]

    def hidden(s):
        n, lane = slots[s][1]
        return arrays[n][:, lane : lane + features]

    def branch(s):
        n, lane = slots[s][2]
        return arrays[n][:, lane : lane + features]

    for s, c in enumerate(cameras):
        if s % 4 == 0:
            project = dot(jnp.concatenate([hidden(i) for i in range(s, s + 4)], axis=0), w_ref[...])
            back_out = dot(jnp.concatenate([branch(i) for i in range(s, s + 4)], axis=0), wo_ref[...])
        rows = slice(tokens * (s % 4), tokens * (s % 4 + 1))
        n, lane = slots[s][1]
        marks = arrays[n][:16, lane + features : lane + features + LANES].astype(F32)
        nb[c, 0] = marks[0, 0].astype(jnp.int32)
        nb[c, 1] = marks[0, 1].astype(jnp.int32)
        turned = project[rows].T
        q, k, v = (turned[dim * i : dim * (i + 1)] for i in range(3))
        rq = lax.rsqrt(jnp.mean(q * q, axis=0, keepdims=True) + EPS)
        rk = lax.rsqrt(jnp.mean(k * k, axis=0, keepdims=True) + EPS)
        q = q * rq
        k = k * rk
        qn[c] = q
        kn[c] = k
        rad[c, 0:1, :] = rq
        rad[c, 1:2, :] = rk
        q = q * qgain
        k = k * kgain
        qh[c] = jnp.concatenate([q, pad], axis=0).astype(BF)
        gh[c] = back_out[rows].T.astype(BF)
        kh[c] = k.astype(BF)
        vh[c] = v.astype(BF)
        krow[c] = jnp.concatenate([k, pad], axis=0).T.astype(BF)
        vrow[c] = jnp.concatenate([v, pad], axis=0).T.astype(BF)

    def camera(c, _):
        left = nb[c, 0]
        right = nb[c, 1]
        q = qh[c]
        g = gh[c]
        keys = jnp.concatenate([krow[left], krow[c], krow[right]], axis=0)
        values = jnp.concatenate([vrow[left], vrow[c], vrow[right]], axis=0)
        keys_t = jnp.concatenate([kh[left], kh[c], kh[right]], axis=1)
        values_t = jnp.concatenate([vh[left], vh[c], vh[right]], axis=1)
        e = jnp.exp(dot(keys, q) * scale)
        probs = e * (1.0 / jnp.sum(e, axis=0, keepdims=True))
        low = probs.astype(BF)
        gprobs = dot(values, g)
        centre = jnp.sum(probs * gprobs, axis=0, keepdims=True)
        gs = (probs * (gprobs - centre) * scale).astype(BF)
        at[c] = dot(values_t, low).astype(BF)
        gq[c] = dot(keys_t, gs)
        gk[c] = dot(q, gs, NT)[:dim]
        gv[c] = dot(g, low, NT)[:dim]
        return 0

    lax.fori_loop(0, cams, camera, 0, unroll=4)

    def back(grad, unit, radius, gain):
        shaped = grad * gain
        return (shaped - unit * jnp.mean(shaped * unit, axis=0, keepdims=True)) * radius

    def finish(c, _):
        left = nb[c, 0]
        right = nb[c, 1]
        grad_k = gk[c, :, tokens : 2 * tokens] + gk[left, :, 2 * tokens :] + gk[right, :, :tokens]
        grad_v = gv[c, :, tokens : 2 * tokens] + gv[left, :, 2 * tokens :] + gv[right, :, :tokens]
        grad_q = back(gq[c], qn[c], rad[c, 0:1, :], qgain)
        grad_k = back(grad_k, kn[c], rad[c, 1:2, :], kgain)
        gp_ref[c] = jnp.concatenate([grad_q, grad_k, grad_v], axis=0).astype(BF)
        return 0

    lax.fori_loop(0, cams, finish, 0, unroll=4)

    out = pltpu.make_async_copy(gp_ref, gp_hbm, sem)
    out.start()
    acc[width:, :] = jnp.zeros_like(acc[width:, :])
    for s in range(0, cams, 4):
        four = range(s, s + 4)
        grads = jnp.concatenate([gp_ref[cameras[i]] for i in four], axis=1)
        atts = jnp.concatenate([at[cameras[i]] for i in four], axis=1)
        one = dot(grads, jnp.concatenate([hidden(i) for i in four], axis=0))
        two = dot(atts, jnp.concatenate([branch(i) for i in four], axis=0))
        acc[:width, :] = one if s == 0 else acc[:width, :] + one
        acc_out[...] = two if s == 0 else acc_out[...] + two
    turned = acc[...].T
    for b in range(features // dim):
        spread[b, :, :width] = turned[dim * b : dim * (b + 1), :width].astype(BF)
        spread[b, :, width:] = acc_out[:, dim * b : dim * (b + 1)].astype(BF)
    me = me_ref[0]
    for k, ref in enumerate(sends):
        for a in range(4):
            ref[a] = spread[near_bits(near(me) ^ k) + 2 * a]
    out.wait()


def heads(me, vt, w, wo, q_gain, k_gain, arrays, slots):
    dim = q_gain.shape[0]
    features = wo.shape[0]
    tokens = arrays[0].shape[0]
    cams = len(slots)
    vm = pl.BlockSpec(memory_space=pltpu.VMEM)
    sm = pl.BlockSpec(memory_space=pltpu.SMEM)

    def body(*refs):
        heads_kernel(slots, dim, features, cams, *refs)

    return pl.pallas_call(
        body,
        in_specs=[sm, sm] + [vm] * (4 + len(arrays)),
        out_specs=[pl.BlockSpec(memory_space=pltpu.HBM)] + [vm] * 4,
        out_shape=[jax.ShapeDtypeStruct((cams, 3 * dim, tokens), BF)]
        + [jax.ShapeDtypeStruct((4, dim, 4 * dim), BF)] * 4,
        scratch_shapes=[
            pltpu.SemaphoreType.DMA,
            pltpu.VMEM((cams, 3 * dim, tokens), BF),
            pltpu.SMEM((cams, 2), jnp.int32),
            pltpu.VMEM((cams, dim, tokens), BF),
            pltpu.VMEM((cams, dim, tokens), F32),
            pltpu.VMEM((cams, dim, tokens), F32),
            pltpu.VMEM((cams, 8, tokens), F32),
            pltpu.VMEM((cams, tokens, tokens), BF),
            pltpu.VMEM((cams, dim, tokens), BF),
            pltpu.VMEM((cams, dim, tokens), BF),
            pltpu.VMEM((cams, tokens, tokens), BF),
            pltpu.VMEM((cams, tokens, tokens), BF),
            pltpu.VMEM((cams, tokens, tokens), BF),
            pltpu.VMEM((cams, dim, tokens), F32),
            pltpu.VMEM((cams, dim, 3 * tokens), F32),
            pltpu.VMEM((cams, dim, 3 * tokens), F32),
            pltpu.VMEM((2 * LANES, features), F32),
            pltpu.VMEM((dim, features), F32),
            pltpu.VMEM((features // dim, dim, 4 * dim), BF),
        ],
        compiler_params=params(36),
        name="heads",
    )(me, vt, w, wo, q_gain.reshape(1, dim), k_gain.reshape(1, dim), *arrays)


def leave_kernel(x_ref, w_ref, tok_ref, cot_ref, mod_ref, out_ref, scr, acc):
    part = pl.program_id(0)
    heads, width, _ = x_ref.shape
    dim = width // 3

    @pl.when(part == 0)
    def _():
        for h in range(heads):
            x = x_ref[h].astype(F32)
            for p in range(3):
                scr[p, dim * h : dim * (h + 1), :] = x[dim * p : dim * (p + 1)]
        acc[...] = jnp.zeros_like(acc)

    acc[...] += dot(w_ref[...], scr[part].astype(BF))

    @pl.when(part == 2)
    def _():
        scaled = acc[...].T * (1.0 + line(mod_ref, 1))
        normed, inverse = normalise(tok_ref[...].astype(F32))
        mean = jnp.mean(scaled, axis=-1, keepdims=True)
        along = jnp.mean(scaled * normed, axis=-1, keepdims=True)
        grad = inverse * (scaled - mean - normed * along)
        out_ref[...] = (cot_ref[...].astype(F32) + grad).astype(BF)


def leave(x, w_qkv, tok, cot, mod):
    rows, features = tok.shape
    return pl.pallas_call(
        leave_kernel,
        grid=(3,),
        in_specs=[
            whole(x.shape),
            pl.BlockSpec((features, features), lambda p: (0, p)),
            whole(tok.shape),
            whole(cot.shape),
            whole(mod.shape),
        ],
        out_specs=whole(tok.shape),
        out_shape=jax.ShapeDtypeStruct(tok.shape, BF),
        scratch_shapes=[
            pltpu.VMEM((3, features, rows), F32),
            pltpu.VMEM((features, rows), F32),
        ],
        compiler_params=params(58),
        name="leave",
    )(x, w_qkv, tok, cot, mod)


def fold_kernel(me_ref, a_ref, b_ref, c_ref, d_ref, *outs):
    dim, width = outs[0].shape
    me = far(me_ref[0])
    for k in range(4):
        a = me ^ k
        total = a_ref[a].astype(F32) + b_ref[a].astype(F32) + c_ref[a].astype(F32) + d_ref[a].astype(F32)
        outs[k][...] = total[:, :width].astype(BF)
    sums = []
    for a in range(4):
        total = a_ref[a].astype(F32) + b_ref[a].astype(F32) + c_ref[a].astype(F32) + d_ref[a].astype(F32)
        sums.append(total[:, width:])
    outs[4][...] = jnp.concatenate(sums, axis=1).astype(BF)


def fold(me, parts):
    _, dim, total = parts[0].shape
    vm = pl.BlockSpec(memory_space=pltpu.VMEM)
    shapes = [jax.ShapeDtypeStruct((dim, total - dim), BF)] * 4 + [jax.ShapeDtypeStruct((dim, 4 * dim), BF)]
    return pl.pallas_call(
        fold_kernel,
        in_specs=[pl.BlockSpec(memory_space=pltpu.SMEM)] + [vm] * 4,
        out_specs=[vm] * 5,
        out_shape=shapes,
        compiler_params=params(16),
        name="fold",
    )(me, *parts)


def close_kernel(factor, a_ref, b_ref, c_ref, d_ref, rest_ref, out_ref):
    width = a_ref.shape[1]
    total = a_ref[...].astype(F32) + b_ref[...].astype(F32) + c_ref[...].astype(F32) + d_ref[...].astype(F32)
    both = jnp.concatenate([total * factor, rest_ref[...].astype(F32)], axis=1)
    out_ref[...] = both.astype(BF)


def close(parts, rest, factor):
    dim, width = parts[0].shape
    vm = pl.BlockSpec(memory_space=pltpu.VMEM)

    def body(*refs):
        close_kernel(factor, *refs)

    return pl.pallas_call(
        body,
        in_specs=[vm] * 5,
        out_specs=vm,
        out_shape=jax.ShapeDtypeStruct((dim, width + 4 * dim), BF),
        compiler_params=params(16),
        name="close",
    )(*parts, rest)


def join_kernel(factor, me_ref, a_ref, b_ref, c_ref, d_ref, out_ref):
    dim = a_ref.shape[0]
    width = out_ref.shape[2] - dim
    me = far(me_ref[0])
    four = [ref[...].astype(F32) for ref in (a_ref, b_ref, c_ref, d_ref)]
    rest = (four[0] + four[1] + four[2] + four[3])[:, width:] * factor
    for k in range(4):
        out_ref[me ^ k, :, :width] = four[k][:, :width].astype(BF)
    for a in range(4):
        out_ref[a, :, width:] = rest[:, dim * a : dim * (a + 1)].astype(BF)


def join(me, parts, factor):
    dim, wide = parts[0].shape
    vm = pl.BlockSpec(memory_space=pltpu.VMEM)

    def body(*refs):
        join_kernel(factor, *refs)

    return pl.pallas_call(
        body,
        in_specs=[pl.BlockSpec(memory_space=pltpu.SMEM)] + [vm] * 4,
        out_specs=vm,
        out_shape=jax.ShapeDtypeStruct((4, dim, wide - 3 * dim), BF),
        compiler_params=params(16),
        name="join",
    )(me, *parts)


def final_kernel(me_ref, a_ref, b_ref, c_ref, d_ref, in_ref, out_ref, all_ref):
    total = a_ref.shape[2]
    heads = 16
    me = me_ref[0]
    for k, ref in enumerate((a_ref, b_ref, c_ref, d_ref)):
        all_ref[k] = ref[...]
    blocks = [all_ref[near(me) ^ near(h), far(h)].astype(F32) for h in range(heads)]
    dim = total // 4
    for p in range(4):
        part = jnp.concatenate([b[:, dim * p : dim * (p + 1)] for b in blocks], axis=1).astype(BF)
        if p < 3:
            in_ref[:, heads * dim * p : heads * dim * (p + 1)] = part
        else:
            out_ref[...] = part


def final(me, parts):
    _, rows, total = parts[0].shape
    wide = 16 * (total // 4)
    vm = pl.BlockSpec(memory_space=pltpu.VMEM)
    return pl.pallas_call(
        final_kernel,
        in_specs=[pl.BlockSpec(memory_space=pltpu.SMEM)] + [vm] * 4,
        out_specs=[vm] * 2,
        out_shape=[
            jax.ShapeDtypeStruct((rows, 3 * wide), BF),
            jax.ShapeDtypeStruct((rows, wide), BF),
        ],
        scratch_shapes=[pltpu.VMEM((4,) + parts[0].shape, BF)],
        compiler_params=params(16),
        name="final",
    )(me, *parts)


def swap(part, bits):
    return lax.ppermute(part, "dp", [(i, i ^ bits) for i in range(16)])


def cross(part, bits):
    return lax.ppermute(part, ("dp", "vt"), [(16 * a + b, 16 * b + (a ^ bits)) for a in range(16) for b in range(16)])


def front(me, vt, tok, cot, mod, q_gain, k_gain, w_qkv, w_out, nb):
    features = tok.shape[-1]
    hb = enter(nb, tok, cot, mod)
    w, wo = weights(vt, w_qkv, w_out, q_gain.shape[0])
    arrays, slots, w, wo = gather(hb, features + LANES, w, wo)
    return heads(me, vt, w, wo, q_gain, k_gain, arrays, slots)


def shards(tokens, cotangent, modulation, q_gain, k_gain, w_qkv, w_out, neighbours):
    rows, features = tokens.shape[-2:]
    factor = 1.0 / (lax.axis_size("dp") * lax.axis_size("vt"))
    me = lax.axis_index("dp").reshape(1)
    vt = lax.axis_index("vt").reshape(1)
    tok = tokens.reshape(rows, features)
    cot = cotangent.reshape(rows, features)
    mod = modulation.reshape(3, features)
    me, vt, tok = lax.optimization_barrier((me, vt, tok))
    gp, *sent = front(me, vt, tok, cot, mod, q_gain, k_gain, w_qkv, w_out, neighbours.reshape(2))
    parts = [sent[0]] + [swap(sent[k], near_bits(k)) for k in (1, 2, 3)]
    gp, *parts = lax.optimization_barrier((gp, *parts))
    gp_mine = lax.all_to_all(gp, "vt", 0, 0)
    *sums, rest = fold(me, parts)
    mine = close([cross(sums[k], 2 * k) for k in range(4)], rest, factor)
    group = join(me, [mine] + [swap(mine, 2 * k) for k in (1, 2, 3)], factor)
    gp_mine, group = lax.optimization_barrier((gp_mine, group))
    grad_in, grad_out = final(me, [group] + [swap(group, near_bits(k)) for k in (1, 2, 3)])
    grad_tokens = leave(gp_mine, w_qkv, tok, cot, mod)
    return grad_tokens.reshape(tokens.shape), grad_in, grad_out


def solution(mesh):
    placed = (
        P("dp", "vt", None, None, None),
        P("dp", "vt", None, None, None),
        P("dp", "vt", None, None),
        P(),
        P(),
        P(),
        P(),
        P("dp", "vt", None),
    )
    return jax.shard_map(
        shards,
        mesh=mesh,
        in_specs=placed,
        out_specs=(P("dp", "vt", None, None, None), P("vt", None), P("vt", None)),
        check_vma=False,
    )
```

```python
import math

import jax
import jax.numpy as jnp
from jax import lax
from jax.experimental import pallas as pl
from jax.experimental.pallas import tpu as pltpu
from jax.sharding import PartitionSpec as P

BF = jnp.bfloat16
F32 = jnp.float32
EPS = 1e-06
NN = (((1,), (0,)), ((), ()))
NT = (((1,), (1,)), ((), ()))
MIB = 1024 * 1024
LANES = 128


def dot(a, b, dims=NN):
    return lax.dot_general(a, b, dims, preferred_element_type=F32)


def whole(shape):
    return pl.BlockSpec(shape, lambda *_: (0,) * len(shape))


def params(mib):
    return pltpu.CompilerParams(vmem_limit_bytes=mib * MIB)


def normalise(values):
    center = values - jnp.mean(values, axis=-1, keepdims=True)
    spread = jnp.mean(center * center, axis=-1, keepdims=True)
    inverse = lax.rsqrt(spread + EPS)
    return center * inverse, inverse


def line(mod_ref, i):
    return mod_ref[i : i + 1, :]


def enter_kernel(nb_ref, tok_ref, cot_ref, mod_ref, out_ref):
    rows, features = tok_ref.shape
    normed, _ = normalise(tok_ref[...].astype(F32))
    hidden = normed * (1.0 + line(mod_ref, 1)) + line(mod_ref, 0)
    out_ref[:, :features] = hidden.astype(BF)
    lane = lax.broadcasted_iota(jnp.int32, (rows, LANES), 1)
    marks = jnp.where(lane == 0, nb_ref[0].astype(F32), nb_ref[1].astype(F32))
    out_ref[:, features : features + LANES] = marks.astype(BF)
    out_ref[:, features + LANES :] = (line(mod_ref, 2) * cot_ref[...].astype(F32)).astype(BF)


def enter(nb, tok, cot, mod):
    rows, features = tok.shape
    vm = pl.BlockSpec(memory_space=pltpu.VMEM)
    return pl.pallas_call(
        enter_kernel,
        in_specs=[pl.BlockSpec(memory_space=pltpu.SMEM), vm, vm, vm],
        out_specs=vm,
        out_shape=jax.ShapeDtypeStruct((rows, 2 * features + LANES), BF),
        compiler_params=params(58),
        name="enter",
    )(nb, tok, cot, mod)


def weights_kernel(head_ref, w_hbm, wo_hbm, w_ref, wo_ref, win, wo_win, sem):
    features, wide = w_ref.shape
    dim = wo_win.shape[0] - 8
    head = head_ref[0]
    copies = []
    gaps = []
    for p in range(3):
        first = features * p + dim * head
        start = jnp.minimum(first // LANES * LANES, 3 * features - wide)
        gaps.append(first - start)
        window = w_hbm.at[:, pl.ds(pl.multiple_of(start, LANES), wide)]
        copies.append(pltpu.make_async_copy(window, win.at[p], sem.at[p]))
    first = dim * head
    start = first // 16 * 16
    window = wo_hbm.at[pl.ds(pl.multiple_of(start, 16), wo_win.shape[0])]
    copies.append(pltpu.make_async_copy(window, wo_win, sem.at[3]))
    for copy in copies:
        copy.start()
    row = lax.broadcasted_iota(jnp.int32, (wide, wide), 0)
    column = lax.broadcasted_iota(jnp.int32, (wide, wide), 1)
    total = jnp.zeros((features, wide), F32)
    for p in range(3):
        inside = (column >= dim * p) & (column < dim * (p + 1))
        pick = jnp.where(inside & (row == column - dim * p + gaps[p]), 1.0, 0.0).astype(BF)
        copies[p].wait()
        total = total + dot(win[p], pick)
    w_ref[...] = total.astype(BF)
    row = lax.broadcasted_iota(jnp.int32, (LANES, dim + 8), 0)
    column = lax.broadcasted_iota(jnp.int32, (LANES, dim + 8), 1)
    pick = jnp.where((row < dim) & (column == row + (first - start)), 1.0, 0.0).astype(BF)
    copies[3].wait()
    wo_ref[...] = dot(pick, wo_win[...]).T.astype(BF)


def weights(head, w_qkv, w_out, dim):
    features = w_out.shape[0]
    wide = 2 * LANES
    vm = pl.BlockSpec(memory_space=pltpu.VMEM)
    hbm = pl.BlockSpec(memory_space=pltpu.HBM)
    return pl.pallas_call(
        weights_kernel,
        in_specs=[pl.BlockSpec(memory_space=pltpu.SMEM), hbm, hbm],
        out_specs=[vm, vm],
        out_shape=[
            jax.ShapeDtypeStruct((features, wide), BF),
            jax.ShapeDtypeStruct((features, LANES), BF),
        ],
        scratch_shapes=[
            pltpu.VMEM((3, features, wide), BF),
            pltpu.VMEM((dim + 8, features), BF),
            pltpu.SemaphoreType.DMA((4,)),
        ],
        compiler_params=params(52),
        name="weights",
    )(head, w_qkv, w_out)


def place(y, x, core):
    return (y * 4 + x) * 2 + core


def move(part, dy, dx, dc):
    pairs = [
        (place(y, x, c), place(y ^ dy, (x + dx) % 4, c ^ dc)) for y in range(2) for x in range(4) for c in range(2)
    ]
    return lax.ppermute(part, "vt", pairs)


def mix_kernel(a_ref, b_ref, c_ref, up_ref, down_ref, over_ref, all_ref):
    wide = a_ref.shape[1]
    half = down_ref.shape[1] // 2
    first = wide - half
    for i, ref in enumerate((a_ref, b_ref, c_ref)):
        all_ref[:, wide * i : wide * (i + 1)] = ref[...]
    up_ref[:, :first] = a_ref[:, :first]
    up_ref[:, first:] = c_ref[:, :first]
    down_ref[:, :half] = b_ref[:, first:]
    down_ref[:, half:] = c_ref[:, first:]
    over_ref[:, :half] = a_ref[:, first:]
    over_ref[:, half:] = b_ref[:, :first]


def mix(a, b, c, first):
    rows, wide = a.shape
    half = wide - first
    return pl.pallas_call(
        mix_kernel,
        out_shape=[
            jax.ShapeDtypeStruct((rows, 2 * first), BF),
            jax.ShapeDtypeStruct((rows, 2 * half), BF),
            jax.ShapeDtypeStruct((rows, wide), BF),
            jax.ShapeDtypeStruct((rows, 3 * wide), BF),
        ],
        compiler_params=params(16),
        name="mix",
    )(a, b, c)


def gather(hb, first, w, wo):
    half = hb.shape[1] - first
    low = move(hb, 0, 1, 0)
    high = move(hb, 0, -1, 0)
    side = move(hb, 1, 0, 0)
    twin = move(hb, 0, 0, 1)
    low, high, side, twin, w, wo = lax.optimization_barrier((low, high, side, twin, w, wo))
    up, down, over, three = mix(low, high, side, first)
    up, down, over, three = move(up, 0, 1, 0), move(down, 0, -1, 0), move(over, 1, 0, 0), move(three, 0, 0, 1)
    far_up = move(up[:, first:], 0, 1, 0)
    far_down = move(down[:, half:], 0, -1, 0)
    late = [up, down, over, far_up, far_down]
    arrays = [hb, low, high, side, twin, three] + late + [move(a, 0, 0, 1) for a in late]
    wide = hb.shape[1]
    slots = []
    for dc in range(2):
        near_four = [(4, 0), (5, 0), (5, wide), (5, 2 * wide)] if dc else [(n, 0) for n in range(4)]
        for at, (n, lane) in zip(((0, 0), (0, 3), (0, 1), (1, 0)), near_four):
            slots.append((at + (dc,), (n, lane), (n, lane + first)))
        n = 6 + 5 * dc
        slots += [
            ((0, 2, dc), (n, 0), (n + 1, 0)),
            ((1, 3, dc), (n, first), (n + 2, 0)),
            ((1, 1, dc), (n + 2, half), (n + 1, half)),
            ((1, 2, dc), (n + 3, 0), (n + 4, 0)),
        ]
    return arrays, slots, w, wo


def near(i):
    return i % 2 + 2 * (i // 8)


def far(i):
    return (i // 2) % 4


def near_bits(k):
    return k % 2 + 8 * (k // 2)


def heads_kernel(slots, dim, features, cams, me_ref, vt_ref, w_ref, wo_ref, qg_ref, kg_ref, *refs):
    count = len({n for _, *pairs in slots for n, _ in pairs})
    arrays, refs = refs[:count], refs[count:]
    gp_hbm, *sends, sem, gp_ref, nb, at, qn, kn, rad, qh, kh, vh, gh, krow, vrow, gq, gk, gv, acc, acc_out, spread = refs
    tokens = arrays[0].shape[0]
    width = 3 * dim
    scale = 1.0 / math.sqrt(dim)
    empty = jnp.zeros((1, tokens - dim), F32)
    qgain, kgain = (
        jnp.broadcast_to(jnp.concatenate([ref[...], empty], axis=1), (tokens, tokens)).T[:dim] for ref in (qg_ref, kg_ref)
    )
    pad = jnp.zeros((tokens - dim, tokens), F32)
    vt = vt_ref[0]
    y, x, core = vt // 8, vt // 2 % 4, vt % 2
    cameras = [place((y + dy) % 2, (x + dx) % 4, (core + dc) % 2) for (dy, dx, dc), _, _ in slots]

    def hidden(s):
        n, lane = slots[s][1]
        return arrays[n][:, lane : lane + features]

    def branch(s):
        n, lane = slots[s][2]
        return arrays[n][:, lane : lane + features]

    for s, c in enumerate(cameras):
        if s % 4 == 0:
            project = dot(jnp.concatenate([hidden(i) for i in range(s, s + 4)], axis=0), w_ref[...])
            back_out = dot(jnp.concatenate([branch(i) for i in range(s, s + 4)], axis=0), wo_ref[...])
        rows = slice(tokens * (s % 4), tokens * (s % 4 + 1))
        n, lane = slots[s][1]
        marks = arrays[n][:16, lane + features : lane + features + LANES].astype(F32)
        nb[c, 0] = marks[0, 0].astype(jnp.int32)
        nb[c, 1] = marks[0, 1].astype(jnp.int32)
        turned = project[rows].T
        q, k, v = (turned[dim * i : dim * (i + 1)] for i in range(3))
        rq = lax.rsqrt(jnp.mean(q * q, axis=0, keepdims=True) + EPS)
        rk = lax.rsqrt(jnp.mean(k * k, axis=0, keepdims=True) + EPS)
        q = q * rq
        k = k * rk
        qn[c] = q
        kn[c] = k
        rad[c, 0:1, :] = rq
        rad[c, 1:2, :] = rk
        q = q * qgain
        k = k * kgain
        qh[c] = jnp.concatenate([q, pad], axis=0).astype(BF)
        gh[c] = back_out[rows].T.astype(BF)
        kh[c] = k.astype(BF)
        vh[c] = v.astype(BF)
        krow[c] = jnp.concatenate([k, pad], axis=0).T.astype(BF)
        vrow[c] = jnp.concatenate([v, pad], axis=0).T.astype(BF)

    def camera(c, _):
        left = nb[c, 0]
        right = nb[c, 1]
        q = qh[c]
        g = gh[c]
        keys = jnp.concatenate([krow[left], krow[c], krow[right]], axis=0)
        values = jnp.concatenate([vrow[left], vrow[c], vrow[right]], axis=0)
        keys_t = jnp.concatenate([kh[left], kh[c], kh[right]], axis=1)
        values_t = jnp.concatenate([vh[left], vh[c], vh[right]], axis=1)
        e = jnp.exp(dot(keys, q) * scale)
        probs = e * (1.0 / jnp.sum(e, axis=0, keepdims=True))
        low = probs.astype(BF)
        gprobs = dot(values, g)
        centre = jnp.sum(probs * gprobs, axis=0, keepdims=True)
        gs = (probs * (gprobs - centre) * scale).astype(BF)
        at[c] = dot(values_t, low).astype(BF)
        gq[c] = dot(keys_t, gs)
        gk[c] = dot(q, gs, NT)[:dim]
        gv[c] = dot(g, low, NT)[:dim]
        return 0

    lax.fori_loop(0, cams, camera, 0, unroll=4)

    def back(grad, unit, radius, gain):
        shaped = grad * gain
        return (shaped - unit * jnp.mean(shaped * unit, axis=0, keepdims=True)) * radius

    def finish(c, _):
        left = nb[c, 0]
        right = nb[c, 1]
        grad_k = gk[c, :, tokens : 2 * tokens] + gk[left, :, 2 * tokens :] + gk[right, :, :tokens]
        grad_v = gv[c, :, tokens : 2 * tokens] + gv[left, :, 2 * tokens :] + gv[right, :, :tokens]
        grad_q = back(gq[c], qn[c], rad[c, 0:1, :], qgain)
        grad_k = back(grad_k, kn[c], rad[c, 1:2, :], kgain)
        gp_ref[c] = jnp.concatenate([grad_q, grad_k, grad_v], axis=0).astype(BF)
        return 0

    lax.fori_loop(0, cams, finish, 0, unroll=4)

    out = pltpu.make_async_copy(gp_ref, gp_hbm, sem)
    out.start()
    acc[width:, :] = jnp.zeros_like(acc[width:, :])
    for s in range(0, cams, 4):
        four = range(s, s + 4)
        grads = jnp.concatenate([gp_ref[cameras[i]] for i in four], axis=1)
        atts = jnp.concatenate([at[cameras[i]] for i in four], axis=1)
        one = dot(grads, jnp.concatenate([hidden(i) for i in four], axis=0))
        two = dot(atts, jnp.concatenate([branch(i) for i in four], axis=0))
        acc[:width, :] = one if s == 0 else acc[:width, :] + one
        acc_out[...] = two if s == 0 else acc_out[...] + two
    turned = acc[...].T
    for b in range(features // dim):
        spread[b, :, :width] = turned[dim * b : dim * (b + 1), :width].astype(BF)
        spread[b, :, width:] = acc_out[:, dim * b : dim * (b + 1)].astype(BF)
    me = me_ref[0]
    for k, ref in enumerate(sends):
        four = [spread[near_bits(near(me) ^ k) + 2 * a].astype(F32) for a in range(4)]
        ref[...] = jnp.concatenate(four, axis=1).astype(BF)
    out.wait()


def heads(me, vt, w, wo, q_gain, k_gain, arrays, slots):
    dim = q_gain.shape[0]
    features = wo.shape[0]
    tokens = arrays[0].shape[0]
    cams = len(slots)
    vm = pl.BlockSpec(memory_space=pltpu.VMEM)
    sm = pl.BlockSpec(memory_space=pltpu.SMEM)

    def body(*refs):
        heads_kernel(slots, dim, features, cams, *refs)

    return pl.pallas_call(
        body,
        in_specs=[sm, sm] + [vm] * (4 + len(arrays)),
        out_specs=[pl.BlockSpec(memory_space=pltpu.HBM)] + [vm] * 4,
        out_shape=[jax.ShapeDtypeStruct((cams, 3 * dim, tokens), BF)]
        + [jax.ShapeDtypeStruct((dim, 16 * dim), BF)] * 4,
        scratch_shapes=[
            pltpu.SemaphoreType.DMA,
            pltpu.VMEM((cams, 3 * dim, tokens), BF),
            pltpu.SMEM((cams, 2), jnp.int32),
            pltpu.VMEM((cams, dim, tokens), BF),
            pltpu.VMEM((cams, dim, tokens), F32),
            pltpu.VMEM((cams, dim, tokens), F32),
            pltpu.VMEM((cams, 8, tokens), F32),
            pltpu.VMEM((cams, tokens, tokens), BF),
            pltpu.VMEM((cams, dim, tokens), BF),
            pltpu.VMEM((cams, dim, tokens), BF),
            pltpu.VMEM((cams, tokens, tokens), BF),
            pltpu.VMEM((cams, tokens, tokens), BF),
            pltpu.VMEM((cams, tokens, tokens), BF),
            pltpu.VMEM((cams, dim, tokens), F32),
            pltpu.VMEM((cams, dim, 3 * tokens), F32),
            pltpu.VMEM((cams, dim, 3 * tokens), F32),
            pltpu.VMEM((2 * LANES, features), F32),
            pltpu.VMEM((dim, features), F32),
            pltpu.VMEM((features // dim, dim, 4 * dim), BF),
        ],
        compiler_params=params(36),
        name="heads",
    )(me, vt, w, wo, q_gain.reshape(1, dim), k_gain.reshape(1, dim), *arrays)


def leave_kernel(x_ref, w_ref, tok_ref, cot_ref, mod_ref, out_ref, scr, acc):
    part = pl.program_id(0)
    heads, width, _ = x_ref.shape
    dim = width // 3

    @pl.when(part == 0)
    def _():
        for h in range(heads):
            x = x_ref[h].astype(F32)
            for p in range(3):
                scr[p, dim * h : dim * (h + 1), :] = x[dim * p : dim * (p + 1)]
        acc[...] = jnp.zeros_like(acc)

    acc[...] += dot(w_ref[...], scr[part].astype(BF))

    @pl.when(part == 2)
    def _():
        scaled = acc[...].T * (1.0 + line(mod_ref, 1))
        normed, inverse = normalise(tok_ref[...].astype(F32))
        mean = jnp.mean(scaled, axis=-1, keepdims=True)
        along = jnp.mean(scaled * normed, axis=-1, keepdims=True)
        grad = inverse * (scaled - mean - normed * along)
        out_ref[...] = (cot_ref[...].astype(F32) + grad).astype(BF)


def leave(x, w_qkv, tok, cot, mod):
    rows, features = tok.shape
    return pl.pallas_call(
        leave_kernel,
        grid=(3,),
        in_specs=[
            whole(x.shape),
            pl.BlockSpec((features, features), lambda p: (0, p)),
            whole(tok.shape),
            whole(cot.shape),
            whole(mod.shape),
        ],
        out_specs=whole(tok.shape),
        out_shape=jax.ShapeDtypeStruct(tok.shape, BF),
        scratch_shapes=[
            pltpu.VMEM((3, features, rows), F32),
            pltpu.VMEM((features, rows), F32),
        ],
        compiler_params=params(58),
        name="leave",
    )(x, w_qkv, tok, cot, mod)


def fold_kernel(me_ref, a_ref, b_ref, c_ref, d_ref, *refs):
    *outs, rest_ref, four = refs
    dim, width = outs[0].shape
    total = a_ref[...].astype(F32) + b_ref[...].astype(F32) + c_ref[...].astype(F32) + d_ref[...].astype(F32)
    chunks = [total[:, (width + dim) * a : (width + dim) * (a + 1)] for a in range(4)]
    for a in range(4):
        four[a] = chunks[a][:, :width].astype(BF)
    rest_ref[...] = jnp.concatenate([c[:, width:] for c in chunks], axis=1).astype(BF)
    for k in range(4):
        outs[k][...] = four[far(me_ref[0]) ^ k]


def fold(me, parts):
    dim = parts[0].shape[0]
    width = 3 * dim
    vm = pl.BlockSpec(memory_space=pltpu.VMEM)
    shapes = [jax.ShapeDtypeStruct((dim, width), BF)] * 4 + [jax.ShapeDtypeStruct((dim, 4 * dim), BF)]
    return pl.pallas_call(
        fold_kernel,
        in_specs=[pl.BlockSpec(memory_space=pltpu.SMEM)] + [vm] * 4,
        out_specs=[vm] * 5,
        out_shape=shapes,
        scratch_shapes=[pltpu.VMEM((4, dim, width), BF)],
        compiler_params=params(16),
        name="fold",
    )(me, *parts)


def close_kernel(factor, a_ref, b_ref, c_ref, d_ref, rest_ref, out_ref):
    width = a_ref.shape[1]
    total = a_ref[...].astype(F32) + b_ref[...].astype(F32) + c_ref[...].astype(F32) + d_ref[...].astype(F32)
    both = jnp.concatenate([total * factor, rest_ref[...].astype(F32)], axis=1)
    out_ref[...] = both.astype(BF)


def close(parts, rest, factor):
    dim, width = parts[0].shape
    vm = pl.BlockSpec(memory_space=pltpu.VMEM)

    def body(*refs):
        close_kernel(factor, *refs)

    return pl.pallas_call(
        body,
        in_specs=[vm] * 5,
        out_specs=vm,
        out_shape=jax.ShapeDtypeStruct((dim, width + 4 * dim), BF),
        compiler_params=params(16),
        name="close",
    )(*parts, rest)


def join_kernel(factor, me_ref, a_ref, b_ref, c_ref, d_ref, out_ref, all_ref):
    dim = a_ref.shape[0]
    width = 3 * dim
    me = far(me_ref[0])
    four = [ref[...].astype(F32) for ref in (a_ref, b_ref, c_ref, d_ref)]
    rest = (four[0] + four[1] + four[2] + four[3])[:, width:] * factor
    for k in range(4):
        all_ref[me ^ k] = four[k][:, :width]
    pieces = []
    for a in range(4):
        pieces += [all_ref[a], rest[:, dim * a : dim * (a + 1)]]
    out_ref[...] = jnp.concatenate(pieces, axis=1).astype(BF)


def join(me, parts, factor):
    dim = parts[0].shape[0]
    vm = pl.BlockSpec(memory_space=pltpu.VMEM)

    def body(*refs):
        join_kernel(factor, *refs)

    return pl.pallas_call(
        body,
        in_specs=[pl.BlockSpec(memory_space=pltpu.SMEM)] + [vm] * 4,
        out_specs=vm,
        out_shape=jax.ShapeDtypeStruct((dim, 16 * dim), BF),
        scratch_shapes=[pltpu.VMEM((4, dim, 3 * dim), F32)],
        compiler_params=params(16),
        name="join",
    )(me, *parts)


def final_kernel(me_ref, a_ref, b_ref, c_ref, d_ref, in_ref, out_ref, all_ref):
    heads = 16
    dim, wide = a_ref.shape
    total = wide // 4
    me = me_ref[0]
    for k, ref in enumerate((a_ref, b_ref, c_ref, d_ref)):
        all_ref[k] = ref[...]
    lines = [all_ref[near(me) ^ k].astype(F32) for k in range(4)]
    blocks = [lines[near(h)][:, total * far(h) : total * (far(h) + 1)] for h in range(heads)]
    for p in range(4):
        part = jnp.concatenate([b[:, dim * p : dim * (p + 1)] for b in blocks], axis=1).astype(BF)
        if p < 3:
            in_ref[:, heads * dim * p : heads * dim * (p + 1)] = part
        else:
            out_ref[...] = part


def final(me, parts):
    dim, wide = parts[0].shape
    vm = pl.BlockSpec(memory_space=pltpu.VMEM)
    return pl.pallas_call(
        final_kernel,
        in_specs=[pl.BlockSpec(memory_space=pltpu.SMEM)] + [vm] * 4,
        out_specs=[vm] * 2,
        out_shape=[
            jax.ShapeDtypeStruct((dim, 3 * wide), BF),
            jax.ShapeDtypeStruct((dim, wide), BF),
        ],
        scratch_shapes=[pltpu.VMEM((4, dim, wide), BF)],
        compiler_params=params(16),
        name="final",
    )(me, *parts)


def swap(part, bits):
    return lax.ppermute(part, "dp", [(i, i ^ bits) for i in range(16)])


def cross(part, bits):
    return lax.ppermute(part, ("dp", "vt"), [(16 * a + b, 16 * b + (a ^ bits)) for a in range(16) for b in range(16)])


def front(me, vt, tok, cot, mod, q_gain, k_gain, w_qkv, w_out, nb):
    features = tok.shape[-1]
    hb = enter(nb, tok, cot, mod)
    w, wo = weights(vt, w_qkv, w_out, q_gain.shape[0])
    arrays, slots, w, wo = gather(hb, features + LANES, w, wo)
    return heads(me, vt, w, wo, q_gain, k_gain, arrays, slots)


def shards(tokens, cotangent, modulation, q_gain, k_gain, w_qkv, w_out, neighbours):
    rows, features = tokens.shape[-2:]
    factor = 1.0 / (lax.axis_size("dp") * lax.axis_size("vt"))
    me = lax.axis_index("dp").reshape(1)
    vt = lax.axis_index("vt").reshape(1)
    tok = tokens.reshape(rows, features)
    cot = cotangent.reshape(rows, features)
    mod = modulation.reshape(3, features)
    me, vt, tok = lax.optimization_barrier((me, vt, tok))
    gp, *sent = front(me, vt, tok, cot, mod, q_gain, k_gain, w_qkv, w_out, neighbours.reshape(2))
    parts = [sent[0]] + [swap(sent[k], near_bits(k)) for k in (1, 2, 3)]
    gp_mine = lax.all_to_all(gp, "vt", 0, 0)
    gp_mine, *parts = lax.optimization_barrier((gp_mine, *parts))
    *sums, rest = fold(me, parts)
    mine = close([cross(sums[k], 2 * k) for k in range(4)], rest, factor)
    group = join(me, [mine] + [swap(mine, 2 * k) for k in (1, 2, 3)], factor)
    grad_in, grad_out = final(me, [group] + [swap(group, near_bits(k)) for k in (1, 2, 3)])
    grad_tokens = leave(gp_mine, w_qkv, tok, cot, mod)
    return grad_tokens.reshape(tokens.shape), grad_in, grad_out


def solution(mesh):
    placed = (
        P("dp", "vt", None, None, None),
        P("dp", "vt", None, None, None),
        P("dp", "vt", None, None),
        P(),
        P(),
        P(),
        P(),
        P("dp", "vt", None),
    )
    return jax.shard_map(
        shards,
        mesh=mesh,
        in_specs=placed,
        out_specs=(P("dp", "vt", None, None, None), P("vt", None), P("vt", None)),
        check_vma=False,
    )
```

```python
import math

import jax
import jax.numpy as jnp
from jax import lax
from jax.experimental import pallas as pl
from jax.experimental.pallas import tpu as pltpu
from jax.sharding import PartitionSpec as P

BF = jnp.bfloat16
F32 = jnp.float32
EPS = 1e-06
NN = (((1,), (0,)), ((), ()))
NT = (((1,), (1,)), ((), ()))
MIB = 1024 * 1024
LANES = 128


def dot(a, b, dims=NN):
    return lax.dot_general(a, b, dims, preferred_element_type=F32)


def whole(shape):
    return pl.BlockSpec(shape, lambda *_: (0,) * len(shape))


def params(mib):
    return pltpu.CompilerParams(vmem_limit_bytes=mib * MIB)


def normalise(values):
    center = values - jnp.mean(values, axis=-1, keepdims=True)
    spread = jnp.mean(center * center, axis=-1, keepdims=True)
    inverse = lax.rsqrt(spread + EPS)
    return center * inverse, inverse


def line(mod_ref, i):
    return mod_ref[i : i + 1, :]


def enter_kernel(nb_ref, tok_ref, cot_ref, mod_ref, out_ref):
    rows, features = tok_ref.shape
    normed, _ = normalise(tok_ref[...].astype(F32))
    hidden = normed * (1.0 + line(mod_ref, 1)) + line(mod_ref, 0)
    out_ref[:, :features] = hidden.astype(BF)
    lane = lax.broadcasted_iota(jnp.int32, (rows, LANES), 1)
    marks = jnp.where(lane == 0, nb_ref[0].astype(F32), nb_ref[1].astype(F32))
    out_ref[:, features : features + LANES] = marks.astype(BF)
    out_ref[:, features + LANES :] = (line(mod_ref, 2) * cot_ref[...].astype(F32)).astype(BF)


def enter(nb, tok, cot, mod):
    rows, features = tok.shape
    vm = pl.BlockSpec(memory_space=pltpu.VMEM)
    return pl.pallas_call(
        enter_kernel,
        in_specs=[pl.BlockSpec(memory_space=pltpu.SMEM), vm, vm, vm],
        out_specs=vm,
        out_shape=jax.ShapeDtypeStruct((rows, 2 * features + LANES), BF),
        compiler_params=params(58),
        name="enter",
    )(nb, tok, cot, mod)


def weights_kernel(id_ref, w_hbm, wo_hbm, w_ref, wo_ref, win, wo_win, sem):
    features, wide = w_ref.shape
    dim = wo_win.shape[0] - 8
    head = id_ref[1]
    copies = []
    gaps = []
    for p in range(3):
        first = features * p + dim * head
        start = jnp.minimum(first // LANES * LANES, 3 * features - wide)
        gaps.append(first - start)
        window = w_hbm.at[:, pl.ds(pl.multiple_of(start, LANES), wide)]
        copies.append(pltpu.make_async_copy(window, win.at[p], sem.at[p]))
    first = dim * head
    start = first // 16 * 16
    window = wo_hbm.at[pl.ds(pl.multiple_of(start, 16), wo_win.shape[0])]
    copies.append(pltpu.make_async_copy(window, wo_win, sem.at[3]))
    for copy in copies:
        copy.start()
    row = lax.broadcasted_iota(jnp.int32, (wide, wide), 0)
    column = lax.broadcasted_iota(jnp.int32, (wide, wide), 1)
    total = jnp.zeros((features, wide), F32)
    for p in range(3):
        inside = (column >= dim * p) & (column < dim * (p + 1))
        pick = jnp.where(inside & (row == column - dim * p + gaps[p]), 1.0, 0.0).astype(BF)
        copies[p].wait()
        total = total + dot(win[p], pick)
    w_ref[...] = total.astype(BF)
    row = lax.broadcasted_iota(jnp.int32, (LANES, dim + 8), 0)
    column = lax.broadcasted_iota(jnp.int32, (LANES, dim + 8), 1)
    pick = jnp.where((row < dim) & (column == row + (first - start)), 1.0, 0.0).astype(BF)
    copies[3].wait()
    wo_ref[...] = dot(pick, wo_win[...]).T.astype(BF)


def weights(ids, w_qkv, w_out, dim):
    features = w_out.shape[0]
    wide = 2 * LANES
    vm = pl.BlockSpec(memory_space=pltpu.VMEM)
    hbm = pl.BlockSpec(memory_space=pltpu.HBM)
    return pl.pallas_call(
        weights_kernel,
        in_specs=[pl.BlockSpec(memory_space=pltpu.SMEM), hbm, hbm],
        out_specs=[vm, vm],
        out_shape=[
            jax.ShapeDtypeStruct((features, wide), BF),
            jax.ShapeDtypeStruct((features, LANES), BF),
        ],
        scratch_shapes=[
            pltpu.VMEM((3, features, wide), BF),
            pltpu.VMEM((dim + 8, features), BF),
            pltpu.SemaphoreType.DMA((4,)),
        ],
        compiler_params=params(52),
        name="weights",
    )(ids, w_qkv, w_out)


def place(y, x, core):
    return (y * 4 + x) * 2 + core


def move(part, dy, dx, dc):
    pairs = [
        (place(y, x, c), place(y ^ dy, (x + dx) % 4, c ^ dc)) for y in range(2) for x in range(4) for c in range(2)
    ]
    return lax.ppermute(part, "vt", pairs)


def mix_kernel(a_ref, b_ref, c_ref, up_ref, down_ref, over_ref, all_ref):
    wide = a_ref.shape[1]
    half = down_ref.shape[1] // 2
    first = wide - half
    for i, ref in enumerate((a_ref, b_ref, c_ref)):
        all_ref[:, wide * i : wide * (i + 1)] = ref[...]
    up_ref[:, :first] = a_ref[:, :first]
    up_ref[:, first:] = c_ref[:, :first]
    down_ref[:, :half] = b_ref[:, first:]
    down_ref[:, half:] = c_ref[:, first:]
    over_ref[:, :half] = a_ref[:, first:]
    over_ref[:, half:] = b_ref[:, :first]


def mix(a, b, c, first):
    rows, wide = a.shape
    half = wide - first
    return pl.pallas_call(
        mix_kernel,
        out_shape=[
            jax.ShapeDtypeStruct((rows, 2 * first), BF),
            jax.ShapeDtypeStruct((rows, 2 * half), BF),
            jax.ShapeDtypeStruct((rows, wide), BF),
            jax.ShapeDtypeStruct((rows, 3 * wide), BF),
        ],
        compiler_params=params(16),
        name="mix",
    )(a, b, c)


def gather(hb, first, w, wo):
    half = hb.shape[1] - first
    low = move(hb, 0, 1, 0)
    high = move(hb, 0, -1, 0)
    side = move(hb, 1, 0, 0)
    twin = move(hb, 0, 0, 1)
    low, high, side, twin, w, wo = lax.optimization_barrier((low, high, side, twin, w, wo))
    up, down, over, three = mix(low, high, side, first)
    up, down, over, three = move(up, 0, 1, 0), move(down, 0, -1, 0), move(over, 1, 0, 0), move(three, 0, 0, 1)
    far_up = move(up[:, first:], 0, 1, 0)
    far_down = move(down[:, half:], 0, -1, 0)
    late = [up, down, over, far_up, far_down]
    arrays = [hb, low, high, side, twin, three] + late + [move(a, 0, 0, 1) for a in late]
    wide = hb.shape[1]
    slots = []
    for dc in range(2):
        near_four = [(4, 0), (5, 0), (5, wide), (5, 2 * wide)] if dc else [(n, 0) for n in range(4)]
        for at, (n, lane) in zip(((0, 0), (0, 3), (0, 1), (1, 0)), near_four):
            slots.append((at + (dc,), (n, lane), (n, lane + first)))
        n = 6 + 5 * dc
        slots += [
            ((0, 2, dc), (n, 0), (n + 1, 0)),
            ((1, 3, dc), (n, first), (n + 2, 0)),
            ((1, 1, dc), (n + 2, half), (n + 1, half)),
            ((1, 2, dc), (n + 3, 0), (n + 4, 0)),
        ]
    return arrays, slots, w, wo


def near(i):
    return i % 2 + 2 * (i // 8)


def far(i):
    return (i // 2) % 4


def near_bits(k):
    return k % 2 + 8 * (k // 2)


def heads_kernel(slots, dim, features, cams, id_ref, w_ref, wo_ref, qg_ref, kg_ref, *refs):
    count = len({n for _, *pairs in slots for n, _ in pairs})
    arrays, refs = refs[:count], refs[count:]
    gp_hbm, *sends, sem, gp_ref, nb, at, qn, kn, rad, qh, kh, vh, gh, krow, vrow, gq, gk, gv, acc, acc_out, spread = refs
    tokens = arrays[0].shape[0]
    width = 3 * dim
    scale = 1.0 / math.sqrt(dim)
    empty = jnp.zeros((1, tokens - dim), F32)
    qgain, kgain = (
        jnp.broadcast_to(jnp.concatenate([ref[...], empty], axis=1), (tokens, tokens)).T[:dim] for ref in (qg_ref, kg_ref)
    )
    pad = jnp.zeros((tokens - dim, tokens), F32)
    me, vt = id_ref[0], id_ref[1]
    y, x, core = vt // 8, vt // 2 % 4, vt % 2
    cameras = [place((y + dy) % 2, (x + dx) % 4, (core + dc) % 2) for (dy, dx, dc), _, _ in slots]

    def hidden(s):
        n, lane = slots[s][1]
        return arrays[n][:, lane : lane + features]

    def branch(s):
        n, lane = slots[s][2]
        return arrays[n][:, lane : lane + features]

    for s, c in enumerate(cameras):
        if s % 4 == 0:
            project = dot(jnp.concatenate([hidden(i) for i in range(s, s + 4)], axis=0), w_ref[...])
            back_out = dot(jnp.concatenate([branch(i) for i in range(s, s + 4)], axis=0), wo_ref[...])
        rows = slice(tokens * (s % 4), tokens * (s % 4 + 1))
        n, lane = slots[s][1]
        marks = arrays[n][:16, lane + features : lane + features + LANES].astype(F32)
        nb[c, 0] = marks[0, 0].astype(jnp.int32)
        nb[c, 1] = marks[0, 1].astype(jnp.int32)
        turned = project[rows].T
        q, k, v = (turned[dim * i : dim * (i + 1)] for i in range(3))
        rq = lax.rsqrt(jnp.mean(q * q, axis=0, keepdims=True) + EPS)
        rk = lax.rsqrt(jnp.mean(k * k, axis=0, keepdims=True) + EPS)
        q = q * rq
        k = k * rk
        qn[c] = q
        kn[c] = k
        rad[c, 0:1, :] = rq
        rad[c, 1:2, :] = rk
        q = q * qgain
        k = k * kgain
        qh[c] = jnp.concatenate([q, pad], axis=0).astype(BF)
        gh[c] = back_out[rows].T.astype(BF)
        kh[c] = k.astype(BF)
        vh[c] = v.astype(BF)
        krow[c] = jnp.concatenate([k, pad], axis=0).T.astype(BF)
        vrow[c] = jnp.concatenate([v, pad], axis=0).T.astype(BF)

    def camera(c, _):
        left = nb[c, 0]
        right = nb[c, 1]
        q = qh[c]
        g = gh[c]
        keys = jnp.concatenate([krow[left], krow[c], krow[right]], axis=0)
        values = jnp.concatenate([vrow[left], vrow[c], vrow[right]], axis=0)
        keys_t = jnp.concatenate([kh[left], kh[c], kh[right]], axis=1)
        values_t = jnp.concatenate([vh[left], vh[c], vh[right]], axis=1)
        e = jnp.exp(dot(keys, q) * scale)
        probs = e * (1.0 / jnp.sum(e, axis=0, keepdims=True))
        low = probs.astype(BF)
        gprobs = dot(values, g)
        centre = jnp.sum(probs * gprobs, axis=0, keepdims=True)
        gs = (probs * (gprobs - centre) * scale).astype(BF)
        at[c] = dot(values_t, low).astype(BF)
        gq[c] = dot(keys_t, gs)
        gk[c] = dot(q, gs, NT)[:dim]
        gv[c] = dot(g, low, NT)[:dim]
        return 0

    lax.fori_loop(0, cams, camera, 0, unroll=4)

    def back(grad, unit, radius, gain):
        shaped = grad * gain
        return (shaped - unit * jnp.mean(shaped * unit, axis=0, keepdims=True)) * radius

    def finish(c, _):
        left = nb[c, 0]
        right = nb[c, 1]
        grad_k = gk[c, :, tokens : 2 * tokens] + gk[left, :, 2 * tokens :] + gk[right, :, :tokens]
        grad_v = gv[c, :, tokens : 2 * tokens] + gv[left, :, 2 * tokens :] + gv[right, :, :tokens]
        grad_q = back(gq[c], qn[c], rad[c, 0:1, :], qgain)
        grad_k = back(grad_k, kn[c], rad[c, 1:2, :], kgain)
        gp_ref[c] = jnp.concatenate([grad_q, grad_k, grad_v], axis=0).astype(BF)
        return 0

    lax.fori_loop(0, cams, finish, 0, unroll=4)

    out = pltpu.make_async_copy(gp_ref, gp_hbm, sem)
    out.start()
    acc[width:, :] = jnp.zeros_like(acc[width:, :])
    for s in range(0, cams, 4):
        four = range(s, s + 4)
        grads = jnp.concatenate([gp_ref[cameras[i]] for i in four], axis=1)
        atts = jnp.concatenate([at[cameras[i]] for i in four], axis=1)
        one = dot(grads, jnp.concatenate([hidden(i) for i in four], axis=0))
        two = dot(atts, jnp.concatenate([branch(i) for i in four], axis=0))
        acc[:width, :] = one if s == 0 else acc[:width, :] + one
        acc_out[...] = two if s == 0 else acc_out[...] + two
    turned = acc[...].T
    for b in range(features // dim):
        spread[b, :, :width] = turned[dim * b : dim * (b + 1), :width].astype(BF)
        spread[b, :, width:] = acc_out[:, dim * b : dim * (b + 1)].astype(BF)
    for k, ref in enumerate(sends):
        four = [spread[(near_bits(near(me) ^ k) + 2 * a) ^ vt].astype(F32) for a in range(4)]
        ref[...] = jnp.concatenate(four, axis=1).astype(BF)
    out.wait()


def heads(ids, w, wo, q_gain, k_gain, arrays, slots):
    dim = q_gain.shape[0]
    features = wo.shape[0]
    tokens = arrays[0].shape[0]
    cams = len(slots)
    vm = pl.BlockSpec(memory_space=pltpu.VMEM)
    sm = pl.BlockSpec(memory_space=pltpu.SMEM)

    def body(*refs):
        heads_kernel(slots, dim, features, cams, *refs)

    return pl.pallas_call(
        body,
        in_specs=[sm] + [vm] * (4 + len(arrays)),
        out_specs=[pl.BlockSpec(memory_space=pltpu.HBM)] + [vm] * 4,
        out_shape=[jax.ShapeDtypeStruct((cams, 3 * dim, tokens), BF)]
        + [jax.ShapeDtypeStruct((dim, 16 * dim), BF)] * 4,
        scratch_shapes=[
            pltpu.SemaphoreType.DMA,
            pltpu.VMEM((cams, 3 * dim, tokens), BF),
            pltpu.SMEM((cams, 2), jnp.int32),
            pltpu.VMEM((cams, dim, tokens), BF),
            pltpu.VMEM((cams, dim, tokens), F32),
            pltpu.VMEM((cams, dim, tokens), F32),
            pltpu.VMEM((cams, 8, tokens), F32),
            pltpu.VMEM((cams, tokens, tokens), BF),
            pltpu.VMEM((cams, dim, tokens), BF),
            pltpu.VMEM((cams, dim, tokens), BF),
            pltpu.VMEM((cams, tokens, tokens), BF),
            pltpu.VMEM((cams, tokens, tokens), BF),
            pltpu.VMEM((cams, tokens, tokens), BF),
            pltpu.VMEM((cams, dim, tokens), F32),
            pltpu.VMEM((cams, dim, 3 * tokens), F32),
            pltpu.VMEM((cams, dim, 3 * tokens), F32),
            pltpu.VMEM((2 * LANES, features), F32),
            pltpu.VMEM((dim, features), F32),
            pltpu.VMEM((features // dim, dim, 4 * dim), BF),
        ],
        compiler_params=params(36),
        name="heads",
    )(ids, w, wo, q_gain.reshape(1, dim), k_gain.reshape(1, dim), *arrays)


def leave_kernel(x_ref, w_ref, tok_ref, cot_ref, mod_ref, out_ref, scr, acc):
    part = pl.program_id(0)
    heads, width, _ = x_ref.shape
    dim = width // 3

    @pl.when(part == 0)
    def _():
        for h in range(heads):
            x = x_ref[h].astype(F32)
            for p in range(3):
                scr[p, dim * h : dim * (h + 1), :] = x[dim * p : dim * (p + 1)]
        acc[...] = jnp.zeros_like(acc)

    acc[...] += dot(w_ref[...], scr[part].astype(BF))

    @pl.when(part == 2)
    def _():
        scaled = acc[...].T * (1.0 + line(mod_ref, 1))
        normed, inverse = normalise(tok_ref[...].astype(F32))
        mean = jnp.mean(scaled, axis=-1, keepdims=True)
        along = jnp.mean(scaled * normed, axis=-1, keepdims=True)
        grad = inverse * (scaled - mean - normed * along)
        out_ref[...] = (cot_ref[...].astype(F32) + grad).astype(BF)


def leave(x, w_qkv, tok, cot, mod):
    rows, features = tok.shape
    return pl.pallas_call(
        leave_kernel,
        grid=(3,),
        in_specs=[
            whole(x.shape),
            pl.BlockSpec((features, features), lambda p: (0, p)),
            whole(tok.shape),
            whole(cot.shape),
            whole(mod.shape),
        ],
        out_specs=whole(tok.shape),
        out_shape=jax.ShapeDtypeStruct(tok.shape, BF),
        scratch_shapes=[
            pltpu.VMEM((3, features, rows), F32),
            pltpu.VMEM((features, rows), F32),
        ],
        compiler_params=params(58),
        name="leave",
    )(x, w_qkv, tok, cot, mod)


def fold_kernel(id_ref, a_ref, b_ref, c_ref, d_ref, *refs):
    *outs, rest_ref, four, rest = refs
    dim, width = outs[0].shape
    total = a_ref[...].astype(F32) + b_ref[...].astype(F32) + c_ref[...].astype(F32) + d_ref[...].astype(F32)
    chunks = [total[:, (width + dim) * a : (width + dim) * (a + 1)] for a in range(4)]
    for a in range(4):
        four[a] = chunks[a][:, :width].astype(BF)
        rest[a] = chunks[a][:, width:]
    rest_ref[...] = jnp.concatenate([rest[far(id_ref[1]) ^ a] for a in range(4)], axis=1).astype(BF)
    for k in range(4):
        outs[k][...] = four[far(id_ref[0]) ^ k]


def fold(ids, parts):
    dim = parts[0].shape[0]
    width = 3 * dim
    vm = pl.BlockSpec(memory_space=pltpu.VMEM)
    shapes = [jax.ShapeDtypeStruct((dim, width), BF)] * 4 + [jax.ShapeDtypeStruct((dim, 4 * dim), BF)]
    return pl.pallas_call(
        fold_kernel,
        in_specs=[pl.BlockSpec(memory_space=pltpu.SMEM)] + [vm] * 4,
        out_specs=[vm] * 5,
        out_shape=shapes,
        scratch_shapes=[pltpu.VMEM((4, dim, width), BF), pltpu.VMEM((4, dim, dim), F32)],
        compiler_params=params(16),
        name="fold",
    )(ids, *parts)


def close_kernel(factor, a_ref, b_ref, c_ref, d_ref, rest_ref, out_ref):
    width = a_ref.shape[1]
    total = a_ref[...].astype(F32) + b_ref[...].astype(F32) + c_ref[...].astype(F32) + d_ref[...].astype(F32)
    both = jnp.concatenate([total * factor, rest_ref[...].astype(F32)], axis=1)
    out_ref[...] = both.astype(BF)


def close(parts, rest, factor):
    dim, width = parts[0].shape
    vm = pl.BlockSpec(memory_space=pltpu.VMEM)

    def body(*refs):
        close_kernel(factor, *refs)

    return pl.pallas_call(
        body,
        in_specs=[vm] * 5,
        out_specs=vm,
        out_shape=jax.ShapeDtypeStruct((dim, width + 4 * dim), BF),
        compiler_params=params(16),
        name="close",
    )(*parts, rest)


def join_kernel(factor, id_ref, a_ref, b_ref, c_ref, d_ref, out_ref, all_ref):
    dim = a_ref.shape[0]
    width = 3 * dim
    me = far(id_ref[2])
    four = [ref[...].astype(F32) for ref in (a_ref, b_ref, c_ref, d_ref)]
    rest = (four[0] + four[1] + four[2] + four[3])[:, width:] * factor
    for k in range(4):
        all_ref[me ^ k] = four[k][:, :width]
    pieces = []
    for a in range(4):
        pieces += [all_ref[a], rest[:, dim * a : dim * (a + 1)]]
    out_ref[...] = jnp.concatenate(pieces, axis=1).astype(BF)


def join(ids, parts, factor):
    dim = parts[0].shape[0]
    vm = pl.BlockSpec(memory_space=pltpu.VMEM)

    def body(*refs):
        join_kernel(factor, *refs)

    return pl.pallas_call(
        body,
        in_specs=[pl.BlockSpec(memory_space=pltpu.SMEM)] + [vm] * 4,
        out_specs=vm,
        out_shape=jax.ShapeDtypeStruct((dim, 16 * dim), BF),
        scratch_shapes=[pltpu.VMEM((4, dim, 3 * dim), F32)],
        compiler_params=params(16),
        name="join",
    )(ids, *parts)


def final_kernel(id_ref, a_ref, b_ref, c_ref, d_ref, in_ref, out_ref, all_ref):
    heads = 16
    dim, wide = a_ref.shape
    total = wide // 4
    me = id_ref[2]
    for k, ref in enumerate((a_ref, b_ref, c_ref, d_ref)):
        all_ref[k] = ref[...]
    lines = [all_ref[near(me) ^ k].astype(F32) for k in range(4)]
    blocks = [lines[near(h)][:, total * far(h) : total * (far(h) + 1)] for h in range(heads)]
    for p in range(4):
        part = jnp.concatenate([b[:, dim * p : dim * (p + 1)] for b in blocks], axis=1).astype(BF)
        if p < 3:
            in_ref[:, heads * dim * p : heads * dim * (p + 1)] = part
        else:
            out_ref[...] = part


def final(ids, parts):
    dim, wide = parts[0].shape
    vm = pl.BlockSpec(memory_space=pltpu.VMEM)
    return pl.pallas_call(
        final_kernel,
        in_specs=[pl.BlockSpec(memory_space=pltpu.SMEM)] + [vm] * 4,
        out_specs=[vm] * 2,
        out_shape=[
            jax.ShapeDtypeStruct((dim, 3 * wide), BF),
            jax.ShapeDtypeStruct((dim, wide), BF),
        ],
        scratch_shapes=[pltpu.VMEM((4, dim, wide), BF)],
        compiler_params=params(16),
        name="final",
    )(ids, *parts)


def swap(part, bits):
    return lax.ppermute(part, "dp", [(i, i ^ bits) for i in range(16)])


def cross(part, bits):
    pairs = [(16 * a + b, 16 * (a ^ bits) + (a ^ bits ^ b)) for a in range(16) for b in range(16)]
    return lax.ppermute(part, ("dp", "vt"), pairs)


def front(ids, tok, cot, mod, q_gain, k_gain, w_qkv, w_out, nb):
    features = tok.shape[-1]
    hb = enter(nb, tok, cot, mod)
    w, wo = weights(ids, w_qkv, w_out, q_gain.shape[0])
    arrays, slots, w, wo = gather(hb, features + LANES, w, wo)
    return heads(ids, w, wo, q_gain, k_gain, arrays, slots)


def shards(tokens, cotangent, modulation, q_gain, k_gain, w_qkv, w_out, neighbours):
    rows, features = tokens.shape[-2:]
    factor = 1.0 / (lax.axis_size("dp") * lax.axis_size("vt"))
    me = lax.axis_index("dp")
    vt = lax.axis_index("vt")
    ids = jnp.stack([me, vt, me ^ vt])
    tok = tokens.reshape(rows, features)
    cot = cotangent.reshape(rows, features)
    mod = modulation.reshape(3, features)
    ids, tok = lax.optimization_barrier((ids, tok))
    gp, *sent = front(ids, tok, cot, mod, q_gain, k_gain, w_qkv, w_out, neighbours.reshape(2))
    parts = [sent[0]] + [swap(sent[k], near_bits(k)) for k in (1, 2, 3)]
    gp, *parts = lax.optimization_barrier((gp, *parts))
    gp_mine = lax.all_to_all(gp, "vt", 0, 0)
    *sums, rest = fold(ids, parts)
    mine = close([cross(sums[k], 2 * k) for k in range(4)], rest, factor)
    group = join(ids, [mine] + [swap(mine, 2 * k) for k in (1, 2, 3)], factor)
    gp_mine, group = lax.optimization_barrier((gp_mine, group))
    grad_in, grad_out = final(ids, [group] + [swap(group, near_bits(k)) for k in (1, 2, 3)])
    grad_tokens = leave(gp_mine, w_qkv, tok, cot, mod)
    return grad_tokens.reshape(tokens.shape), grad_in, grad_out


def solution(mesh):
    placed = (
        P("dp", "vt", None, None, None),
        P("dp", "vt", None, None, None),
        P("dp", "vt", None, None),
        P(),
        P(),
        P(),
        P(),
        P("dp", "vt", None),
    )
    return jax.shard_map(
        shards,
        mesh=mesh,
        in_specs=placed,
        out_specs=(P("dp", "vt", None, None, None), P("vt", None), P("vt", None)),
        check_vma=False,
    )
```

```python
import math

import jax
import jax.numpy as jnp
from jax import lax
from jax.experimental import pallas as pl
from jax.experimental.pallas import tpu as pltpu
from jax.sharding import PartitionSpec as P

BF = jnp.bfloat16
F32 = jnp.float32
EPS = 1e-06
NN = (((1,), (0,)), ((), ()))
NT = (((1,), (1,)), ((), ()))
MIB = 1024 * 1024
LANES = 128


def dot(a, b, dims=NN):
    return lax.dot_general(a, b, dims, preferred_element_type=F32)


def whole(shape):
    return pl.BlockSpec(shape, lambda *_: (0,) * len(shape))


def params(mib):
    return pltpu.CompilerParams(vmem_limit_bytes=mib * MIB)


def normalise(values):
    center = values - jnp.mean(values, axis=-1, keepdims=True)
    spread = jnp.mean(center * center, axis=-1, keepdims=True)
    inverse = lax.rsqrt(spread + EPS)
    return center * inverse, inverse


def line(mod_ref, i):
    return mod_ref[i]


def enter_kernel(nb_ref, tok_ref, cot_ref, mod_ref, out_ref):
    rows, features = tok_ref.shape
    normed, _ = normalise(tok_ref[...].astype(F32))
    hidden = normed * (1.0 + line(mod_ref, 1)) + line(mod_ref, 0)
    out_ref[:, :features] = hidden.astype(BF)
    lane = lax.broadcasted_iota(jnp.int32, (rows, LANES), 1)
    marks = jnp.where(lane == 0, nb_ref[0].astype(F32), nb_ref[1].astype(F32))
    out_ref[:, features : features + LANES] = marks.astype(BF)
    out_ref[:, features + LANES :] = (line(mod_ref, 2) * cot_ref[...].astype(F32)).astype(BF)


def enter(nb, tok, cot, mod):
    rows, features = tok.shape
    vm = pl.BlockSpec(memory_space=pltpu.VMEM)
    return pl.pallas_call(
        enter_kernel,
        in_specs=[pl.BlockSpec(memory_space=pltpu.SMEM), vm, vm, vm],
        out_specs=vm,
        out_shape=jax.ShapeDtypeStruct((rows, 2 * features + LANES), BF),
        compiler_params=params(58),
        name="enter",
    )(nb, tok, cot, mod)


def weights_kernel(id_ref, w_hbm, wo_hbm, w_ref, wo_ref, win, wo_win, sem):
    features, wide = w_ref.shape
    dim = wo_win.shape[0] - 8
    head = id_ref[1]
    copies = []
    gaps = []
    for p in range(3):
        first = features * p + dim * head
        start = jnp.minimum(first // LANES * LANES, 3 * features - wide)
        gaps.append(first - start)
        window = w_hbm.at[:, pl.ds(pl.multiple_of(start, LANES), wide)]
        copies.append(pltpu.make_async_copy(window, win.at[p], sem.at[p]))
    first = dim * head
    start = first // 16 * 16
    window = wo_hbm.at[pl.ds(pl.multiple_of(start, 16), wo_win.shape[0])]
    copies.append(pltpu.make_async_copy(window, wo_win, sem.at[3]))
    for copy in copies:
        copy.start()
    row = lax.broadcasted_iota(jnp.int32, (wide, wide), 0)
    column = lax.broadcasted_iota(jnp.int32, (wide, wide), 1)
    total = jnp.zeros((features, wide), F32)
    for p in range(3):
        inside = (column >= dim * p) & (column < dim * (p + 1))
        pick = jnp.where(inside & (row == column - dim * p + gaps[p]), 1.0, 0.0).astype(BF)
        copies[p].wait()
        total = total + dot(win[p], pick)
    w_ref[...] = total.astype(BF)
    row = lax.broadcasted_iota(jnp.int32, (LANES, dim + 8), 0)
    column = lax.broadcasted_iota(jnp.int32, (LANES, dim + 8), 1)
    pick = jnp.where((row < dim) & (column == row + (first - start)), 1.0, 0.0).astype(BF)
    copies[3].wait()
    wo_ref[...] = dot(pick, wo_win[...]).T.astype(BF)


def weights(ids, w_qkv, w_out, dim):
    features = w_out.shape[0]
    wide = 2 * LANES
    vm = pl.BlockSpec(memory_space=pltpu.VMEM)
    hbm = pl.BlockSpec(memory_space=pltpu.HBM)
    return pl.pallas_call(
        weights_kernel,
        in_specs=[pl.BlockSpec(memory_space=pltpu.SMEM), hbm, hbm],
        out_specs=[vm, vm],
        out_shape=[
            jax.ShapeDtypeStruct((features, wide), BF),
            jax.ShapeDtypeStruct((features, LANES), BF),
        ],
        scratch_shapes=[
            pltpu.VMEM((3, features, wide), BF),
            pltpu.VMEM((dim + 8, features), BF),
            pltpu.SemaphoreType.DMA((4,)),
        ],
        compiler_params=params(52),
        name="weights",
    )(ids, w_qkv, w_out)


def place(y, x, core):
    return (y * 4 + x) * 2 + core


def move(part, dy, dx, dc):
    pairs = [
        (place(y, x, c), place(y ^ dy, (x + dx) % 4, c ^ dc)) for y in range(2) for x in range(4) for c in range(2)
    ]
    return lax.ppermute(part, "vt", pairs)


def mix_kernel(a_ref, b_ref, c_ref, up_ref, down_ref, over_ref, all_ref):
    wide = a_ref.shape[1]
    half = down_ref.shape[1] // 2
    first = wide - half
    for i, ref in enumerate((a_ref, b_ref, c_ref)):
        all_ref[:, wide * i : wide * (i + 1)] = ref[...]
    up_ref[:, :first] = a_ref[:, :first]
    up_ref[:, first:] = c_ref[:, :first]
    down_ref[:, :half] = b_ref[:, first:]
    down_ref[:, half:] = c_ref[:, first:]
    over_ref[:, :half] = a_ref[:, first:]
    over_ref[:, half:] = b_ref[:, :first]


def mix(a, b, c, first):
    rows, wide = a.shape
    half = wide - first
    return pl.pallas_call(
        mix_kernel,
        out_shape=[
            jax.ShapeDtypeStruct((rows, 2 * first), BF),
            jax.ShapeDtypeStruct((rows, 2 * half), BF),
            jax.ShapeDtypeStruct((rows, wide), BF),
            jax.ShapeDtypeStruct((rows, 3 * wide), BF),
        ],
        compiler_params=params(16),
        name="mix",
    )(a, b, c)


def gather(hb, first, w, wo, gains):
    half = hb.shape[1] - first
    low = move(hb, 0, 1, 0)
    high = move(hb, 0, -1, 0)
    side = move(hb, 1, 0, 0)
    twin = move(hb, 0, 0, 1)
    low, high, side, twin, w, wo = lax.optimization_barrier((low, high, side, twin, w, wo))
    up, down, over, three = mix(low, high, side, first)
    up, down, over, three = move(up, 0, 1, 0), move(down, 0, -1, 0), move(over, 1, 0, 0), move(three, 0, 0, 1)
    wide = hb.shape[1]
    slots = []
    for dc in range(2):
        near_four = [(4, 0), (5, 0), (5, wide), (5, 2 * wide)] if dc else [(n, 0) for n in range(4)]
        for at, (n, lane) in zip(((0, 0), (0, 3), (0, 1), (1, 0)), near_four):
            slots.append((at + (dc,), (n, lane), (n, lane + first)))
        n = 6 + 5 * dc
        slots += [
            ((0, 2, dc), (n, 0), (n + 1, 0)),
            ((1, 3, dc), (n, first), (n + 2, 0)),
            ((1, 1, dc), (n + 2, half), (n + 1, half)),
            ((1, 2, dc), (n + 3, 0), (n + 4, 0)),
        ]
    soon = [hb, low, high, side, twin, three]
    readies = early(w, wo, gains, soon, slots)
    up, down, *readies = lax.optimization_barrier((up, down, *readies))
    far_up = move(up[:, first:], 0, 1, 0)
    far_down = move(down[:, half:], 0, -1, 0)
    late = [up, down, over, far_up, far_down]
    arrays = soon + late + [move(a, 0, 0, 1) for a in late]
    return arrays, slots, readies, w, wo


def near(i):
    return i % 2 + 2 * (i // 8)


def far(i):
    return (i // 2) % 4


def near_bits(k):
    return k % 2 + 8 * (k // 2)


EARLY = (0, 1, 2, 3, 8, 9, 10, 11)


def column(ref, tokens):
    dim = ref.shape[1]
    row = jnp.concatenate([ref[...], jnp.zeros((1, tokens - dim), F32)], axis=1)
    return jnp.broadcast_to(row, (tokens, tokens)).T[:dim]


def ready_shapes(count, dim, tokens):
    thin, square = (count, dim, tokens), (count, tokens, tokens)
    shapes = [thin, thin, (count, 8, tokens), square, thin, thin, square, square, square]
    return [(shape, F32 if i < 3 else BF) for i, shape in enumerate(shapes)]


def ready_kernel(picked, places, hidden, branch, w_ref, wo_ref, qgain, kgain, stores):
    qn, kn, rad, qh, kh, vh, gh, krow, vrow = stores
    dim, tokens = qgain.shape
    pad = jnp.zeros((tokens - dim, tokens), F32)
    for i, c in enumerate(places):
        if i % 4 == 0:
            four = picked[i : i + 4]
            project = dot(jnp.concatenate([hidden(s) for s in four], axis=0), w_ref[...])
            back_out = dot(jnp.concatenate([branch(s) for s in four], axis=0), wo_ref[...])
        rows = slice(tokens * (i % 4), tokens * (i % 4 + 1))
        turned = project[rows].T
        q, k, v = (turned[dim * n : dim * (n + 1)] for n in range(3))
        rq = lax.rsqrt(jnp.mean(q * q, axis=0, keepdims=True) + EPS)
        rk = lax.rsqrt(jnp.mean(k * k, axis=0, keepdims=True) + EPS)
        q = q * rq
        k = k * rk
        qn[c] = q
        kn[c] = k
        rad[c] = jnp.concatenate([rq, rk, jnp.zeros((6, tokens), F32)], axis=0)
        q = q * qgain
        k = k * kgain
        qh[c] = jnp.concatenate([q, pad], axis=0).astype(BF)
        gh[c] = back_out[rows].T.astype(BF)
        kh[c] = k.astype(BF)
        vh[c] = v.astype(BF)
        krow[c] = jnp.concatenate([k, pad], axis=0).T.astype(BF)
        vrow[c] = jnp.concatenate([v, pad], axis=0).T.astype(BF)


def early_kernel(slots, features, w_ref, wo_ref, qg_ref, kg_ref, *refs):
    arrays, stores = refs[:-9], refs[-9:]
    tokens = arrays[0].shape[0]

    def hidden(s):
        n, lane = slots[s][1]
        return arrays[n][:, lane : lane + features]

    def branch(s):
        n, lane = slots[s][2]
        return arrays[n][:, lane : lane + features]

    gains = column(qg_ref, tokens), column(kg_ref, tokens)
    ready_kernel(EARLY, range(len(EARLY)), hidden, branch, w_ref, wo_ref, *gains, stores)


def early(w, wo, gains, arrays, slots):
    features = wo.shape[0]
    dim = gains[0].shape[1]
    tokens = arrays[0].shape[0]
    vm = pl.BlockSpec(memory_space=pltpu.VMEM)

    def body(*refs):
        early_kernel(slots, features, *refs)

    return pl.pallas_call(
        body,
        in_specs=[vm] * (4 + len(arrays)),
        out_specs=[vm] * 9,
        out_shape=[jax.ShapeDtypeStruct(*shape) for shape in ready_shapes(len(EARLY), dim, tokens)],
        compiler_params=params(24),
        name="early",
    )(w, wo, *gains, *arrays)


def heads_kernel(slots, dim, features, cams, id_ref, w_ref, wo_ref, qg_ref, kg_ref, *refs):
    count = len({n for _, *pairs in slots for n, _ in pairs})
    arrays, refs = refs[:count], refs[count:]
    readies, refs = refs[:9], refs[9:]
    gp_hbm, *sends, sem, gp_ref, nb, at, gq, gk, gv, acc, acc_out, spread = refs[:-9]
    stores = refs[-9:]
    qn, kn, rad, qh, kh, vh, gh, krow, vrow = stores
    tokens = arrays[0].shape[0]
    width = 3 * dim
    scale = 1.0 / math.sqrt(dim)
    qgain, kgain = column(qg_ref, tokens), column(kg_ref, tokens)
    me, vt = id_ref[0], id_ref[1]
    y, x, core = vt // 8, vt // 2 % 4, vt % 2
    cameras = [place((y + dy) % 2, (x + dx) % 4, (core + dc) % 2) for (dy, dx, dc), _, _ in slots]

    def hidden(s):
        n, lane = slots[s][1]
        return arrays[n][:, lane : lane + features]

    def branch(s):
        n, lane = slots[s][2]
        return arrays[n][:, lane : lane + features]

    for s, c in enumerate(cameras):
        n, lane = slots[s][1]
        marks = arrays[n][:16, lane + features : lane + features + LANES].astype(F32)
        nb[c, 0] = marks[0, 0].astype(jnp.int32)
        nb[c, 1] = marks[0, 1].astype(jnp.int32)
    for e, s in enumerate(EARLY):
        for ref, ready in zip(stores, readies):
            ref[cameras[s]] = ready[e]
    late = [s for s in range(cams) if s not in EARLY]
    ready_kernel(late, [cameras[s] for s in late], hidden, branch, w_ref, wo_ref, qgain, kgain, stores)

    def camera(c, _):
        left = nb[c, 0]
        right = nb[c, 1]
        q = qh[c]
        g = gh[c]
        keys = jnp.concatenate([krow[left], krow[c], krow[right]], axis=0)
        values = jnp.concatenate([vrow[left], vrow[c], vrow[right]], axis=0)
        keys_t = jnp.concatenate([kh[left], kh[c], kh[right]], axis=1)
        values_t = jnp.concatenate([vh[left], vh[c], vh[right]], axis=1)
        e = jnp.exp(dot(keys, q) * scale)
        probs = e * (1.0 / jnp.sum(e, axis=0, keepdims=True))
        low = probs.astype(BF)
        gprobs = dot(values, g)
        centre = jnp.sum(probs * gprobs, axis=0, keepdims=True)
        gs = (probs * (gprobs - centre) * scale).astype(BF)
        at[c] = dot(values_t, low).astype(BF)
        gq[c] = dot(keys_t, gs)
        gk[c] = dot(q, gs, NT)[:dim]
        gv[c] = dot(g, low, NT)[:dim]
        return 0

    lax.fori_loop(0, cams, camera, 0, unroll=4)

    def back(grad, unit, radius, gain):
        shaped = grad * gain
        return (shaped - unit * jnp.mean(shaped * unit, axis=0, keepdims=True)) * radius

    def finish(c, _):
        left = nb[c, 0]
        right = nb[c, 1]
        grad_k = gk[c, :, tokens : 2 * tokens] + gk[left, :, 2 * tokens :] + gk[right, :, :tokens]
        grad_v = gv[c, :, tokens : 2 * tokens] + gv[left, :, 2 * tokens :] + gv[right, :, :tokens]
        grad_q = back(gq[c], qn[c], rad[c, 0:1, :], qgain)
        grad_k = back(grad_k, kn[c], rad[c, 1:2, :], kgain)
        gp_ref[c] = jnp.concatenate([grad_q, grad_k, grad_v], axis=0).astype(BF)
        return 0

    lax.fori_loop(0, cams, finish, 0, unroll=4)

    out = pltpu.make_async_copy(gp_ref, gp_hbm, sem)
    out.start()
    acc[width:, :] = jnp.zeros_like(acc[width:, :])
    for s in range(0, cams, 4):
        four = range(s, s + 4)
        grads = jnp.concatenate([gp_ref[cameras[i]] for i in four], axis=1)
        atts = jnp.concatenate([at[cameras[i]] for i in four], axis=1)
        one = dot(grads, jnp.concatenate([hidden(i) for i in four], axis=0))
        two = dot(atts, jnp.concatenate([branch(i) for i in four], axis=0))
        acc[:width, :] = one if s == 0 else acc[:width, :] + one
        acc_out[...] = two if s == 0 else acc_out[...] + two
    turned = acc[...].T
    for b in range(features // dim):
        spread[b, :, :width] = turned[dim * b : dim * (b + 1), :width].astype(BF)
        spread[b, :, width:] = acc_out[:, dim * b : dim * (b + 1)].astype(BF)
    for k, ref in enumerate(sends):
        four = [spread[(near_bits(near(me) ^ k) + 2 * a) ^ vt].astype(F32) for a in range(4)]
        ref[...] = jnp.concatenate(four, axis=1).astype(BF)
    out.wait()


def heads(ids, w, wo, gains, arrays, slots, readies):
    dim = gains[0].shape[1]
    features = wo.shape[0]
    tokens = arrays[0].shape[0]
    cams = len(slots)
    vm = pl.BlockSpec(memory_space=pltpu.VMEM)
    sm = pl.BlockSpec(memory_space=pltpu.SMEM)

    def body(*refs):
        heads_kernel(slots, dim, features, cams, *refs)

    return pl.pallas_call(
        body,
        in_specs=[sm] + [vm] * (13 + len(arrays)),
        out_specs=[pl.BlockSpec(memory_space=pltpu.HBM)] + [vm] * 4,
        out_shape=[jax.ShapeDtypeStruct((cams, 3 * dim, tokens), BF)]
        + [jax.ShapeDtypeStruct((dim, 16 * dim), BF)] * 4,
        scratch_shapes=[
            pltpu.SemaphoreType.DMA,
            pltpu.VMEM((cams, 3 * dim, tokens), BF),
            pltpu.SMEM((cams, 2), jnp.int32),
            pltpu.VMEM((cams, dim, tokens), BF),
            pltpu.VMEM((cams, dim, tokens), F32),
            pltpu.VMEM((cams, dim, 3 * tokens), F32),
            pltpu.VMEM((cams, dim, 3 * tokens), F32),
            pltpu.VMEM((2 * LANES, features), F32),
            pltpu.VMEM((dim, features), F32),
            pltpu.VMEM((features // dim, dim, 4 * dim), BF),
        ]
        + [pltpu.VMEM(*shape) for shape in ready_shapes(cams, dim, tokens)],
        compiler_params=params(36),
        name="heads",
    )(ids, w, wo, *gains, *arrays, *readies)


def leave_kernel(x_ref, w_ref, tok_ref, cot_ref, mod_ref, out_ref, scr, acc):
    part = pl.program_id(0)
    heads, width, _ = x_ref.shape
    dim = width // 3

    @pl.when(part == 0)
    def _():
        for h in range(heads):
            x = x_ref[h].astype(F32)
            for p in range(3):
                scr[p, dim * h : dim * (h + 1), :] = x[dim * p : dim * (p + 1)]
        acc[...] = jnp.zeros_like(acc)

    acc[...] += dot(w_ref[...], scr[part].astype(BF))

    @pl.when(part == 2)
    def _():
        scaled = acc[...].T * (1.0 + line(mod_ref, 1))
        normed, inverse = normalise(tok_ref[...].astype(F32))
        mean = jnp.mean(scaled, axis=-1, keepdims=True)
        along = jnp.mean(scaled * normed, axis=-1, keepdims=True)
        grad = inverse * (scaled - mean - normed * along)
        out_ref[...] = (cot_ref[...].astype(F32) + grad).astype(BF)


def leave(x, w_qkv, tok, cot, mod):
    rows, features = tok.shape
    return pl.pallas_call(
        leave_kernel,
        grid=(3,),
        in_specs=[
            whole(x.shape),
            pl.BlockSpec((features, features), lambda p: (0, p)),
            whole(tok.shape),
            whole(cot.shape),
            whole(mod.shape),
        ],
        out_specs=whole(tok.shape),
        out_shape=jax.ShapeDtypeStruct(tok.shape, BF),
        scratch_shapes=[
            pltpu.VMEM((3, features, rows), F32),
            pltpu.VMEM((features, rows), F32),
        ],
        compiler_params=params(58),
        name="leave",
    )(x, w_qkv, tok, cot, mod)


def fold_kernel(id_ref, a_ref, b_ref, c_ref, d_ref, *refs):
    *outs, rest_ref, four, rest = refs
    dim, width = outs[0].shape
    total = a_ref[...].astype(F32) + b_ref[...].astype(F32) + c_ref[...].astype(F32) + d_ref[...].astype(F32)
    chunks = [total[:, (width + dim) * a : (width + dim) * (a + 1)] for a in range(4)]
    for a in range(4):
        four[a] = chunks[a][:, :width].astype(BF)
        rest[a] = chunks[a][:, width:]
    rest_ref[...] = jnp.concatenate([rest[far(id_ref[1]) ^ a] for a in range(4)], axis=1).astype(BF)
    for k in range(4):
        outs[k][...] = four[far(id_ref[0]) ^ k]


def fold(ids, parts):
    dim = parts[0].shape[0]
    width = 3 * dim
    vm = pl.BlockSpec(memory_space=pltpu.VMEM)
    shapes = [jax.ShapeDtypeStruct((dim, width), BF)] * 4 + [jax.ShapeDtypeStruct((dim, 4 * dim), BF)]
    return pl.pallas_call(
        fold_kernel,
        in_specs=[pl.BlockSpec(memory_space=pltpu.SMEM)] + [vm] * 4,
        out_specs=[vm] * 5,
        out_shape=shapes,
        scratch_shapes=[pltpu.VMEM((4, dim, width), BF), pltpu.VMEM((4, dim, dim), F32)],
        compiler_params=params(16),
        name="fold",
    )(ids, *parts)


def close_kernel(factor, a_ref, b_ref, c_ref, d_ref, rest_ref, out_ref):
    width = a_ref.shape[1]
    total = a_ref[...].astype(F32) + b_ref[...].astype(F32) + c_ref[...].astype(F32) + d_ref[...].astype(F32)
    both = jnp.concatenate([total * factor, rest_ref[...].astype(F32)], axis=1)
    out_ref[...] = both.astype(BF)


def close(parts, rest, factor):
    dim, width = parts[0].shape
    vm = pl.BlockSpec(memory_space=pltpu.VMEM)

    def body(*refs):
        close_kernel(factor, *refs)

    return pl.pallas_call(
        body,
        in_specs=[vm] * 5,
        out_specs=vm,
        out_shape=jax.ShapeDtypeStruct((dim, width + 4 * dim), BF),
        compiler_params=params(16),
        name="close",
    )(*parts, rest)


def join_kernel(factor, id_ref, a_ref, b_ref, c_ref, d_ref, out_ref, all_ref):
    dim = a_ref.shape[0]
    width = 3 * dim
    me = far(id_ref[2])
    four = [ref[...].astype(F32) for ref in (a_ref, b_ref, c_ref, d_ref)]
    rest = (four[0] + four[1] + four[2] + four[3])[:, width:] * factor
    for k in range(4):
        all_ref[me ^ k] = four[k][:, :width]
    pieces = []
    for a in range(4):
        pieces += [all_ref[a], rest[:, dim * a : dim * (a + 1)]]
    out_ref[...] = jnp.concatenate(pieces, axis=1).astype(BF)


def join(ids, parts, factor):
    dim = parts[0].shape[0]
    vm = pl.BlockSpec(memory_space=pltpu.VMEM)

    def body(*refs):
        join_kernel(factor, *refs)

    return pl.pallas_call(
        body,
        in_specs=[pl.BlockSpec(memory_space=pltpu.SMEM)] + [vm] * 4,
        out_specs=vm,
        out_shape=jax.ShapeDtypeStruct((dim, 16 * dim), BF),
        scratch_shapes=[pltpu.VMEM((4, dim, 3 * dim), F32)],
        compiler_params=params(16),
        name="join",
    )(ids, *parts)


def final_kernel(id_ref, a_ref, b_ref, c_ref, d_ref, in_ref, out_ref, all_ref):
    heads = 16
    dim, wide = a_ref.shape
    total = wide // 4
    me = id_ref[2]
    for k, ref in enumerate((a_ref, b_ref, c_ref, d_ref)):
        all_ref[k] = ref[...]
    lines = [all_ref[near(me) ^ k].astype(F32) for k in range(4)]
    blocks = [lines[near(h)][:, total * far(h) : total * (far(h) + 1)] for h in range(heads)]
    for p in range(4):
        part = jnp.concatenate([b[:, dim * p : dim * (p + 1)] for b in blocks], axis=1).astype(BF)
        if p < 3:
            in_ref[:, heads * dim * p : heads * dim * (p + 1)] = part
        else:
            out_ref[...] = part


def final(ids, parts):
    dim, wide = parts[0].shape
    vm = pl.BlockSpec(memory_space=pltpu.VMEM)
    return pl.pallas_call(
        final_kernel,
        in_specs=[pl.BlockSpec(memory_space=pltpu.SMEM)] + [vm] * 4,
        out_specs=[vm] * 2,
        out_shape=[
            jax.ShapeDtypeStruct((dim, 3 * wide), BF),
            jax.ShapeDtypeStruct((dim, wide), BF),
        ],
        scratch_shapes=[pltpu.VMEM((4, dim, wide), BF)],
        compiler_params=params(16),
        name="final",
    )(ids, *parts)


def swap(part, bits):
    return lax.ppermute(part, "dp", [(i, i ^ bits) for i in range(16)])


def cross(part, bits):
    pairs = [(16 * a + b, 16 * (a ^ bits) + (a ^ bits ^ b)) for a in range(16) for b in range(16)]
    return lax.ppermute(part, ("dp", "vt"), pairs)


def front(ids, tok, cot, mod, q_gain, k_gain, w_qkv, w_out, nb):
    features = tok.shape[-1]
    hb = enter(nb, tok, cot, mod)
    w, wo = weights(ids, w_qkv, w_out, q_gain.shape[0])
    gains = q_gain.reshape(1, -1), k_gain.reshape(1, -1)
    arrays, slots, readies, w, wo = gather(hb, features + LANES, w, wo, gains)
    return heads(ids, w, wo, gains, arrays, slots, readies)


def shards(tokens, cotangent, modulation, q_gain, k_gain, w_qkv, w_out, neighbours):
    rows, features = tokens.shape[-2:]
    factor = 1.0 / (lax.axis_size("dp") * lax.axis_size("vt"))
    me = lax.axis_index("dp")
    vt = lax.axis_index("vt")
    ids = jnp.stack([me, vt, me ^ vt])
    tok = tokens.reshape(rows, features)
    cot = cotangent.reshape(rows, features)
    mod = modulation.reshape(3, 1, features)
    ids, tok = lax.optimization_barrier((ids, tok))
    gp, *sent = front(ids, tok, cot, mod, q_gain, k_gain, w_qkv, w_out, neighbours.reshape(2))
    parts = [sent[0]] + [swap(sent[k], near_bits(k)) for k in (1, 2, 3)]
    *sums, rest = fold(ids, parts)
    sums = [cross(sums[k], 2 * k) for k in range(4)]
    gp, *sums = lax.optimization_barrier((gp, *sums))
    gp_mine = lax.all_to_all(gp, "vt", 0, 0)
    mine = close(sums, rest, factor)
    group = join(ids, [mine] + [swap(mine, 2 * k) for k in (1, 2, 3)], factor)
    gp_mine, group = lax.optimization_barrier((gp_mine, group))
    grad_in, grad_out = final(ids, [group] + [swap(group, near_bits(k)) for k in (1, 2, 3)])
    grad_tokens = leave(gp_mine, w_qkv, tok, cot, mod)
    return grad_tokens.reshape(tokens.shape), grad_in, grad_out


def solution(mesh):
    placed = (
        P("dp", "vt", None, None, None),
        P("dp", "vt", None, None, None),
        P("dp", "vt", None, None),
        P(),
        P(),
        P(),
        P(),
        P("dp", "vt", None),
    )
    return jax.shard_map(
        shards,
        mesh=mesh,
        in_specs=placed,
        out_specs=(P("dp", "vt", None, None, None), P("vt", None), P("vt", None)),
        check_vma=False,
    )
```

```python
import functools
import math

import jax
import jax.numpy as jnp
from jax import lax
from jax.experimental import pallas as pl
from jax.experimental.pallas import tpu as pltpu
from jax.sharding import PartitionSpec as P

BF = jnp.bfloat16
F32 = jnp.float32
EPS = 1e-06
NN = (((1,), (0,)), ((), ()))
NT = (((1,), (1,)), ((), ()))
MIB = 1024 * 1024
LANES = 128


def dot(a, b, dims=NN):
    return lax.dot_general(a, b, dims, preferred_element_type=F32)


def whole(shape):
    return pl.BlockSpec(shape, lambda *_: (0,) * len(shape))


def params(mib):
    return pltpu.CompilerParams(vmem_limit_bytes=mib * MIB)


def normalise(values):
    center = values - jnp.mean(values, axis=-1, keepdims=True)
    spread = jnp.mean(center * center, axis=-1, keepdims=True)
    inverse = lax.rsqrt(spread + EPS)
    return center * inverse, inverse


def line(mod_ref, i):
    return mod_ref[i]


def enter_kernel(nb_ref, tok_ref, cot_ref, mod_ref, out_ref):
    rows, features = tok_ref.shape
    normed, _ = normalise(tok_ref[...].astype(F32))
    hidden = normed * (1.0 + line(mod_ref, 1)) + line(mod_ref, 0)
    out_ref[:, :features] = hidden.astype(BF)
    lane = lax.broadcasted_iota(jnp.int32, (rows, LANES), 1)
    marks = jnp.where(lane == 0, nb_ref[0].astype(F32), nb_ref[1].astype(F32))
    out_ref[:, features : features + LANES] = marks.astype(BF)
    out_ref[:, features + LANES :] = (line(mod_ref, 2) * cot_ref[...].astype(F32)).astype(BF)


def enter(nb, tok, cot, mod):
    rows, features = tok.shape
    vm = pl.BlockSpec(memory_space=pltpu.VMEM)
    return pl.pallas_call(
        enter_kernel,
        in_specs=[pl.BlockSpec(memory_space=pltpu.SMEM), vm, vm, vm],
        out_specs=vm,
        out_shape=jax.ShapeDtypeStruct((rows, 2 * features + LANES), BF),
        compiler_params=params(58),
        name="enter",
    )(nb, tok, cot, mod)


def weights_kernel(id_ref, w_hbm, wo_hbm, w_ref, wo_ref, win, wo_win, sem):
    features, wide = w_ref.shape
    dim = wo_win.shape[0] - 8
    head = id_ref[1]
    copies = []
    gaps = []
    for p in range(3):
        first = features * p + dim * head
        start = jnp.minimum(first // LANES * LANES, 3 * features - wide)
        gaps.append(first - start)
        window = w_hbm.at[:, pl.ds(pl.multiple_of(start, LANES), wide)]
        copies.append(pltpu.make_async_copy(window, win.at[p], sem.at[p]))
    first = dim * head
    start = first // 16 * 16
    window = wo_hbm.at[pl.ds(pl.multiple_of(start, 16), wo_win.shape[0])]
    copies.append(pltpu.make_async_copy(window, wo_win, sem.at[3]))
    for copy in copies:
        copy.start()
    row = lax.broadcasted_iota(jnp.int32, (wide, wide), 0)
    column = lax.broadcasted_iota(jnp.int32, (wide, wide), 1)
    total = jnp.zeros((features, wide), F32)
    for p in range(3):
        inside = (column >= dim * p) & (column < dim * (p + 1))
        pick = jnp.where(inside & (row == column - dim * p + gaps[p]), 1.0, 0.0).astype(BF)
        copies[p].wait()
        total = total + dot(win[p], pick)
    w_ref[...] = total.astype(BF)
    row = lax.broadcasted_iota(jnp.int32, (LANES, dim + 8), 0)
    column = lax.broadcasted_iota(jnp.int32, (LANES, dim + 8), 1)
    pick = jnp.where((row < dim) & (column == row + (first - start)), 1.0, 0.0).astype(BF)
    copies[3].wait()
    wo_ref[...] = dot(pick, wo_win[...]).T.astype(BF)


def weights(ids, w_qkv, w_out, dim):
    features = w_out.shape[0]
    wide = 2 * LANES
    vm = pl.BlockSpec(memory_space=pltpu.VMEM)
    hbm = pl.BlockSpec(memory_space=pltpu.HBM)
    return pl.pallas_call(
        weights_kernel,
        in_specs=[pl.BlockSpec(memory_space=pltpu.SMEM), hbm, hbm],
        out_specs=[vm, vm],
        out_shape=[
            jax.ShapeDtypeStruct((features, wide), BF),
            jax.ShapeDtypeStruct((features, LANES), BF),
        ],
        scratch_shapes=[
            pltpu.VMEM((3, features, wide), BF),
            pltpu.VMEM((dim + 8, features), BF),
            pltpu.SemaphoreType.DMA((4,)),
        ],
        compiler_params=params(52),
        name="weights",
    )(ids, w_qkv, w_out)


def place(y, x, core):
    return (y * 4 + x) * 2 + core


def move(part, dy, dx, dc):
    pairs = [
        (place(y, x, c), place(y ^ dy, (x + dx) % 4, c ^ dc)) for y in range(2) for x in range(4) for c in range(2)
    ]
    return lax.ppermute(part, "vt", pairs)


def mix_kernel(a_ref, b_ref, c_ref, up_ref, down_ref, over_ref, all_ref):
    wide = a_ref.shape[1]
    half = down_ref.shape[1] // 2
    first = wide - half
    for i, ref in enumerate((a_ref, b_ref, c_ref)):
        all_ref[:, wide * i : wide * (i + 1)] = ref[...]
    up_ref[:, :first] = a_ref[:, :first]
    up_ref[:, first:] = c_ref[:, :first]
    down_ref[:, :half] = b_ref[:, first:]
    down_ref[:, half:] = c_ref[:, first:]
    over_ref[:, :half] = a_ref[:, first:]
    over_ref[:, half:] = b_ref[:, :first]


def mix(a, b, c, first):
    rows, wide = a.shape
    half = wide - first
    return pl.pallas_call(
        mix_kernel,
        out_shape=[
            jax.ShapeDtypeStruct((rows, 2 * first), BF),
            jax.ShapeDtypeStruct((rows, 2 * half), BF),
            jax.ShapeDtypeStruct((rows, wide), BF),
            jax.ShapeDtypeStruct((rows, 3 * wide), BF),
        ],
        compiler_params=params(16),
        name="mix",
    )(a, b, c)


def gather(hb, first, w, wo, gains):
    half = hb.shape[1] - first
    low = move(hb, 0, 1, 0)
    high = move(hb, 0, -1, 0)
    side = move(hb, 1, 0, 0)
    twin = move(hb, 0, 0, 1)
    low, high, side, twin, w, wo = lax.optimization_barrier((low, high, side, twin, w, wo))
    up, down, over, three = mix(low, high, side, first)
    up, down, over, three = move(up, 0, 1, 0), move(down, 0, -1, 0), move(over, 1, 0, 0), move(three, 0, 0, 1)
    wide = hb.shape[1]
    slots = []
    for dc in range(2):
        near_four = [(4, 0), (5, 0), (5, wide), (5, 2 * wide)] if dc else [(n, 0) for n in range(4)]
        for at, (n, lane) in zip(((0, 0), (0, 3), (0, 1), (1, 0)), near_four):
            slots.append((at + (dc,), (n, lane), (n, lane + first)))
        n = 6 + 5 * dc
        slots += [
            ((0, 2, dc), (n, 0), (n + 1, 0)),
            ((1, 3, dc), (n, first), (n + 2, 0)),
            ((1, 1, dc), (n + 2, half), (n + 1, half)),
            ((1, 2, dc), (n + 3, 0), (n + 4, 0)),
        ]
    soon = [hb, low, high, side, twin, three]
    readies = early(w, wo, gains, soon, slots)
    up, down, *readies = lax.optimization_barrier((up, down, *readies))
    far_up = move(up[:, first:], 0, 1, 0)
    far_down = move(down[:, half:], 0, -1, 0)
    late = [up, down, over, far_up, far_down]
    arrays = soon + late + [move(a, 0, 0, 1) for a in late]
    return arrays, slots, readies, w, wo


def near(i):
    return i % 2 + 2 * (i // 8)


def far(i):
    return (i // 2) % 4


def near_bits(k):
    return k % 2 + 8 * (k // 2)


EARLY = (0, 1, 2, 3, 8, 9, 10, 11)


def column(ref, tokens):
    dim = ref.shape[1]
    row = jnp.concatenate([ref[...], jnp.zeros((1, tokens - dim), F32)], axis=1)
    return jnp.broadcast_to(row, (tokens, tokens)).T[:dim]


def ready_shapes(count, dim, tokens):
    thin, square = (count, dim, tokens), (count, tokens, tokens)
    shapes = [thin, thin, (count, 8, tokens), square, thin, thin, square, square, square]
    return [(shape, F32 if i < 3 else BF) for i, shape in enumerate(shapes)]


def ready_kernel(picked, places, hidden, branch, w_ref, wo_ref, qgain, kgain, stores):
    qn, kn, rad, qh, kh, vh, gh, krow, vrow = stores
    dim, tokens = qgain.shape
    pad = jnp.zeros((tokens - dim, tokens), F32)
    for i, c in enumerate(places):
        if i % 4 == 0:
            four = picked[i : i + 4]
            project = dot(jnp.concatenate([hidden(s) for s in four], axis=0), w_ref[...])
            back_out = dot(jnp.concatenate([branch(s) for s in four], axis=0), wo_ref[...])
        rows = slice(tokens * (i % 4), tokens * (i % 4 + 1))
        turned = project[rows].T
        q, k, v = (turned[dim * n : dim * (n + 1)] for n in range(3))
        rq = lax.rsqrt(jnp.mean(q * q, axis=0, keepdims=True) + EPS)
        rk = lax.rsqrt(jnp.mean(k * k, axis=0, keepdims=True) + EPS)
        q = q * rq
        k = k * rk
        qn[c] = q
        kn[c] = k
        rad[c] = jnp.concatenate([rq, rk, jnp.zeros((6, tokens), F32)], axis=0)
        q = q * qgain
        k = k * kgain
        qh[c] = jnp.concatenate([q, pad], axis=0).astype(BF)
        gh[c] = back_out[rows].T.astype(BF)
        kh[c] = k.astype(BF)
        vh[c] = v.astype(BF)
        krow[c] = jnp.concatenate([k, pad], axis=0).T.astype(BF)
        vrow[c] = jnp.concatenate([v, pad], axis=0).T.astype(BF)


def early_kernel(slots, features, w_ref, wo_ref, qg_ref, kg_ref, *refs):
    arrays, stores = refs[:-9], refs[-9:]
    tokens = arrays[0].shape[0]

    def hidden(s):
        n, lane = slots[s][1]
        return arrays[n][:, lane : lane + features]

    def branch(s):
        n, lane = slots[s][2]
        return arrays[n][:, lane : lane + features]

    gains = column(qg_ref, tokens), column(kg_ref, tokens)
    ready_kernel(EARLY, range(len(EARLY)), hidden, branch, w_ref, wo_ref, *gains, stores)


def early(w, wo, gains, arrays, slots):
    features = wo.shape[0]
    dim = gains[0].shape[1]
    tokens = arrays[0].shape[0]
    vm = pl.BlockSpec(memory_space=pltpu.VMEM)

    def body(*refs):
        early_kernel(slots, features, *refs)

    return pl.pallas_call(
        body,
        in_specs=[vm] * (4 + len(arrays)),
        out_specs=[vm] * 9,
        out_shape=[jax.ShapeDtypeStruct(*shape) for shape in ready_shapes(len(EARLY), dim, tokens)],
        compiler_params=params(24),
        name="early",
    )(w, wo, *gains, *arrays)


def heads_kernel(slots, dim, features, cams, id_ref, w_ref, wo_ref, qg_ref, kg_ref, *refs):
    count = len({n for _, *pairs in slots for n, _ in pairs})
    arrays, refs = refs[:count], refs[count:]
    readies, refs = refs[:9], refs[9:]
    gp_hbm, *sends, sem, gp_ref, nb, at, gq, gk, gv, acc, acc_out, spread = refs[:-9]
    stores = refs[-9:]
    qn, kn, rad, qh, kh, vh, gh, krow, vrow = stores
    tokens = arrays[0].shape[0]
    width = 3 * dim
    scale = 1.0 / math.sqrt(dim)
    qgain, kgain = column(qg_ref, tokens), column(kg_ref, tokens)
    me, vt = id_ref[0], id_ref[1]
    y, x, core = vt // 8, vt // 2 % 4, vt % 2
    cameras = [place((y + dy) % 2, (x + dx) % 4, (core + dc) % 2) for (dy, dx, dc), _, _ in slots]

    def hidden(s):
        n, lane = slots[s][1]
        return arrays[n][:, lane : lane + features]

    def branch(s):
        n, lane = slots[s][2]
        return arrays[n][:, lane : lane + features]

    for s, c in enumerate(cameras):
        n, lane = slots[s][1]
        marks = arrays[n][:16, lane + features : lane + features + LANES].astype(F32)
        nb[c, 0] = marks[0, 0].astype(jnp.int32)
        nb[c, 1] = marks[0, 1].astype(jnp.int32)
    for e, s in enumerate(EARLY):
        for ref, ready in zip(stores, readies):
            ref[cameras[s]] = ready[e]
    late = [s for s in range(cams) if s not in EARLY]
    ready_kernel(late, [cameras[s] for s in late], hidden, branch, w_ref, wo_ref, qgain, kgain, stores)

    def camera(c, _):
        left = nb[c, 0]
        right = nb[c, 1]
        q = qh[c]
        g = gh[c]
        keys = jnp.concatenate([krow[left], krow[c], krow[right]], axis=0)
        values = jnp.concatenate([vrow[left], vrow[c], vrow[right]], axis=0)
        keys_t = jnp.concatenate([kh[left], kh[c], kh[right]], axis=1)
        values_t = jnp.concatenate([vh[left], vh[c], vh[right]], axis=1)
        e = jnp.exp(dot(keys, q) * scale)
        probs = e * (1.0 / jnp.sum(e, axis=0, keepdims=True))
        low = probs.astype(BF)
        gprobs = dot(values, g)
        centre = jnp.sum(probs * gprobs, axis=0, keepdims=True)
        gs = (probs * (gprobs - centre) * scale).astype(BF)
        at[c] = dot(values_t, low).astype(BF)
        gq[c] = dot(keys_t, gs)
        gk[c] = dot(q, gs, NT)[:dim]
        gv[c] = dot(g, low, NT)[:dim]
        return 0

    lax.fori_loop(0, cams, camera, 0, unroll=16)

    def back(grad, unit, radius, gain):
        shaped = grad * gain
        return (shaped - unit * jnp.mean(shaped * unit, axis=0, keepdims=True)) * radius

    def finish(c, _):
        left = nb[c, 0]
        right = nb[c, 1]
        grad_k = gk[c, :, tokens : 2 * tokens] + gk[left, :, 2 * tokens :] + gk[right, :, :tokens]
        grad_v = gv[c, :, tokens : 2 * tokens] + gv[left, :, 2 * tokens :] + gv[right, :, :tokens]
        grad_q = back(gq[c], qn[c], rad[c, 0:1, :], qgain)
        grad_k = back(grad_k, kn[c], rad[c, 1:2, :], kgain)
        gp_ref[c] = jnp.concatenate([grad_q, grad_k, grad_v], axis=0).astype(BF)
        return 0

    lax.fori_loop(0, cams, finish, 0, unroll=8)

    out = pltpu.make_async_copy(gp_ref, gp_hbm, sem)
    out.start()
    acc[width:, :] = jnp.zeros_like(acc[width:, :])
    for s in range(0, cams, 4):
        four = range(s, s + 4)
        grads = jnp.concatenate([gp_ref[cameras[i]] for i in four], axis=1)
        atts = jnp.concatenate([at[cameras[i]] for i in four], axis=1)
        one = dot(grads, jnp.concatenate([hidden(i) for i in four], axis=0))
        two = dot(atts, jnp.concatenate([branch(i) for i in four], axis=0))
        acc[:width, :] = one if s == 0 else acc[:width, :] + one
        acc_out[...] = two if s == 0 else acc_out[...] + two
    turned = acc[...].T
    for b in range(features // dim):
        spread[b, :, :width] = turned[dim * b : dim * (b + 1), :width].astype(BF)
        spread[b, :, width:] = acc_out[:, dim * b : dim * (b + 1)].astype(BF)
    for k, ref in enumerate(sends):
        four = [spread[(near_bits(near(me) ^ k) + 2 * a) ^ vt].astype(F32) for a in range(4)]
        ref[...] = jnp.concatenate(four, axis=1).astype(BF)
    out.wait()


def heads(ids, w, wo, gains, arrays, slots, readies):
    dim = gains[0].shape[1]
    features = wo.shape[0]
    tokens = arrays[0].shape[0]
    cams = len(slots)
    vm = pl.BlockSpec(memory_space=pltpu.VMEM)
    sm = pl.BlockSpec(memory_space=pltpu.SMEM)

    def body(*refs):
        heads_kernel(slots, dim, features, cams, *refs)

    return pl.pallas_call(
        body,
        in_specs=[sm] + [vm] * (13 + len(arrays)),
        out_specs=[pl.BlockSpec(memory_space=pltpu.HBM)] + [vm] * 4,
        out_shape=[jax.ShapeDtypeStruct((cams, 3 * dim, tokens), BF)]
        + [jax.ShapeDtypeStruct((dim, 16 * dim), BF)] * 4,
        scratch_shapes=[
            pltpu.SemaphoreType.DMA,
            pltpu.VMEM((cams, 3 * dim, tokens), BF),
            pltpu.SMEM((cams, 2), jnp.int32),
            pltpu.VMEM((cams, dim, tokens), BF),
            pltpu.VMEM((cams, dim, tokens), F32),
            pltpu.VMEM((cams, dim, 3 * tokens), F32),
            pltpu.VMEM((cams, dim, 3 * tokens), F32),
            pltpu.VMEM((2 * LANES, features), F32),
            pltpu.VMEM((dim, features), F32),
            pltpu.VMEM((features // dim, dim, 4 * dim), BF),
        ]
        + [pltpu.VMEM(*shape) for shape in ready_shapes(cams, dim, tokens)],
        compiler_params=params(36),
        name="heads",
    )(ids, w, wo, *gains, *arrays, *readies)


def leave_kernel(x_ref, w_ref, tok_ref, cot_ref, mod_ref, out_ref, scr, acc):
    part = pl.program_id(0)
    heads, width, _ = x_ref.shape
    dim = width // 3

    @pl.when(part == 0)
    def _():
        for h in range(heads):
            x = x_ref[h].astype(F32)
            for p in range(3):
                scr[p, dim * h : dim * (h + 1), :] = x[dim * p : dim * (p + 1)]
        acc[...] = jnp.zeros_like(acc)

    acc[...] += dot(w_ref[...], scr[part].astype(BF))

    @pl.when(part == 2)
    def _():
        scaled = acc[...].T * (1.0 + line(mod_ref, 1))
        normed, inverse = normalise(tok_ref[...].astype(F32))
        mean = jnp.mean(scaled, axis=-1, keepdims=True)
        along = jnp.mean(scaled * normed, axis=-1, keepdims=True)
        grad = inverse * (scaled - mean - normed * along)
        out_ref[...] = (cot_ref[...].astype(F32) + grad).astype(BF)


def leave(x, w_qkv, tok, cot, mod):
    rows, features = tok.shape
    return pl.pallas_call(
        leave_kernel,
        grid=(3,),
        in_specs=[
            whole(x.shape),
            pl.BlockSpec((features, features), lambda p: (0, p)),
            whole(tok.shape),
            whole(cot.shape),
            whole(mod.shape),
        ],
        out_specs=whole(tok.shape),
        out_shape=jax.ShapeDtypeStruct(tok.shape, BF),
        scratch_shapes=[
            pltpu.VMEM((3, features, rows), F32),
            pltpu.VMEM((features, rows), F32),
        ],
        compiler_params=params(58),
        name="leave",
    )(x, w_qkv, tok, cot, mod)


def fold_kernel(id_ref, a_ref, b_ref, c_ref, d_ref, send_ref, keep_ref, four, rest):
    dim, width = four.shape[1:]
    total = a_ref[...].astype(F32) + b_ref[...].astype(F32) + c_ref[...].astype(F32) + d_ref[...].astype(F32)
    for a in range(4):
        chunk = total[:, (width + dim) * a : (width + dim) * (a + 1)]
        four[a] = chunk[:, :width]
        rest[a] = chunk[:, width:]
    tail = [rest[far(id_ref[1]) ^ a] for a in range(4)]
    me = far(id_ref[0])
    send_ref[...] = jnp.concatenate([four[me ^ 1], four[me ^ 2]] + tail, axis=1).astype(BF)
    keep_ref[...] = jnp.concatenate([four[me], four[me ^ 3]] + tail, axis=1).astype(BF)


def fold(ids, parts):
    dim = parts[0].shape[0]
    vm = pl.BlockSpec(memory_space=pltpu.VMEM)
    return pl.pallas_call(
        fold_kernel,
        in_specs=[pl.BlockSpec(memory_space=pltpu.SMEM)] + [vm] * 4,
        out_specs=[vm] * 2,
        out_shape=[jax.ShapeDtypeStruct((dim, 10 * dim), BF)] * 2,
        scratch_shapes=[pltpu.VMEM((4, dim, 3 * dim), F32), pltpu.VMEM((4, dim, dim), F32)],
        compiler_params=params(16),
        name="fold",
    )(ids, *parts)


def halve_kernel(a_ref, b_ref, own_ref, other_ref, rest_ref):
    width = own_ref.shape[1]
    total = a_ref[...].astype(F32) + b_ref[...].astype(F32)
    own_ref[...] = total[:, :width].astype(BF)
    other_ref[...] = total[:, width : 2 * width].astype(BF)
    rest_ref[...] = total[:, 2 * width :].astype(BF)


def close_kernel(factor, a_ref, b_ref, rest_ref, out_ref):
    total = (a_ref[...].astype(F32) + b_ref[...].astype(F32)) * factor
    out_ref[...] = jnp.concatenate([total, rest_ref[...].astype(F32)], axis=1).astype(BF)


def pair_kernel(factor, a_ref, b_ref, pair_ref, rest_ref):
    width = pair_ref.shape[1] // 2
    a, b = a_ref[...].astype(F32), b_ref[...].astype(F32)
    pair_ref[...] = jnp.concatenate([a[:, :width], b[:, :width]], axis=1).astype(BF)
    rest_ref[...] = ((a[:, width:] + b[:, width:]) * factor).astype(BF)


def join_kernel(id_ref, a_ref, b_ref, rest_ref, out_ref, all_ref):
    dim = a_ref.shape[0]
    width = 3 * dim
    me = far(id_ref[2])
    a, b = a_ref[...].astype(F32), b_ref[...].astype(F32)
    all_ref[me] = a[:, :width]
    all_ref[me ^ 3] = a[:, width:]
    all_ref[me ^ 1] = b[:, :width]
    all_ref[me ^ 2] = b[:, width:]
    rest = rest_ref[...].astype(F32)
    pieces = []
    for i in range(4):
        pieces += [all_ref[i], rest[:, dim * i : dim * (i + 1)]]
    out_ref[...] = jnp.concatenate(pieces, axis=1).astype(BF)


def small(body, name, parts, widths, ids=None, scratch=()):
    dim = parts[0].shape[0]
    vm = pl.BlockSpec(memory_space=pltpu.VMEM)
    first = [] if ids is None else [pl.BlockSpec(memory_space=pltpu.SMEM)]
    return pl.pallas_call(
        body,
        in_specs=first + [vm] * len(parts),
        out_specs=[vm] * len(widths),
        out_shape=[jax.ShapeDtypeStruct((dim, width), BF) for width in widths],
        scratch_shapes=list(scratch),
        compiler_params=params(16),
        name=name,
    )(*([] if ids is None else [ids]), *parts)


def final_kernel(id_ref, a_ref, b_ref, c_ref, d_ref, in_ref, out_ref, all_ref):
    heads = 16
    dim, wide = a_ref.shape
    total = wide // 4
    me = id_ref[2]
    for k, ref in enumerate((a_ref, b_ref, c_ref, d_ref)):
        all_ref[k] = ref[...]
    lines = [all_ref[near(me) ^ k].astype(F32) for k in range(4)]
    blocks = [lines[near(h)][:, total * far(h) : total * (far(h) + 1)] for h in range(heads)]
    for p in range(4):
        part = jnp.concatenate([b[:, dim * p : dim * (p + 1)] for b in blocks], axis=1).astype(BF)
        if p < 3:
            in_ref[:, heads * dim * p : heads * dim * (p + 1)] = part
        else:
            out_ref[...] = part


def final(ids, parts):
    dim, wide = parts[0].shape
    vm = pl.BlockSpec(memory_space=pltpu.VMEM)
    return pl.pallas_call(
        final_kernel,
        in_specs=[pl.BlockSpec(memory_space=pltpu.SMEM)] + [vm] * 4,
        out_specs=[vm] * 2,
        out_shape=[
            jax.ShapeDtypeStruct((dim, 3 * wide), BF),
            jax.ShapeDtypeStruct((dim, wide), BF),
        ],
        scratch_shapes=[pltpu.VMEM((4, dim, wide), BF)],
        compiler_params=params(16),
        name="final",
    )(ids, *parts)


def swap(part, bits):
    return lax.ppermute(part, "dp", [(i, i ^ bits) for i in range(16)])


def cross(part, bits):
    pairs = [(16 * a + b, 16 * (a ^ bits) + (a ^ bits ^ b)) for a in range(16) for b in range(16)]
    return lax.ppermute(part, ("dp", "vt"), pairs)


def front(ids, tok, cot, mod, q_gain, k_gain, w_qkv, w_out, nb):
    features = tok.shape[-1]
    hb = enter(nb, tok, cot, mod)
    w, wo = weights(ids, w_qkv, w_out, q_gain.shape[0])
    gains = q_gain.reshape(1, -1), k_gain.reshape(1, -1)
    arrays, slots, readies, w, wo = gather(hb, features + LANES, w, wo, gains)
    return heads(ids, w, wo, gains, arrays, slots, readies)


def shards(tokens, cotangent, modulation, q_gain, k_gain, w_qkv, w_out, neighbours):
    rows, features = tokens.shape[-2:]
    factor = 1.0 / (lax.axis_size("dp") * lax.axis_size("vt"))
    me = lax.axis_index("dp")
    vt = lax.axis_index("vt")
    ids = jnp.stack([me, vt, me ^ vt])
    tok = tokens.reshape(rows, features)
    cot = cotangent.reshape(rows, features)
    mod = modulation.reshape(3, 1, features)
    ids, tok = lax.optimization_barrier((ids, tok))
    gp, *sent = front(ids, tok, cot, mod, q_gain, k_gain, w_qkv, w_out, neighbours.reshape(2))
    parts = [sent[0]] + [swap(sent[k], near_bits(k)) for k in (1, 2, 3)]
    dim = q_gain.shape[0]
    send, keep = fold(ids, parts)
    own, other, rest = small(halve_kernel, "halve", [keep, swap(send, 2)], [3 * dim, 3 * dim, 4 * dim])
    own, other = cross(own, 0), cross(other, 6)
    gp, own, other = lax.optimization_barrier((gp, own, other))
    gp_mine = lax.all_to_all(gp, "vt", 0, 0)
    (mine,) = small(functools.partial(close_kernel, factor), "close", [own, other, rest], [7 * dim])
    pair, rest = small(functools.partial(pair_kernel, factor), "pair", [mine, swap(mine, 6)], [6 * dim, 4 * dim])
    scratch = [pltpu.VMEM((4, dim, 3 * dim), F32)]
    (group,) = small(join_kernel, "join", [pair, swap(pair, 2), rest], [16 * dim], ids, scratch)
    gp_mine, group = lax.optimization_barrier((gp_mine, group))
    grad_in, grad_out = final(ids, [group] + [swap(group, near_bits(k)) for k in (1, 2, 3)])
    grad_tokens = leave(gp_mine, w_qkv, tok, cot, mod)
    return grad_tokens.reshape(tokens.shape), grad_in, grad_out


def solution(mesh):
    placed = (
        P("dp", "vt", None, None, None),
        P("dp", "vt", None, None, None),
        P("dp", "vt", None, None),
        P(),
        P(),
        P(),
        P(),
        P("dp", "vt", None),
    )
    return jax.shard_map(
        shards,
        mesh=mesh,
        in_specs=placed,
        out_specs=(P("dp", "vt", None, None, None), P("vt", None), P("vt", None)),
        check_vma=False,
    )
```

```python
import functools
import math

import jax
import jax.numpy as jnp
from jax import lax
from jax.experimental import pallas as pl
from jax.experimental.pallas import tpu as pltpu
from jax.sharding import PartitionSpec as P

BF = jnp.bfloat16
F32 = jnp.float32
EPS = 1e-06
NN = (((1,), (0,)), ((), ()))
NT = (((1,), (1,)), ((), ()))
MIB = 1024 * 1024
LANES = 128


def dot(a, b, dims=NN):
    return lax.dot_general(a, b, dims, preferred_element_type=F32)


def whole(shape):
    return pl.BlockSpec(shape, lambda *_: (0,) * len(shape))


def params(mib):
    return pltpu.CompilerParams(vmem_limit_bytes=mib * MIB)


def normalise(values):
    center = values - jnp.mean(values, axis=-1, keepdims=True)
    spread = jnp.mean(center * center, axis=-1, keepdims=True)
    inverse = lax.rsqrt(spread + EPS)
    return center * inverse, inverse


def line(mod_ref, i):
    return mod_ref[i]


def enter_kernel(nb_ref, tok_ref, cot_ref, mod_ref, out_ref):
    rows, features = tok_ref.shape
    normed, _ = normalise(tok_ref[...].astype(F32))
    hidden = normed * (1.0 + line(mod_ref, 1)) + line(mod_ref, 0)
    out_ref[:, :features] = hidden.astype(BF)
    lane = lax.broadcasted_iota(jnp.int32, (rows, LANES), 1)
    marks = jnp.where(lane == 0, nb_ref[0].astype(F32), nb_ref[1].astype(F32))
    out_ref[:, features : features + LANES] = marks.astype(BF)
    out_ref[:, features + LANES :] = (line(mod_ref, 2) * cot_ref[...].astype(F32)).astype(BF)


def enter(nb, tok, cot, mod):
    rows, features = tok.shape

    def half(wide):
        return pl.BlockSpec((rows // 2, wide), lambda i: (i, 0))

    return pl.pallas_call(
        enter_kernel,
        grid=(2,),
        in_specs=[pl.BlockSpec(memory_space=pltpu.SMEM), half(features), half(features), whole(mod.shape)],
        out_specs=half(2 * features + LANES),
        out_shape=jax.ShapeDtypeStruct((rows, 2 * features + LANES), BF),
        compiler_params=params(58),
        name="enter",
    )(nb, tok, cot, mod)


def weights_kernel(id_ref, w_hbm, wo_hbm, w_ref, wo_ref, win, wo_win, sem):
    features, wide = w_ref.shape
    dim = wo_win.shape[0] - 8
    head = id_ref[1]
    copies = []
    gaps = []
    for p in range(3):
        first = features * p + dim * head
        start = jnp.minimum(first // LANES * LANES, 3 * features - wide)
        gaps.append(first - start)
        window = w_hbm.at[:, pl.ds(pl.multiple_of(start, LANES), wide)]
        copies.append(pltpu.make_async_copy(window, win.at[p], sem.at[p]))
    first = dim * head
    start = first // 16 * 16
    window = wo_hbm.at[pl.ds(pl.multiple_of(start, 16), wo_win.shape[0])]
    copies.append(pltpu.make_async_copy(window, wo_win, sem.at[3]))
    for copy in copies:
        copy.start()
    row = lax.broadcasted_iota(jnp.int32, (wide, wide), 0)
    column = lax.broadcasted_iota(jnp.int32, (wide, wide), 1)
    total = jnp.zeros((features, wide), F32)
    for p in range(3):
        inside = (column >= dim * p) & (column < dim * (p + 1))
        pick = jnp.where(inside & (row == column - dim * p + gaps[p]), 1.0, 0.0).astype(BF)
        copies[p].wait()
        total = total + dot(win[p], pick)
    w_ref[...] = total.astype(BF)
    row = lax.broadcasted_iota(jnp.int32, (LANES, dim + 8), 0)
    column = lax.broadcasted_iota(jnp.int32, (LANES, dim + 8), 1)
    pick = jnp.where((row < dim) & (column == row + (first - start)), 1.0, 0.0).astype(BF)
    copies[3].wait()
    wo_ref[...] = dot(pick, wo_win[...]).T.astype(BF)


def weights(ids, w_qkv, w_out, dim):
    features = w_out.shape[0]
    wide = 2 * LANES
    vm = pl.BlockSpec(memory_space=pltpu.VMEM)
    hbm = pl.BlockSpec(memory_space=pltpu.HBM)
    return pl.pallas_call(
        weights_kernel,
        in_specs=[pl.BlockSpec(memory_space=pltpu.SMEM), hbm, hbm],
        out_specs=[vm, vm],
        out_shape=[
            jax.ShapeDtypeStruct((features, wide), BF),
            jax.ShapeDtypeStruct((features, LANES), BF),
        ],
        scratch_shapes=[
            pltpu.VMEM((3, features, wide), BF),
            pltpu.VMEM((dim + 8, features), BF),
            pltpu.SemaphoreType.DMA((4,)),
        ],
        compiler_params=params(52),
        name="weights",
    )(ids, w_qkv, w_out)


def place(y, x, core):
    return (y * 4 + x) * 2 + core


def move(part, dy, dx, dc):
    pairs = [
        (place(y, x, c), place(y ^ dy, (x + dx) % 4, c ^ dc)) for y in range(2) for x in range(4) for c in range(2)
    ]
    return lax.ppermute(part, "vt", pairs)


def mix_kernel(a_ref, b_ref, c_ref, up_ref, down_ref, over_ref, all_ref):
    wide = a_ref.shape[1]
    half = down_ref.shape[1] // 2
    first = wide - half
    for i, ref in enumerate((a_ref, b_ref, c_ref)):
        all_ref[:, wide * i : wide * (i + 1)] = ref[...]
    up_ref[:, :first] = a_ref[:, :first]
    up_ref[:, first:] = c_ref[:, :first]
    down_ref[:, :half] = b_ref[:, first:]
    down_ref[:, half:] = c_ref[:, first:]
    over_ref[:, :half] = a_ref[:, first:]
    over_ref[:, half:] = b_ref[:, :first]


def mix(a, b, c, first):
    rows, wide = a.shape
    half = wide - first
    return pl.pallas_call(
        mix_kernel,
        out_shape=[
            jax.ShapeDtypeStruct((rows, 2 * first), BF),
            jax.ShapeDtypeStruct((rows, 2 * half), BF),
            jax.ShapeDtypeStruct((rows, wide), BF),
            jax.ShapeDtypeStruct((rows, 3 * wide), BF),
        ],
        compiler_params=params(16),
        name="mix",
    )(a, b, c)


def gather(hb, first, w, wo, gains):
    half = hb.shape[1] - first
    low = move(hb, 0, 1, 0)
    high = move(hb, 0, -1, 0)
    side = move(hb, 1, 0, 0)
    twin = move(hb, 0, 0, 1)
    low, high, side, twin, w, wo = lax.optimization_barrier((low, high, side, twin, w, wo))
    up, down, over, three = mix(low, high, side, first)
    up, down, over, three = move(up, 0, 1, 0), move(down, 0, -1, 0), move(over, 1, 0, 0), move(three, 0, 0, 1)
    wide = hb.shape[1]
    slots = []
    for dc in range(2):
        near_four = [(4, 0), (5, 0), (5, wide), (5, 2 * wide)] if dc else [(n, 0) for n in range(4)]
        for at, (n, lane) in zip(((0, 0), (0, 3), (0, 1), (1, 0)), near_four):
            slots.append((at + (dc,), (n, lane), (n, lane + first)))
        n = 6 + 5 * dc
        slots += [
            ((0, 2, dc), (n, 0), (n + 1, 0)),
            ((1, 3, dc), (n, first), (n + 2, 0)),
            ((1, 1, dc), (n + 2, half), (n + 1, half)),
            ((1, 2, dc), (n + 3, 0), (n + 4, 0)),
        ]
    soon = [hb, low, high, side, twin, three]
    readies = early(w, wo, gains, soon, slots)
    up, down, *readies = lax.optimization_barrier((up, down, *readies))
    far_up = move(up[:, first:], 0, 1, 0)
    far_down = move(down[:, half:], 0, -1, 0)
    late = [up, down, over, far_up, far_down]
    arrays = soon + late + [move(a, 0, 0, 1) for a in late]
    return arrays, slots, readies, w, wo


def near(i):
    return i % 2 + 2 * (i // 8)


def far(i):
    return (i // 2) % 4


def near_bits(k):
    return k % 2 + 8 * (k // 2)


EARLY = (0, 1, 2, 3, 8, 9, 10, 11)


def column(ref, tokens):
    dim = ref.shape[1]
    row = jnp.concatenate([ref[...], jnp.zeros((1, tokens - dim), F32)], axis=1)
    return jnp.broadcast_to(row, (tokens, tokens)).T[:dim]


def ready_shapes(count, dim, tokens):
    thin, square = (count, dim, tokens), (count, tokens, tokens)
    shapes = [thin, thin, (count, 8, tokens), square, thin, thin, square, square, square]
    return [(shape, F32 if i < 3 else BF) for i, shape in enumerate(shapes)]


def ready_kernel(picked, places, hidden, branch, w_ref, wo_ref, qgain, kgain, stores):
    qn, kn, rad, qh, kh, vh, gh, krow, vrow = stores
    dim, tokens = qgain.shape
    pad = jnp.zeros((tokens - dim, tokens), F32)
    for i, c in enumerate(places):
        if i % 4 == 0:
            four = picked[i : i + 4]
            project = dot(jnp.concatenate([hidden(s) for s in four], axis=0), w_ref[...])
            back_out = dot(jnp.concatenate([branch(s) for s in four], axis=0), wo_ref[...])
        rows = slice(tokens * (i % 4), tokens * (i % 4 + 1))
        turned = project[rows].T
        q, k, v = (turned[dim * n : dim * (n + 1)] for n in range(3))
        rq = lax.rsqrt(jnp.mean(q * q, axis=0, keepdims=True) + EPS)
        rk = lax.rsqrt(jnp.mean(k * k, axis=0, keepdims=True) + EPS)
        q = q * rq
        k = k * rk
        qn[c] = q
        kn[c] = k
        rad[c] = jnp.concatenate([rq, rk, jnp.zeros((6, tokens), F32)], axis=0)
        q = q * qgain
        k = k * kgain
        qh[c] = jnp.concatenate([q, pad], axis=0).astype(BF)
        gh[c] = back_out[rows].T.astype(BF)
        kh[c] = k.astype(BF)
        vh[c] = v.astype(BF)
        krow[c] = jnp.concatenate([k, pad], axis=0).T.astype(BF)
        vrow[c] = jnp.concatenate([v, pad], axis=0).T.astype(BF)


def early_kernel(slots, features, w_ref, wo_ref, qg_ref, kg_ref, *refs):
    arrays, stores = refs[:-9], refs[-9:]
    tokens = arrays[0].shape[0]

    def hidden(s):
        n, lane = slots[s][1]
        return arrays[n][:, lane : lane + features]

    def branch(s):
        n, lane = slots[s][2]
        return arrays[n][:, lane : lane + features]

    gains = column(qg_ref, tokens), column(kg_ref, tokens)
    ready_kernel(EARLY, range(len(EARLY)), hidden, branch, w_ref, wo_ref, *gains, stores)


def early(w, wo, gains, arrays, slots):
    features = wo.shape[0]
    dim = gains[0].shape[1]
    tokens = arrays[0].shape[0]
    vm = pl.BlockSpec(memory_space=pltpu.VMEM)

    def body(*refs):
        early_kernel(slots, features, *refs)

    return pl.pallas_call(
        body,
        in_specs=[vm] * (4 + len(arrays)),
        out_specs=[vm] * 9,
        out_shape=[jax.ShapeDtypeStruct(*shape) for shape in ready_shapes(len(EARLY), dim, tokens)],
        compiler_params=params(24),
        name="early",
    )(w, wo, *gains, *arrays)


def heads_kernel(slots, dim, features, cams, id_ref, w_ref, wo_ref, qg_ref, kg_ref, *refs):
    count = len({n for _, *pairs in slots for n, _ in pairs})
    arrays, refs = refs[:count], refs[count:]
    readies, refs = refs[:9], refs[9:]
    gp_hbm, *sends, sem, gp_ref, nb, at, gq, gk, gv, acc, acc_out, spread = refs[:-9]
    stores = refs[-9:]
    qn, kn, rad, qh, kh, vh, gh, krow, vrow = stores
    tokens = arrays[0].shape[0]
    width = 3 * dim
    scale = 1.0 / math.sqrt(dim)
    qgain, kgain = column(qg_ref, tokens), column(kg_ref, tokens)
    me, vt = id_ref[0], id_ref[1]
    y, x, core = vt // 8, vt // 2 % 4, vt % 2
    cameras = [place((y + dy) % 2, (x + dx) % 4, (core + dc) % 2) for (dy, dx, dc), _, _ in slots]

    def hidden(s):
        n, lane = slots[s][1]
        return arrays[n][:, lane : lane + features]

    def branch(s):
        n, lane = slots[s][2]
        return arrays[n][:, lane : lane + features]

    for s, c in enumerate(cameras):
        n, lane = slots[s][1]
        marks = arrays[n][:16, lane + features : lane + features + LANES].astype(F32)
        nb[c, 0] = marks[0, 0].astype(jnp.int32)
        nb[c, 1] = marks[0, 1].astype(jnp.int32)
    for e, s in enumerate(EARLY):
        for ref, ready in zip(stores, readies):
            ref[cameras[s]] = ready[e]
    late = [s for s in range(cams) if s not in EARLY]
    ready_kernel(late, [cameras[s] for s in late], hidden, branch, w_ref, wo_ref, qgain, kgain, stores)

    def camera(c, _):
        left = nb[c, 0]
        right = nb[c, 1]
        q = qh[c]
        g = gh[c]
        keys = jnp.concatenate([krow[left], krow[c], krow[right]], axis=0)
        values = jnp.concatenate([vrow[left], vrow[c], vrow[right]], axis=0)
        keys_t = jnp.concatenate([kh[left], kh[c], kh[right]], axis=1)
        values_t = jnp.concatenate([vh[left], vh[c], vh[right]], axis=1)
        e = jnp.exp(dot(keys, q) * scale)
        probs = e * (1.0 / jnp.sum(e, axis=0, keepdims=True))
        low = probs.astype(BF)
        gprobs = dot(values, g)
        centre = jnp.sum(probs * gprobs, axis=0, keepdims=True)
        gs = (probs * (gprobs - centre) * scale).astype(BF)
        at[c] = dot(values_t, low).astype(BF)
        gq[c] = dot(keys_t, gs)
        gk[c] = dot(q, gs, NT)[:dim]
        gv[c] = dot(g, low, NT)[:dim]
        return 0

    lax.fori_loop(0, cams, camera, 0, unroll=16)

    def back(grad, unit, radius, gain):
        shaped = grad * gain
        return (shaped - unit * jnp.mean(shaped * unit, axis=0, keepdims=True)) * radius

    def finish(c, _):
        left = nb[c, 0]
        right = nb[c, 1]
        grad_k = gk[c, :, tokens : 2 * tokens] + gk[left, :, 2 * tokens :] + gk[right, :, :tokens]
        grad_v = gv[c, :, tokens : 2 * tokens] + gv[left, :, 2 * tokens :] + gv[right, :, :tokens]
        grad_q = back(gq[c], qn[c], rad[c, 0:1, :], qgain)
        grad_k = back(grad_k, kn[c], rad[c, 1:2, :], kgain)
        gp_ref[c] = jnp.concatenate([grad_q, grad_k, grad_v], axis=0).astype(BF)
        return 0

    lax.fori_loop(0, cams, finish, 0, unroll=8)

    out = pltpu.make_async_copy(gp_ref, gp_hbm, sem)
    out.start()
    acc[width:, :] = jnp.zeros_like(acc[width:, :])
    for s in range(0, cams, 4):
        four = range(s, s + 4)
        grads = jnp.concatenate([gp_ref[cameras[i]] for i in four], axis=1)
        atts = jnp.concatenate([at[cameras[i]] for i in four], axis=1)
        one = dot(grads, jnp.concatenate([hidden(i) for i in four], axis=0))
        two = dot(atts, jnp.concatenate([branch(i) for i in four], axis=0))
        acc[:width, :] = one if s == 0 else acc[:width, :] + one
        acc_out[...] = two if s == 0 else acc_out[...] + two
    turned = acc[...].T
    for b in range(features // dim):
        spread[b, :, :width] = turned[dim * b : dim * (b + 1), :width].astype(BF)
        spread[b, :, width:] = acc_out[:, dim * b : dim * (b + 1)].astype(BF)
    for k, ref in enumerate(sends):
        four = [spread[(near_bits(near(me) ^ k) + 2 * a) ^ vt].astype(F32) for a in range(4)]
        ref[...] = jnp.concatenate(four, axis=1).astype(BF)
    out.wait()


def heads(ids, w, wo, gains, arrays, slots, readies):
    dim = gains[0].shape[1]
    features = wo.shape[0]
    tokens = arrays[0].shape[0]
    cams = len(slots)
    vm = pl.BlockSpec(memory_space=pltpu.VMEM)
    sm = pl.BlockSpec(memory_space=pltpu.SMEM)

    def body(*refs):
        heads_kernel(slots, dim, features, cams, *refs)

    return pl.pallas_call(
        body,
        in_specs=[sm] + [vm] * (13 + len(arrays)),
        out_specs=[pl.BlockSpec(memory_space=pltpu.HBM)] + [vm] * 4,
        out_shape=[jax.ShapeDtypeStruct((cams, 3 * dim, tokens), BF)]
        + [jax.ShapeDtypeStruct((dim, 16 * dim), BF)] * 4,
        scratch_shapes=[
            pltpu.SemaphoreType.DMA,
            pltpu.VMEM((cams, 3 * dim, tokens), BF),
            pltpu.SMEM((cams, 2), jnp.int32),
            pltpu.VMEM((cams, dim, tokens), BF),
            pltpu.VMEM((cams, dim, tokens), F32),
            pltpu.VMEM((cams, dim, 3 * tokens), F32),
            pltpu.VMEM((cams, dim, 3 * tokens), F32),
            pltpu.VMEM((2 * LANES, features), F32),
            pltpu.VMEM((dim, features), F32),
            pltpu.VMEM((features // dim, dim, 4 * dim), BF),
        ]
        + [pltpu.VMEM(*shape) for shape in ready_shapes(cams, dim, tokens)],
        compiler_params=params(36),
        name="heads",
    )(ids, w, wo, *gains, *arrays, *readies)


def leave_kernel(x_ref, w_hbm, tok_ref, cot_ref, mod_ref, out_ref, w, scr, sem):
    heads, width, _ = x_ref.shape
    dim = width // 3
    features = tok_ref.shape[1]
    copies = [
        pltpu.make_async_copy(w_hbm.at[:, pl.ds(features * p, features)], w.at[p], sem.at[p]) for p in range(3)
    ]
    for copy in copies:
        copy.start()
    for h in range(heads):
        x = x_ref[h].astype(F32)
        for p in range(3):
            scr[p, dim * h : dim * (h + 1), :] = x[dim * p : dim * (p + 1)]
    normed, inverse = normalise(tok_ref[...].astype(F32))
    total = None
    for p in range(3):
        copies[p].wait()
        part = dot(w[p], scr[p].astype(BF))
        total = part if p == 0 else total + part
    scaled = total.T * (1.0 + line(mod_ref, 1))
    mean = jnp.mean(scaled, axis=-1, keepdims=True)
    along = jnp.mean(scaled * normed, axis=-1, keepdims=True)
    grad = inverse * (scaled - mean - normed * along)
    out_ref[...] = (cot_ref[...].astype(F32) + grad).astype(BF)


def leave(x, w_qkv, tok, cot, mod):
    rows, features = tok.shape
    vm = pl.BlockSpec(memory_space=pltpu.VMEM)
    return pl.pallas_call(
        leave_kernel,
        in_specs=[vm, pl.BlockSpec(memory_space=pltpu.HBM), vm, vm, vm],
        out_specs=vm,
        out_shape=jax.ShapeDtypeStruct(tok.shape, BF),
        scratch_shapes=[
            pltpu.VMEM((3, features, features), BF),
            pltpu.VMEM((3, features, rows), F32),
            pltpu.SemaphoreType.DMA((3,)),
        ],
        compiler_params=params(58),
        name="leave",
    )(x, w_qkv, tok, cot, mod)


def fold_kernel(id_ref, a_ref, b_ref, c_ref, d_ref, send_ref, keep_ref, four, rest):
    dim, width = four.shape[1:]
    total = a_ref[...].astype(F32) + b_ref[...].astype(F32) + c_ref[...].astype(F32) + d_ref[...].astype(F32)
    for a in range(4):
        chunk = total[:, (width + dim) * a : (width + dim) * (a + 1)]
        four[a] = chunk[:, :width]
        rest[a] = chunk[:, width:]
    tail = [rest[far(id_ref[1]) ^ a] for a in range(4)]
    me = far(id_ref[0])
    send_ref[...] = jnp.concatenate([four[me ^ 1], four[me ^ 2]] + tail, axis=1).astype(BF)
    keep_ref[...] = jnp.concatenate([four[me], four[me ^ 3]] + tail, axis=1).astype(BF)


def fold(ids, parts):
    dim = parts[0].shape[0]
    vm = pl.BlockSpec(memory_space=pltpu.VMEM)
    return pl.pallas_call(
        fold_kernel,
        in_specs=[pl.BlockSpec(memory_space=pltpu.SMEM)] + [vm] * 4,
        out_specs=[vm] * 2,
        out_shape=[jax.ShapeDtypeStruct((dim, 10 * dim), BF)] * 2,
        scratch_shapes=[pltpu.VMEM((4, dim, 3 * dim), F32), pltpu.VMEM((4, dim, dim), F32)],
        compiler_params=params(16),
        name="fold",
    )(ids, *parts)


def halve_kernel(a_ref, b_ref, own_ref, other_ref, rest_ref):
    width = own_ref.shape[1]
    total = a_ref[...].astype(F32) + b_ref[...].astype(F32)
    own_ref[...] = total[:, :width].astype(BF)
    other_ref[...] = total[:, width : 2 * width].astype(BF)
    rest_ref[...] = total[:, 2 * width :].astype(BF)


def close_kernel(factor, a_ref, b_ref, rest_ref, out_ref):
    total = (a_ref[...].astype(F32) + b_ref[...].astype(F32)) * factor
    out_ref[...] = jnp.concatenate([total, rest_ref[...].astype(F32)], axis=1).astype(BF)


def pair_kernel(factor, a_ref, b_ref, pair_ref, rest_ref):
    width = pair_ref.shape[1] // 2
    a, b = a_ref[...].astype(F32), b_ref[...].astype(F32)
    pair_ref[...] = jnp.concatenate([a[:, :width], b[:, :width]], axis=1).astype(BF)
    rest_ref[...] = ((a[:, width:] + b[:, width:]) * factor).astype(BF)


def join_kernel(id_ref, a_ref, b_ref, rest_ref, out_ref, all_ref):
    dim = a_ref.shape[0]
    width = 3 * dim
    me = far(id_ref[2])
    a, b = a_ref[...].astype(F32), b_ref[...].astype(F32)
    all_ref[me] = a[:, :width]
    all_ref[me ^ 3] = a[:, width:]
    all_ref[me ^ 1] = b[:, :width]
    all_ref[me ^ 2] = b[:, width:]
    rest = rest_ref[...].astype(F32)
    pieces = []
    for i in range(4):
        pieces += [all_ref[i], rest[:, dim * i : dim * (i + 1)]]
    out_ref[...] = jnp.concatenate(pieces, axis=1).astype(BF)


def small(body, name, parts, widths, ids=None, scratch=()):
    dim = parts[0].shape[0]
    vm = pl.BlockSpec(memory_space=pltpu.VMEM)
    first = [] if ids is None else [pl.BlockSpec(memory_space=pltpu.SMEM)]
    return pl.pallas_call(
        body,
        in_specs=first + [vm] * len(parts),
        out_specs=[vm] * len(widths),
        out_shape=[jax.ShapeDtypeStruct((dim, width), BF) for width in widths],
        scratch_shapes=list(scratch),
        compiler_params=params(16),
        name=name,
    )(*([] if ids is None else [ids]), *parts)


def final_kernel(id_ref, a_ref, b_ref, c_ref, d_ref, in_ref, out_ref, all_ref):
    heads = 16
    dim, wide = a_ref.shape
    total = wide // 4
    me = id_ref[2]
    for k, ref in enumerate((a_ref, b_ref, c_ref, d_ref)):
        all_ref[k] = ref[...]
    lines = [all_ref[near(me) ^ k].astype(F32) for k in range(4)]
    blocks = [lines[near(h)][:, total * far(h) : total * (far(h) + 1)] for h in range(heads)]
    for p in range(4):
        part = jnp.concatenate([b[:, dim * p : dim * (p + 1)] for b in blocks], axis=1).astype(BF)
        if p < 3:
            in_ref[:, heads * dim * p : heads * dim * (p + 1)] = part
        else:
            out_ref[...] = part


def final(ids, parts):
    dim, wide = parts[0].shape
    vm = pl.BlockSpec(memory_space=pltpu.VMEM)
    return pl.pallas_call(
        final_kernel,
        in_specs=[pl.BlockSpec(memory_space=pltpu.SMEM)] + [vm] * 4,
        out_specs=[vm] * 2,
        out_shape=[
            jax.ShapeDtypeStruct((dim, 3 * wide), BF),
            jax.ShapeDtypeStruct((dim, wide), BF),
        ],
        scratch_shapes=[pltpu.VMEM((4, dim, wide), BF)],
        compiler_params=params(16),
        name="final",
    )(ids, *parts)


def swap(part, bits):
    return lax.ppermute(part, "dp", [(i, i ^ bits) for i in range(16)])


def cross(part, bits):
    pairs = [(16 * a + b, 16 * (a ^ bits) + (a ^ bits ^ b)) for a in range(16) for b in range(16)]
    return lax.ppermute(part, ("dp", "vt"), pairs)


def front(ids, tok, cot, mod, q_gain, k_gain, w_qkv, w_out, nb):
    features = tok.shape[-1]
    hb = enter(nb, tok, cot, mod)
    w, wo = weights(ids, w_qkv, w_out, q_gain.shape[0])
    gains = q_gain.reshape(1, -1), k_gain.reshape(1, -1)
    arrays, slots, readies, w, wo = gather(hb, features + LANES, w, wo, gains)
    return heads(ids, w, wo, gains, arrays, slots, readies)


def shards(tokens, cotangent, modulation, q_gain, k_gain, w_qkv, w_out, neighbours):
    rows, features = tokens.shape[-2:]
    factor = 1.0 / (lax.axis_size("dp") * lax.axis_size("vt"))
    me = lax.axis_index("dp")
    vt = lax.axis_index("vt")
    ids = jnp.stack([me, vt, me ^ vt])
    tok = tokens.reshape(rows, features)
    cot = cotangent.reshape(rows, features)
    mod = modulation.reshape(3, 1, features)
    ids, tok = lax.optimization_barrier((ids, tok))
    gp, *sent = front(ids, tok, cot, mod, q_gain, k_gain, w_qkv, w_out, neighbours.reshape(2))
    parts = [sent[0]] + [swap(sent[k], near_bits(k)) for k in (1, 2, 3)]
    dim = q_gain.shape[0]
    send, keep = fold(ids, parts)
    own, other, rest = small(halve_kernel, "halve", [keep, swap(send, 2)], [3 * dim, 3 * dim, 4 * dim])
    own, other = cross(own, 0), cross(other, 6)
    gp, own, other = lax.optimization_barrier((gp, own, other))
    gp_mine = lax.all_to_all(gp, "vt", 0, 0)
    (mine,) = small(functools.partial(close_kernel, factor), "close", [own, other, rest], [7 * dim])
    pair, rest = small(functools.partial(pair_kernel, factor), "pair", [mine, swap(mine, 6)], [6 * dim, 4 * dim])
    scratch = [pltpu.VMEM((4, dim, 3 * dim), F32)]
    (group,) = small(join_kernel, "join", [pair, swap(pair, 2), rest], [16 * dim], ids, scratch)
    gp_mine, group = lax.optimization_barrier((gp_mine, group))
    grad_in, grad_out = final(ids, [group] + [swap(group, near_bits(k)) for k in (1, 2, 3)])
    grad_tokens = leave(gp_mine, w_qkv, tok, cot, mod)
    return grad_tokens.reshape(tokens.shape), grad_in, grad_out


def solution(mesh):
    placed = (
        P("dp", "vt", None, None, None),
        P("dp", "vt", None, None, None),
        P("dp", "vt", None, None),
        P(),
        P(),
        P(),
        P(),
        P("dp", "vt", None),
    )
    return jax.shard_map(
        shards,
        mesh=mesh,
        in_specs=placed,
        out_specs=(P("dp", "vt", None, None, None), P("vt", None), P("vt", None)),
        check_vma=False,
    )
```
